32 devices in a mesh: lon: 8 (over y, x, core), lat: 4 (over z).
Axes of the slice: x: 2, y: 2, z: 4, core: 2. Of those that a mesh axis runs over, the one named last changes fastest.
Arguments:
- fields_in: bfloat16 [64, 128, 1024], P(None, 'lat', 'lon'), may hold values from -6 to 6
- weight_one: bfloat16 [3, 3, 64, 64], replicated, may hold values from -0.25 to 0.25
- weight_two: bfloat16 [3, 3, 64, 64], replicated, may hold values from -0.25 to 0.25
- cotangent: bfloat16 [64, 128, 1024], P(None, 'lat', 'lon'), may hold values from -6 to 6
- north_map: int32 [8], replicated, may hold values from 0 to 7, each once
- north_code: int32 [8], replicated, may hold values from 0 to 1
- south_map: int32 [8], replicated, may hold values from 0 to 7, each once
- south_code: int32 [8], replicated, may hold values from 0 to 1
Outputs:
- output: bfloat16 [64, 128, 1024], P(None, 'lat', 'lon')
- d_fields: bfloat16 [64, 128, 1024], P(None, 'lat', 'lon')
- grad_one: float32 [3, 3, 64, 64], replicated
- grad_two: float32 [3, 3, 64, 64], replicated
The draws below stay inside these ranges and needn't reach their ends.
Inputs may be any that keep to these rules, and one draw needn't show every extreme that they name: north_map holds each longitude tile index once. south_map holds each longitude tile index once.
All inputs are finite; a program needn't handle non-finite values.
Results may differ from the reference program's by a relative error of at most 0.005.
Values may be sent and summed in bfloat16 or wider, within the bound.
No kernel may reach another device: no remote copies, remote signals or barrier semaphores. Data moves between devices by JAX's collectives and lax.ppermute only.
A program may use at most 64 MiB of HBM per device.

```python
import jax
import jax.numpy as jnp

CHANNELS = 64
TILE_COLS = 128
GRID_ROWS = 128
GRID_COLS = 1024
PIXELS = 131072
N_LON = 8


def touch_ends(drawn, own_key, low, largest):
    spot = [jax.random.randint(jax.random.fold_in(own_key, axis), (), 0, length) for axis, length in enumerate(drawn.shape)]
    widest = drawn.shape.index(max(drawn.shape))
    beside = spot[:widest] + [(spot[widest] + 1) % drawn.shape[widest]] + spot[widest + 1:]
    return drawn.at[tuple(spot)].set(low).at[tuple(beside)].set(largest)


def block_scale(rng, dims, shards, low, largest):
    def one(axis_at, shards_of):
        steps = jax.random.uniform(jax.random.fold_in(jax.random.fold_in(rng, 6), axis_at), (shards_of,), jnp.float32, low / len(shards), largest / len(shards))
        return jnp.repeat(jnp.exp(steps), dims[axis_at] // shards_of).reshape((-1,) + (1,) * (len(dims) - axis_at - 1))

    factor_of = one(*shards[0])
    for cut in shards[1:]:
        factor_of = factor_of * one(*cut)
    return factor_of


def bell_draw(rng, dims, deviation, limit, split=(), kind=jnp.bfloat16):
    drawn = deviation * jax.random.normal(rng, dims, jnp.float32)
    if split:
        drawn = drawn * block_scale(rng, dims, split, -0.22, 0.18)
    return jnp.clip(drawn, -limit, limit).astype(kind)


def setup_inputs(seed: int = 0) -> dict:
    key_list = jax.random.split(jax.random.key(seed), 9)
    return {
        "fields_in": bell_draw(key_list[0], (CHANNELS, GRID_ROWS, GRID_COLS), 1.0, 6.0, ((1, 4), (2, 8))),
        "weight_one": bell_draw(key_list[1], (3, 3, CHANNELS, CHANNELS), (9 * CHANNELS) ** -0.5, 0.25),
        "weight_two": bell_draw(key_list[2], (3, 3, CHANNELS, CHANNELS), (9 * CHANNELS) ** -0.5, 0.25),
        "cotangent": bell_draw(key_list[3], (CHANNELS, GRID_ROWS, GRID_COLS), 1.0, 6.0, ((1, 4), (2, 8))),
        "north_map": jax.random.permutation(key_list[4], N_LON).astype(jnp.int32),
        "north_code": touch_ends(jax.random.randint(key_list[5], (N_LON,), 0, 2), jax.random.fold_in(key_list[5], 1), 0, 1).astype(jnp.int32),
        "south_map": jax.random.permutation(key_list[6], N_LON).astype(jnp.int32),
        "south_code": touch_ends(jax.random.randint(key_list[7], (N_LON,), 0, 2), jax.random.fold_in(key_list[7], 1), 0, 1).astype(jnp.int32),
    }


def pole_row(edge_row, partner, code_row):
    tile_rows = edge_row.reshape(edge_row.shape[0], N_LON, TILE_COLS)
    chosen = tile_rows[:, partner, :]
    chosen = jnp.where((code_row == 1)[None, :, None], chosen[:, :, ::-1], chosen)
    return chosen.reshape(edge_row.shape[0], GRID_COLS)

def extend_global(values, north_map, north_code, south_map, south_code):
    north_row = pole_row(values[:, 0, :], north_map, north_code)
    south_row = pole_row(values[:, -1, :], south_map, south_code)
    tall_field = jnp.concatenate([north_row[:, None, :], values, south_row[:, None, :]], axis=1)
    return jnp.concatenate([tall_field[:, :, -1:], tall_field, tall_field[:, :, :1]], axis=2)

def convolve(padded, weight):
    summed = jnp.zeros((weight.shape[2], GRID_ROWS * GRID_COLS), jnp.float32)
    for shift_row in range(3):
        for shift_col in range(3):
            window = padded[:, shift_row:shift_row + GRID_ROWS, shift_col:shift_col + GRID_COLS].reshape(padded.shape[0], -1)
            summed = summed + jnp.dot(weight[shift_row, shift_col], window, preferred_element_type=jnp.float32)
    return summed.reshape(weight.shape[2], GRID_ROWS, GRID_COLS)

def back_conv(upstream, weight, padded):
    flat_up = upstream.reshape(upstream.shape[0], -1)
    d_pad = jnp.zeros(padded.shape, jnp.float32)
    grads = []
    for shift_row in range(3):
        for shift_col in range(3):
            window = padded[:, shift_row:shift_row + GRID_ROWS, shift_col:shift_col + GRID_COLS].reshape(padded.shape[0], -1)
            grads.append(jnp.dot(flat_up, window.T, preferred_element_type=jnp.float32))
            spread = jnp.dot(weight[shift_row, shift_col].T, flat_up, preferred_element_type=jnp.float32)
            spread = spread.reshape(weight.shape[3], GRID_ROWS, GRID_COLS)
            d_pad = d_pad.at[:, shift_row:shift_row + GRID_ROWS, shift_col:shift_col + GRID_COLS].add(spread)
    return (d_pad, jnp.stack(grads).reshape(3, 3, weight.shape[2], weight.shape[3]))

def reference(fields_in, weight_one, weight_two, cotangent, north_map, north_code, south_map, south_code):

    def extend(values):
        return extend_global(values, north_map, north_code, south_map, south_code)
    grad_scale = 1.0 / jnp.sqrt(jnp.float32(PIXELS))
    padded_in = extend(fields_in)
    pre_act = convolve(padded_in, weight_one)
    hidden = jax.nn.gelu(pre_act).astype(jnp.bfloat16)
    padded_hidden = extend(hidden)
    output = convolve(padded_hidden, weight_two).astype(jnp.bfloat16)
    spread_two, grad_two = back_conv(cotangent, weight_two, padded_hidden)
    _, pull_ext = jax.vjp(extend, hidden.astype(jnp.float32))
    back_hidden = pull_ext(spread_two)[0]
    _, pull_gelu = jax.vjp(jax.nn.gelu, pre_act)
    d_pre = pull_gelu(back_hidden)[0].astype(jnp.bfloat16)
    spread_one, grad_one = back_conv(d_pre, weight_one, padded_in)
    _, pull_in = jax.vjp(extend, fields_in.astype(jnp.float32))
    d_fields = pull_in(spread_one)[0].astype(jnp.bfloat16)
    return (output, d_fields, grad_one * grad_scale, grad_two * grad_scale)
```

```python
import math

import jax
import jax.numpy as jnp
from jax import lax
from jax.experimental import pallas as pl
from jax.experimental.pallas import tpu as pltpu
from jax.sharding import PartitionSpec as P

BF = jnp.bfloat16
F32 = jnp.float32
GELU_K = math.sqrt(2.0 / math.pi)
VMEM_LIMIT = 48 * 1024 * 1024


def mm(a, b):
    return jnp.dot(a, b, preferred_element_type=F32)


def mm_t(a, b):
    return lax.dot_general(a, b, (((1,), (1,)), ((), ())), preferred_element_type=F32)


def lane_of(like):
    return lax.broadcasted_iota(jnp.int32, like.shape, like.ndim - 1)


def rot(x, by):
    return pltpu.roll(x, by, x.ndim - 1)


def gelu_parts(u):
    square = u * u
    t = jnp.tanh(GELU_K * u * (1.0 + 0.044715 * square))
    half = 0.5 + 0.5 * t
    slope = half + (0.5 * GELU_K) * u * (1.0 - t * t) * (1.0 + (3 * 0.044715) * square)
    return u * half, slope


def pack_kernel(x_ref, c_ref, out_ref):
    rows = x_ref.shape[0]
    bottom = jnp.where(lax.axis_index("lat") == 0, 0, 1)
    edge = bottom * (rows - 1)
    beside = 1 + bottom * (rows - 3)
    out_ref[0] = x_ref[edge]
    out_ref[1] = x_ref[beside]
    out_ref[2] = c_ref[edge]
    out_ref[3] = c_ref[beside]
    for at, ref in ((4, x_ref), (5, c_ref)):
        packed = jnp.zeros(ref.shape[1:], F32)
        lane = lane_of(packed)
        for i in range(rows):
            turned = rot(ref[i].astype(F32), (4 * i + 2) % 128)
            packed = jnp.where((lane >= 4 * i) & (lane < 4 * i + 4), turned, packed)
        out_ref[at] = packed.astype(BF)


def strip_kernel(x_ref, c_ref, all_ref, sx_ref, sc_ref, south_ref, north_ref):
    rows, chans, cols = x_ref.shape
    n = all_ref.shape[0]
    me = lax.axis_index("lon")
    west = lax.rem(me + n - 1, n)
    east = lax.rem(me + 1, n)
    target = lax.broadcasted_iota(jnp.int32, (3 * cols, 3 * cols), 1)
    source = lax.broadcasted_iota(jnp.int32, (3 * cols, 3 * cols), 0)
    block = target // 128
    side = (target % 128) // 64
    row = target % 64 - 2
    origin = jnp.where(side == 0, block // 2, 1 + (block + 1) // 2)
    wanted = 128 * origin + 4 * row + block + side
    hit = (source == wanted) & (row >= 0) & (row < rows)
    chooser = jnp.where(hit, 1.0, 0.0).astype(BF)
    to_south = jnp.zeros((chans, cols), F32)
    to_north = jnp.zeros((chans, cols), F32)
    lane = lane_of(to_south)
    pair = (lane % 64) // 2
    for at, ref in ((0, sx_ref), (1, sc_ref)):
        taken = jnp.concatenate([all_ref[west, 4 + at], all_ref[me, 4 + at], all_ref[east, 4 + at]], axis=1)
        strip = mm(taken, chooser)
        ref[...] = strip.astype(BF)
        for b in range(3):
            m = 3 * at + b
            piece = strip[:, 128 * b : 128 * b + 128]
            to_south = jnp.where(pair == m, rot(piece, (2 * m - rows) % 128), to_south)
            to_north = jnp.where(pair == m, rot(piece, (2 * m - 2) % 128), to_north)
    for k in range(2):
        south_ref[k] = x_ref[rows - 2 + k]
        south_ref[2 + k] = c_ref[rows - 2 + k]
        north_ref[k] = x_ref[k]
        north_ref[2 + k] = c_ref[k]
    south_ref[4] = to_south.astype(BF)
    north_ref[4] = to_north.astype(BF)


def row_stack(strip):
    wide = strip.astype(F32)
    parts = [wide[:, at : at + 128] for at in range(0, wide.shape[1], 128)]
    above = jnp.concatenate([rot(p, 1) for p in parts], axis=1).astype(BF)
    below = jnp.concatenate([rot(p, 127) for p in parts], axis=1).astype(BF)
    return jnp.concatenate([above, strip, below], axis=0)


def joined(z, chans, place, edge_w, edge_e):
    lane = lane_of(edge_w)
    low = jnp.where(lane == 0, rot(edge_w, 128 - place), rot(z[:chans], 1))
    high = jnp.where(lane == 127, rot(edge_e, 63 - place), rot(z[2 * chans :], 127))
    return low + z[chans : 2 * chans] + high


def pair_of_rows(ref, at):
    four = ref[pl.ds(at, 4)]
    _, chans, cols = four.shape
    return jnp.concatenate(
        [four[:3].reshape(3 * chans, cols), four[1:].reshape(3 * chans, cols)], axis=1
    )


def ring_sum(z, chans):
    return rot(z[:chans], 1) + z[chans : 2 * chans] + rot(z[2 * chans :], z.shape[1] - 1)


def main_kernel(
    nmap, ncode, smap, scode, x_ref, c_ref, all_ref, sx_ref, sc_ref, fn_ref, fs_ref, a1_ref, a2_ref, a3_ref,
    h_ref, hs_ref, d_ref, ds_ref, rim_ref, g_ref,
    xe, ce, sxe, sce, stack, tiles, hring, dring, acc1, acc2,
):
    rows, chans, cols = x_ref.shape
    n = all_ref.shape[0]
    lat = lax.axis_index("lat")
    me = lax.axis_index("lon")
    at_top = lat == 0
    at_bottom = lat == lax.axis_size("lat") - 1
    block = (chans, cols)
    lane = lax.broadcasted_iota(jnp.int32, block, 1)
    row_lane = lane % 64

    xe[0:2] = fn_ref[0:2]
    ce[0:2] = fn_ref[2:4]
    xe[2 : rows + 2] = x_ref[...]
    ce[2 : rows + 2] = c_ref[...]
    xe[rows + 2 : rows + 4] = fs_ref[0:2]
    ce[rows + 2 : rows + 4] = fs_ref[2:4]
    corner_n = fn_ref[4].astype(F32)
    corner_s = fs_ref[4].astype(F32)
    for at, (src, dst) in enumerate(((sx_ref, sxe), (sc_ref, sce))):
        for b in range(3):
            m = 3 * at + b
            piece = src[:, 128 * b : 128 * b + 128].astype(F32)
            piece = jnp.where(row_lane < 2, rot(corner_n, (-2 * m) % 128), piece)
            piece = jnp.where(
                (row_lane >= rows + 2) & (row_lane < rows + 4),
                rot(corner_s, (rows + 2 - 2 * m) % 128),
                piece,
            )
            dst[:, 128 * b : 128 * b + 128] = piece.astype(BF)

    a1 = a1_ref[...]
    a2 = a2_ref[...]
    zx = mm(a1, row_stack(sxe[...]))
    zc = mm(a2, row_stack(sce[...]))

    def three(z):
        return z[:chans, :128] + z[chans : 2 * chans, 128:256] + z[2 * chans :, 256:]

    value, slope = gelu_parts(three(zx))
    hs_ref[...] = value.astype(BF)
    ds_ref[...] = (slope * three(zc)).astype(BF)
    xw, xeast = zx[:chans, 128:256], zx[2 * chans :, 128:256]
    cw, ceast = zc[:chans, 128:256], zc[2 * chans :, 128:256]

    def two_rows(step, _):
        t = 2 * step
        z1 = mm(a1, pair_of_rows(xe, t))
        z2 = mm(a2, pair_of_rows(ce, t))
        for k in range(2):
            span = slice(128 * k, 128 * k + 128)
            u = joined(z1[:, span], chans, t + k + 1, xw, xeast)
            back = joined(z2[:, span], chans, t + k + 1, cw, ceast)
            value, slope = gelu_parts(u)
            h_ref[t + k] = value.astype(BF)
            d_ref[t + k] = (slope * back).astype(BF)
        return 0

    lax.fori_loop(0, (rows + 2) // 2, two_rows, 0)
    rim_ref[...] = jnp.zeros(block, F32)

    @pl.when(at_top | at_bottom)
    def _():
        west = lax.rem(me + n - 1, n)
        east = lax.rem(me + 1, n)
        first = jnp.where(at_top, 0, 2)
        last = 2 - first
        place = jnp.where(at_top, 1, rows + 2)
        inner = jnp.where(at_top, 2, rows + 1)
        outer_row = jnp.where(at_top, 0, rows + 1)
        inner_row = jnp.where(at_top, 1, rows)
        flip = jnp.where(
            lax.broadcasted_iota(jnp.int32, (cols, cols), 0)
            + lax.broadcasted_iota(jnp.int32, (cols, cols), 1)
            == cols - 1,
            1.0,
            0.0,
        ).astype(BF)

        def partner(b):
            return jnp.where(at_top, nmap[b], smap[b])

        def code(b):
            return jnp.where(at_top, ncode[b], scode[b])

        def turned(tile, b):
            return jnp.where(code(b) == 1, mm(tile, flip), tile.astype(F32))

        def turned_wide(tile, b):
            high = tile.astype(BF)
            low = (tile - high.astype(F32)).astype(BF)
            return jnp.where(code(b) == 1, mm(high, flip) + mm(low, flip), tile)

        for b in range(n):
            span = slice(128 * b, 128 * b + 128)
            across = turned(all_ref[partner(b), 0], b).astype(BF)
            stack[first, :, span] = across
            tiles[b] = across.astype(F32)
            stack[1, :, span] = all_ref[b, 0]
            stack[last, :, span] = all_ref[b, 1]
        u = ring_sum(mm(a1, stack[...].reshape(3 * chans, n * cols)), chans)
        value, slope = gelu_parts(u)
        for b in range(n):
            hring[b] = value[:, 128 * b : 128 * b + 128].astype(BF)
        xe[jnp.where(at_top, 1, rows + 2)] = tiles[me].astype(BF)
        edge = sxe[:, 128:256].astype(F32)
        edge = jnp.where(lane == place, rot(tiles[west], place + 1), edge)
        edge = jnp.where(lane == 64 + place, rot(tiles[east], 64 + place), edge)
        sxe[:, 128:256] = edge.astype(BF)
        empty = jnp.zeros((chans, n * cols), BF)
        stack[first] = empty
        stack[1] = empty
        for b in range(n):
            stack[last, :, 128 * b : 128 * b + 128] = all_ref[b, 2]
        rim = ring_sum(mm(a2, stack[...].reshape(3 * chans, n * cols)), chans)
        for b in range(n):
            tiles[partner(b)] = turned_wide(rim[:, 128 * b : 128 * b + 128], b)
        for b in range(n):
            span = slice(128 * b, 128 * b + 128)
            stack[1, :, span] = all_ref[b, 2]
            stack[last, :, span] = all_ref[b, 3]
        back = ring_sum(mm(a2, stack[...].reshape(3 * chans, n * cols)), chans)
        for b in range(n):
            span = slice(128 * b, 128 * b + 128)
            dring[b] = (slope[:, span] * (back[:, span] + tiles[b])).astype(BF)
        stack[first] = empty
        stack[1] = empty
        origin = 0
        for b in range(n):
            stack[last, :, 128 * b : 128 * b + 128] = dring[b]
            origin = origin + jnp.where(partner(b) == me, b, 0)
        rim = ring_sum(mm(a3_ref[...], stack[...].reshape(3 * chans, n * cols)), chans)
        for b in range(n):
            tiles[b] = rim[:, 128 * b : 128 * b + 128]
        rim_ref[...] = turned_wide(tiles[origin], origin)
        h_ref[inner_row] = hring[me]
        d_ref[inner_row] = dring[me]
        h_ref[outer_row] = turned(hring[partner(me)], me).astype(BF)
        d_ref[outer_row] = jnp.zeros(block, BF)
        hs = hs_ref[...].astype(F32)
        hw = turned(hring[partner(west)], west)
        he = turned(hring[partner(east)], east)
        hs = jnp.where(lane == place, rot(hw, place + 1), hs)
        hs = jnp.where(lane == 64 + place, rot(he, 64 + place), hs)
        hs = jnp.where(lane == inner, rot(hring[west].astype(F32), inner + 1), hs)
        hs = jnp.where(lane == 64 + inner, rot(hring[east].astype(F32), 64 + inner), hs)
        hs_ref[...] = hs.astype(BF)
        ds = ds_ref[...].astype(F32)
        ds = jnp.where(row_lane == place, 0.0, ds)
        ds = jnp.where(lane == inner, rot(dring[west].astype(F32), inner + 1), ds)
        ds = jnp.where(lane == 64 + inner, rot(dring[east].astype(F32), 64 + inner), ds)
        ds_ref[...] = ds.astype(BF)

    own = (row_lane >= 2) & (row_lane < rows + 2)
    none = jnp.zeros(block, F32)

    def rim_terms(west_part, east_part):
        return jnp.concatenate(
            [
                jnp.where(own & (lane < 64), west_part, none),
                none,
                jnp.where(own & (lane >= 64), east_part, none),
            ],
            axis=0,
        ).astype(BF)

    sc = sce[...].astype(F32)
    acc2[...] = mm_t(rim_terms(sc[:, 256:], sc[:, :128]), row_stack(hs_ref[...]))
    def place_column(i, held):
        tile = d_ref[i + 1].astype(F32)
        held = jnp.where(lane == i + 2, rot(tile, i + 2), held)
        return jnp.where(lane == 66 + i, rot(tile, 67 + i), held)

    dcol = lax.fori_loop(0, rows, place_column, none)
    acc1[...] = mm_t(rim_terms(dcol, dcol), row_stack(sxe[:, 128:256]))

    def shifted_rows(ref, at):
        parts = []
        for k in range(2):
            tile = ref[at + k].astype(F32)
            ahead = jnp.where(lane == 127, 0.0, rot(tile, 127))
            behind = jnp.where(lane == 0, 0.0, rot(tile, 1))
            parts.append(jnp.concatenate([ahead, tile, behind], axis=0).astype(BF))
        return jnp.concatenate(parts, axis=1)

    def add_rows(step, _):
        y = 2 * step
        acc2[...] += mm_t(shifted_rows(ce, y + 2), pair_of_rows(h_ref, y))
        acc1[...] += mm_t(shifted_rows(d_ref, y + 1), pair_of_rows(xe, y + 1))
        return 0

    lax.fori_loop(0, rows // 2, add_rows, 0)
    g2 = acc2[...]
    g1 = acc1[...]
    g_ref[0] = g2[:, :128]
    g_ref[1] = g1[:, :128]
    g_ref[2] = jnp.concatenate([g2[:, 128:], g1[:, 128:]], axis=1)


def out_kernel(h_ref, hs_ref, d_ref, ds_ref, rim_ref, b2_ref, b1_ref, out_ref, df_ref):
    rows, chans, cols = out_ref.shape
    lat = lax.axis_index("lat")
    b2 = b2_ref[...]
    b1 = b1_ref[...]
    zh = mm(b2, row_stack(hs_ref[...]))
    zd = mm(b1, row_stack(ds_ref[...]))
    hw, he = zh[:chans], zh[2 * chans :]
    dw, de = zd[:chans], zd[2 * chans :]

    def two_rows(step, _):
        t = 2 * step
        z2 = mm(b2, pair_of_rows(h_ref, t))
        z1 = mm(b1, pair_of_rows(d_ref, t))
        for k in range(2):
            span = slice(128 * k, 128 * k + 128)
            out_ref[t + k] = joined(z2[:, span], chans, t + k + 2, hw, he).astype(BF)
            rim_here = ((t + k == 0) & (lat == 0)) | (
                (t + k == rows - 1) & (lat == lax.axis_size("lat") - 1)
            )
            back = joined(z1[:, span], chans, t + k + 2, dw, de)
            df_ref[t + k] = (back + jnp.where(rim_here, 1.0, 0.0) * rim_ref[...]).astype(BF)
        return 0

    lax.fori_loop(0, rows // 2, two_rows, 0)


def call(kernel, outs, args, scratch=(), flops=0, smem=0):
    space = [pl.BlockSpec(memory_space=pltpu.SMEM)] * smem
    space += [pl.BlockSpec(memory_space=pltpu.VMEM)] * (len(args) - smem)
    moved = sum(math.prod(a.shape) * a.dtype.itemsize for a in list(args) + list(outs))
    return pl.pallas_call(
        kernel,
        out_shape=tuple(outs),
        in_specs=space,
        out_specs=tuple(pl.BlockSpec(memory_space=pltpu.VMEM) for _ in outs),
        scratch_shapes=list(scratch),
        compiler_params=pltpu.CompilerParams(vmem_limit_bytes=VMEM_LIMIT),
        cost_estimate=pl.CostEstimate(flops=flops, bytes_accessed=moved, transcendentals=0),
    )(*args)


def summed(values, axes):
    for axis in axes:
        size = lax.axis_size(axis)
        step = 1
        while step < size:
            pairs = [(i, i ^ step) for i in range(size)]
            values = values + lax.ppermute(values, axis, pairs)
            step *= 2
    return values


def on_device(
    fields_in, weight_one, weight_two, cotangent, north_map, north_code, south_map, south_code
):
    chans, rows, cols = fields_in.shape
    n = lax.axis_size("lon")
    lat_count = lax.axis_size("lat")
    pixel_total = rows * cols * n * lat_count
    shape = jax.ShapeDtypeStruct
    x = fields_in.transpose(1, 0, 2)
    c = cotangent.transpose(1, 0, 2)
    forward_one = weight_one.transpose(1, 2, 0, 3).reshape(3 * chans, 3 * chans)
    forward_two = weight_two.transpose(1, 2, 0, 3).reshape(3 * chans, 3 * chans)
    back_one = weight_one[::-1, ::-1].transpose(1, 3, 0, 2).reshape(3 * chans, 3 * chans)
    back_two = weight_two[::-1, ::-1].transpose(1, 3, 0, 2).reshape(3 * chans, 3 * chans)

    (packed,) = call(pack_kernel, [shape((6, chans, cols), BF)], [x, c])
    gathered = lax.all_gather(packed, "lon", axis=0)
    strip = shape((chans, 3 * cols), BF)
    five = shape((5, chans, cols), BF)
    sx, sc, to_south, to_north = call(strip_kernel, [strip, strip, five, five], [x, c, gathered])
    from_north = lax.ppermute(to_south, "lat", [(i, i + 1) for i in range(lat_count - 1)])
    from_south = lax.ppermute(to_north, "lat", [(i + 1, i) for i in range(lat_count - 1)])

    conv_flops = 2 * 9 * chans * chans * rows * cols
    taller = shape((rows + 2, chans, cols), BF)
    edges = shape((chans, cols), BF)
    h, hs, d, ds, rim, grads = call(
        main_kernel,
        [taller, edges, taller, edges, shape((chans, cols), F32), shape((3, 3 * chans, cols), F32)],
        [north_map, north_code, south_map, south_code, x, c, gathered, sx, sc, from_north, from_south]
        + [forward_one, back_two, back_one],
        [
            pltpu.VMEM((rows + 4, chans, cols), BF),
            pltpu.VMEM((rows + 4, chans, cols), BF),
            pltpu.VMEM((chans, 3 * cols), BF),
            pltpu.VMEM((chans, 3 * cols), BF),
            pltpu.VMEM((3, chans, n * cols), BF),
            pltpu.VMEM((n, chans, cols), F32),
            pltpu.VMEM((n, chans, cols), BF),
            pltpu.VMEM((n, chans, cols), BF),
            pltpu.VMEM((3 * chans, 3 * chans), F32),
            pltpu.VMEM((3 * chans, 3 * chans), F32),
        ],
        flops=4 * conv_flops,
        smem=4,
    )
    low = shape((rows, chans, cols), BF)
    out, d_fields = call(
        out_kernel, [low, low], [h, hs, d, ds, rim, forward_two, back_one], flops=2 * conv_flops
    )
    flat = grads.reshape(2, -1, cols)
    mine = lax.axis_index("lon") % 2
    swap = [(i, i ^ 1) for i in range(n)]
    kept = lax.dynamic_index_in_dim(flat, mine, 0, keepdims=False)
    given = lax.dynamic_index_in_dim(flat, 1 - mine, 0, keepdims=False)
    half = kept + lax.ppermute(given, "lon", swap)
    step = 2
    while step < n:
        half = half + lax.ppermute(half, "lon", [(i, i ^ step) for i in range(n)])
        step *= 2
    half = summed(half, ("lat",))
    other = lax.ppermute(half, "lon", swap)
    both = jnp.where(mine == 0, jnp.stack([half, other]), jnp.stack([other, half]))
    total = both.reshape(3, 3 * chans, cols) * (1.0 / math.sqrt(pixel_total))
    half_cols = cols // 2
    two = jnp.concatenate([total[0], total[2][:, :half_cols]], axis=1)
    one = jnp.concatenate([total[1], total[2][:, half_cols:]], axis=1)

    def unfold(g):
        return g.reshape(3, chans, 3, chans).transpose(2, 0, 1, 3)

    return (out.transpose(1, 0, 2), d_fields.transpose(1, 0, 2), unfold(one), unfold(two))


def solution(mesh):
    placed = (P(None, "lat", "lon"), P(), P(), P(None, "lat", "lon"), P(), P(), P(), P())
    return jax.shard_map(
        on_device,
        mesh=mesh,
        in_specs=placed,
        out_specs=(P(None, "lat", "lon"), P(None, "lat", "lon"), P(), P()),
        check_vma=False,
    )
```

```python
import functools
import math

import jax
import jax.numpy as jnp
from jax import lax
from jax.experimental import pallas as pl
from jax.experimental.pallas import tpu as pltpu
from jax.sharding import PartitionSpec as P

BF = jnp.bfloat16
F32 = jnp.float32
GELU_K = math.sqrt(2.0 / math.pi)
VMEM_LIMIT = 48 * 1024 * 1024
UNROLL = 5
UNROLL_G = 4
UNROLL_O = 4


def mm(a, b):
    return jnp.dot(a, b, preferred_element_type=F32)


def mm_t(a, b):
    return lax.dot_general(a, b, (((1,), (1,)), ((), ())), preferred_element_type=F32)


def lane_of(like):
    return lax.broadcasted_iota(jnp.int32, like.shape, like.ndim - 1)


def rot(x, by):
    return pltpu.roll(x, by, x.ndim - 1)


def gelu_parts(u):
    square = u * u
    t = jnp.tanh(GELU_K * u * (1.0 + 0.044715 * square))
    half = 0.5 + 0.5 * t
    slope = half + (0.5 * GELU_K) * u * (1.0 - t * t) * (1.0 + (3 * 0.044715) * square)
    return u * half, slope


def pack_kernel(x_ref, c_ref, out_ref):
    rows = x_ref.shape[0]
    bottom = jnp.where(lax.axis_index("lat") == 0, 0, 1)
    edge = bottom * (rows - 1)
    beside = 1 + bottom * (rows - 3)
    out_ref[0] = x_ref[edge]
    out_ref[1] = x_ref[beside]
    out_ref[2] = c_ref[edge]
    out_ref[3] = c_ref[beside]
    for at, ref in ((4, x_ref), (5, c_ref)):
        packed = jnp.zeros(ref.shape[1:], F32)
        lane = lane_of(packed)
        for i in range(rows):
            turned = rot(ref[i].astype(F32), (4 * i + 2) % 128)
            packed = jnp.where((lane >= 4 * i) & (lane < 4 * i + 4), turned, packed)
        out_ref[at] = packed.astype(BF)


def strip_kernel(x_ref, c_ref, all_ref, sx_ref, sc_ref, to1_ref, to2_ref):
    rows, chans, cols = x_ref.shape
    n = all_ref.shape[0]
    me = lax.axis_index("lon")
    west = lax.rem(me + n - 1, n)
    east = lax.rem(me + 1, n)
    target = lax.broadcasted_iota(jnp.int32, (3 * cols, 3 * cols), 1)
    source = lax.broadcasted_iota(jnp.int32, (3 * cols, 3 * cols), 0)
    block = target // 128
    side = (target % 128) // 64
    row = target % 64 - 2
    origin = jnp.where(side == 0, block // 2, 1 + (block + 1) // 2)
    wanted = 128 * origin + 4 * row + block + side
    hit = (source == wanted) & (row >= 0) & (row < rows)
    chooser = jnp.where(hit, 1.0, 0.0).astype(BF)
    to_south = jnp.zeros((chans, cols), F32)
    to_north = jnp.zeros((chans, cols), F32)
    lane = lane_of(to_south)
    pair = (lane % 64) // 2
    for at, ref in ((0, sx_ref), (1, sc_ref)):
        taken = jnp.concatenate([all_ref[west, 4 + at], all_ref[me, 4 + at], all_ref[east, 4 + at]], axis=1)
        strip = mm(taken, chooser)
        ref[...] = strip.astype(BF)
        for b in range(3):
            m = 3 * at + b
            piece = strip[:, 128 * b : 128 * b + 128]
            to_south = jnp.where(pair == m, rot(piece, (2 * m - rows) % 128), to_south)
            to_north = jnp.where(pair == m, rot(piece, (2 * m - 2) % 128), to_north)
    odd = lax.rem(lax.axis_index("lat"), 2)
    for ref, northward in ((to1_ref, odd), (to2_ref, 1 - odd)):
        start = (rows - 2) * (1 - northward)
        for k in range(2):
            ref[k] = x_ref[start + k]
            ref[2 + k] = c_ref[start + k]
        ref[4] = jnp.where(northward == 1, to_north, to_south).astype(BF)


def row_stack(strip):
    wide = strip.astype(F32)
    parts = [wide[:, at : at + 128] for at in range(0, wide.shape[1], 128)]
    above = jnp.concatenate([rot(p, 1) for p in parts], axis=1).astype(BF)
    below = jnp.concatenate([rot(p, 127) for p in parts], axis=1).astype(BF)
    return jnp.concatenate([above, strip, below], axis=0)


def joined(z, chans, place, edge_w, edge_e):
    lane = lane_of(edge_w)
    low = jnp.where(lane == 0, rot(edge_w, 128 - place), rot(z[:chans], 1))
    high = jnp.where(lane == 127, rot(edge_e, 63 - place), rot(z[2 * chans :], 127))
    return low + z[chans : 2 * chans] + high


def pair_of_rows(ref, at):
    four = ref[pl.ds(at, 4)]
    _, chans, cols = four.shape
    return jnp.concatenate(
        [four[:3].reshape(3 * chans, cols), four[1:].reshape(3 * chans, cols)], axis=1
    )


def ring_sum(z, chans):
    return rot(z[:chans], 1) + z[chans : 2 * chans] + rot(z[2 * chans :], z.shape[1] - 1)


def interior_kernel(
    nmap, ncode, smap, scode, x_ref, c_ref, all_ref, sx_ref, sc_ref, a1_ref, a2_ref, a3_ref,
    h_ref, d_ref, pole_ref, patch_ref, rim_ref,
    stack, tiles, hring, dring,
):
    rows, chans, cols = x_ref.shape
    n = all_ref.shape[0]
    lat = lax.axis_index("lat")
    me = lax.axis_index("lon")
    at_top = lat == 0
    at_bottom = lat == lax.axis_size("lat") - 1
    block = (chans, cols)
    lane = lax.broadcasted_iota(jnp.int32, block, 1)
    a1 = a1_ref[...]
    a2 = a2_ref[...]
    zx = mm(a1, row_stack(sx_ref[:, 128:256]))
    zc = mm(a2, row_stack(sc_ref[:, 128:256]))

    def two_rows(step, _):
        y = 1 + 2 * step
        rows_at_once(
            mm(a1, pair_of_rows(x_ref, y - 1)), mm(a2, pair_of_rows(c_ref, y - 1)),
            zx, zc, chans, y + 2, h_ref, d_ref, y + 1,
        )
        return 0

    lax.fori_loop(0, (rows - 2) // 2, two_rows, 0, unroll=UNROLL)
    rim_ref[...] = jnp.zeros(block, F32)

    @pl.when(at_top | at_bottom)
    def _():
        west = lax.rem(me + n - 1, n)
        east = lax.rem(me + 1, n)
        first = jnp.where(at_top, 0, 2)
        last = 2 - first
        place = jnp.where(at_top, 1, rows + 2)
        inner = jnp.where(at_top, 2, rows + 1)
        flip = jnp.where(
            lax.broadcasted_iota(jnp.int32, (cols, cols), 0)
            + lax.broadcasted_iota(jnp.int32, (cols, cols), 1)
            == cols - 1,
            1.0,
            0.0,
        ).astype(BF)

        def partner(b):
            return jnp.where(at_top, nmap[b], smap[b])

        def code(b):
            return jnp.where(at_top, ncode[b], scode[b])

        def turned(tile, b):
            return jnp.where(code(b) == 1, mm(tile, flip), tile.astype(F32))

        def turned_wide(tile, b):
            high = tile.astype(BF)
            low = (tile - high.astype(F32)).astype(BF)
            return jnp.where(code(b) == 1, mm(high, flip) + mm(low, flip), tile)

        def ends(held, at, west_tile, east_tile):
            held = jnp.where(lane == at, rot(west_tile, at + 1), held)
            return jnp.where(lane == 64 + at, rot(east_tile, 64 + at), held)

        for b in range(n):
            span = slice(128 * b, 128 * b + 128)
            across = turned(all_ref[partner(b), 0], b).astype(BF)
            stack[first, :, span] = across
            tiles[b] = across.astype(F32)
            stack[1, :, span] = all_ref[b, 0]
            stack[last, :, span] = all_ref[b, 1]
        u = ring_sum(mm(a1, stack[...].reshape(3 * chans, n * cols)), chans)
        value, slope = gelu_parts(u)
        for b in range(n):
            hring[b] = value[:, 128 * b : 128 * b + 128].astype(BF)
        pole_ref[3] = tiles[me].astype(BF)
        none = jnp.zeros(block, F32)
        patch_ref[2] = ends(none, place, tiles[west], tiles[east])
        empty = jnp.zeros((chans, n * cols), BF)
        stack[first] = empty
        stack[1] = empty
        for b in range(n):
            stack[last, :, 128 * b : 128 * b + 128] = all_ref[b, 2]
        rim = ring_sum(mm(a2, stack[...].reshape(3 * chans, n * cols)), chans)
        for b in range(n):
            tiles[partner(b)] = turned_wide(rim[:, 128 * b : 128 * b + 128], b)
        for b in range(n):
            span = slice(128 * b, 128 * b + 128)
            stack[1, :, span] = all_ref[b, 2]
            stack[last, :, span] = all_ref[b, 3]
        back = ring_sum(mm(a2, stack[...].reshape(3 * chans, n * cols)), chans)
        for b in range(n):
            span = slice(128 * b, 128 * b + 128)
            dring[b] = (slope[:, span] * (back[:, span] + tiles[b])).astype(BF)
        stack[first] = empty
        stack[1] = empty
        origin = 0
        for b in range(n):
            stack[last, :, 128 * b : 128 * b + 128] = dring[b]
            origin = origin + jnp.where(partner(b) == me, b, 0)
        rim = ring_sum(mm(a3_ref[...], stack[...].reshape(3 * chans, n * cols)), chans)
        for b in range(n):
            tiles[b] = rim[:, 128 * b : 128 * b + 128]
        rim_ref[...] = turned_wide(tiles[origin], origin)
        pole_ref[0] = hring[me]
        pole_ref[1] = dring[me]
        pole_ref[2] = turned(hring[partner(me)], me).astype(BF)
        held = ends(none, place, turned(hring[partner(west)], west), turned(hring[partner(east)], east))
        patch_ref[0] = ends(held, inner, hring[west].astype(F32), hring[east].astype(F32))
        patch_ref[1] = ends(none, inner, dring[west].astype(F32), dring[east].astype(F32))


def rows_at_once(z1, z2, zx, zc, chans, place, h_ref, d_ref, at):
    for k in range(2):
        span = slice(128 * k, 128 * k + 128)
        u = joined(z1[:, span], chans, place + k, zx[:chans], zx[2 * chans :])
        back = joined(z2[:, span], chans, place + k, zc[:chans], zc[2 * chans :])
        value, slope = gelu_parts(u)
        h_ref[at + k] = value.astype(BF)
        d_ref[at + k] = (slope * back).astype(BF)


def finish_kernel(
    hin_ref, din_ref, pole_ref, patch_ref, x_ref, c_ref, sx_ref, sc_ref, got1_ref, got2_ref, a1_ref, a2_ref,
    h_ref, d_ref, hs_ref, ds_ref, g_ref,
    xe, ce, sxe, sce, acc1, acc2,
):
    rows, chans, cols = x_ref.shape
    lat = lax.axis_index("lat")
    even = lax.rem(lat, 2) == 0
    at_top = lat == 0
    at_bottom = lat == lax.axis_size("lat") - 1
    block = (chans, cols)
    lane = lax.broadcasted_iota(jnp.int32, block, 1)
    row_lane = lane % 64
    h_ref[2:rows] = hin_ref[2:rows]
    d_ref[2:rows] = din_ref[2:rows]

    xe[2 : rows + 2] = x_ref[...]
    ce[2 : rows + 2] = c_ref[...]
    corner_n = jnp.where(even, got2_ref[4].astype(F32), got1_ref[4].astype(F32))
    corner_s = jnp.where(even, got1_ref[4].astype(F32), got2_ref[4].astype(F32))

    def place_rows(north, south):
        xe[0:2] = north[0:2]
        ce[0:2] = north[2:4]
        xe[rows + 2 : rows + 4] = south[0:2]
        ce[rows + 2 : rows + 4] = south[2:4]

    @pl.when(even)
    def _():
        place_rows(got2_ref, got1_ref)

    @pl.when(jnp.logical_not(even))
    def _():
        place_rows(got1_ref, got2_ref)

    for at, (src, dst) in enumerate(((sx_ref, sxe), (sc_ref, sce))):
        for b in range(3):
            m = 3 * at + b
            piece = src[:, 128 * b : 128 * b + 128].astype(F32)
            piece = jnp.where(row_lane < 2, rot(corner_n, (-2 * m) % 128), piece)
            piece = jnp.where(
                (row_lane >= rows + 2) & (row_lane < rows + 4),
                rot(corner_s, (rows + 2 - 2 * m) % 128),
                piece,
            )
            dst[:, 128 * b : 128 * b + 128] = piece.astype(BF)

    a1 = a1_ref[...]
    a2 = a2_ref[...]
    zx = mm(a1, row_stack(sxe[...]))
    zc = mm(a2, row_stack(sce[...]))

    def three(z):
        return z[:chans, :128] + z[chans : 2 * chans, 128:256] + z[2 * chans :, 256:]

    value, slope = gelu_parts(three(zx))
    hs_ref[...] = value.astype(BF)
    ds_ref[...] = (slope * three(zc)).astype(BF)
    for t in (0, rows):
        rows_at_once(
            mm(a1, pair_of_rows(xe, t)), mm(a2, pair_of_rows(ce, t)),
            zx[:, 128:256], zc[:, 128:256], chans, t + 1, h_ref, d_ref, t,
        )

    @pl.when(at_top | at_bottom)
    def _():
        place = jnp.where(at_top, 1, rows + 2)
        inner = jnp.where(at_top, 2, rows + 1)
        outer_row = jnp.where(at_top, 0, rows + 1)
        inner_row = jnp.where(at_top, 1, rows)
        h_ref[inner_row] = pole_ref[0]
        d_ref[inner_row] = pole_ref[1]
        h_ref[outer_row] = pole_ref[2]
        d_ref[outer_row] = jnp.zeros(block, BF)
        xe[jnp.where(at_top, 1, rows + 2)] = pole_ref[3]
        at_place = row_lane == place
        at_pole = at_place | (row_lane == inner)
        hs_ref[...] = jnp.where(at_pole, patch_ref[0], hs_ref[...].astype(F32)).astype(BF)
        ds_ref[...] = jnp.where(at_pole, patch_ref[1], ds_ref[...].astype(F32)).astype(BF)
        sxe[:, 128:256] = jnp.where(at_place, patch_ref[2], sxe[:, 128:256].astype(F32)).astype(BF)

    own = (row_lane >= 2) & (row_lane < rows + 2)
    none = jnp.zeros(block, F32)

    def rim_terms(west_part, east_part):
        return jnp.concatenate(
            [
                jnp.where(own & (lane < 64), west_part, none),
                none,
                jnp.where(own & (lane >= 64), east_part, none),
            ],
            axis=0,
        ).astype(BF)

    sc = sce[...].astype(F32)
    acc2[...] = mm_t(rim_terms(sc[:, 256:], sc[:, :128]), row_stack(hs_ref[...]))

    def place_column(i, held):
        tile = d_ref[i + 1].astype(F32)
        held = jnp.where(lane == i + 2, rot(tile, i + 2), held)
        return jnp.where(lane == 66 + i, rot(tile, 67 + i), held)

    dcol = lax.fori_loop(0, rows, place_column, none, unroll=8)
    acc1[...] = mm_t(rim_terms(dcol, dcol), row_stack(sxe[:, 128:256]))

    def shifted_rows(ref, at):
        parts = []
        for k in range(2):
            tile = ref[at + k].astype(F32)
            ahead = jnp.where(lane == 127, 0.0, rot(tile, 127))
            behind = jnp.where(lane == 0, 0.0, rot(tile, 1))
            parts.append(jnp.concatenate([ahead, tile, behind], axis=0).astype(BF))
        return jnp.concatenate(parts, axis=1)

    def add_rows(step, _):
        y = 2 * step
        acc2[...] += mm_t(shifted_rows(ce, y + 2), pair_of_rows(h_ref, y))
        acc1[...] += mm_t(shifted_rows(d_ref, y + 1), pair_of_rows(xe, y + 1))
        return 0

    lax.fori_loop(0, rows // 2, add_rows, 0, unroll=UNROLL_G)
    g2 = acc2[...]
    g1 = acc1[...]
    g_ref[0] = g2[:, :128]
    g_ref[1] = g1[:, :128]
    g_ref[2] = jnp.concatenate([g2[:, 128:], g1[:, 128:]], axis=1)


def out_kernel(h_ref, hs_ref, b2_ref, out_ref):
    rows, chans, _ = out_ref.shape
    b2 = b2_ref[...]
    zh = mm(b2, row_stack(hs_ref[...]))

    def two_rows(step, _):
        t = 2 * step
        z = mm(b2, pair_of_rows(h_ref, t))
        for k in range(2):
            row = joined(z[:, 128 * k : 128 * k + 128], chans, t + k + 2, zh[:chans], zh[2 * chans :])
            out_ref[t + k] = row.astype(BF)
        return 0

    lax.fori_loop(0, rows // 2, two_rows, 0, unroll=UNROLL_O)


def fields_kernel(d_ref, ds_ref, rim_ref, b1_ref, out_ref):
    rows, chans, _ = out_ref.shape
    lat = lax.axis_index("lat")
    b1 = b1_ref[...]
    zd = mm(b1, row_stack(ds_ref[...]))

    def two_rows(step, _):
        t = 2 * step
        z = mm(b1, pair_of_rows(d_ref, t))
        for k in range(2):
            row = joined(z[:, 128 * k : 128 * k + 128], chans, t + k + 2, zd[:chans], zd[2 * chans :])
            rim_here = ((t + k == 0) & (lat == 0)) | (
                (t + k == rows - 1) & (lat == lax.axis_size("lat") - 1)
            )
            out_ref[t + k] = (row + jnp.where(rim_here, 1.0, 0.0) * rim_ref[...]).astype(BF)
        return 0

    lax.fori_loop(0, rows // 2, two_rows, 0, unroll=UNROLL_O)


def unpack_kernel(half_ref, other_ref, one_ref, two_ref, whole, *, scale):
    chans = one_ref.shape[2]
    lower = lax.rem(lax.axis_index("lon"), 2) == 0
    count = half_ref.shape[0]
    half = half_ref[...] * scale
    other = other_ref[...] * scale
    whole[:count] = jnp.where(lower, half, other)
    whole[count:] = jnp.where(lower, other, half)
    for at, ref in enumerate((two_ref, one_ref)):
        for s in range(3):
            wide = whole[(3 * at + s) * chans : (3 * at + s + 1) * chans]
            ref[0, s] = wide[:, :chans]
            ref[1, s] = wide[:, chans:]
            ref[2, s] = whole[(6 + s) * chans : (7 + s) * chans][:, chans * at : chans * at + chans]


def call(kernel, outs, args, scratch=(), flops=0, smem=0):
    space = [pl.BlockSpec(memory_space=pltpu.SMEM)] * smem
    space += [pl.BlockSpec(memory_space=pltpu.VMEM)] * (len(args) - smem)
    moved = sum(math.prod(a.shape) * a.dtype.itemsize for a in list(args) + list(outs))
    return pl.pallas_call(
        kernel,
        out_shape=tuple(outs),
        in_specs=space,
        out_specs=tuple(pl.BlockSpec(memory_space=pltpu.VMEM) for _ in outs),
        scratch_shapes=list(scratch),
        compiler_params=pltpu.CompilerParams(vmem_limit_bytes=VMEM_LIMIT),
        cost_estimate=pl.CostEstimate(flops=flops, bytes_accessed=moved, transcendentals=0),
    )(*args)


def on_device(
    fields_in, weight_one, weight_two, cotangent, north_map, north_code, south_map, south_code
):
    chans, rows, cols = fields_in.shape
    n = lax.axis_size("lon")
    lat_count = lax.axis_size("lat")
    pixel_total = rows * cols * n * lat_count
    shape = jax.ShapeDtypeStruct
    x = fields_in.transpose(1, 0, 2)
    c = cotangent.transpose(1, 0, 2)
    forward_one = weight_one.transpose(1, 2, 0, 3).reshape(3 * chans, 3 * chans)
    forward_two = weight_two.transpose(1, 2, 0, 3).reshape(3 * chans, 3 * chans)
    back_one = weight_one[::-1, ::-1].transpose(1, 3, 0, 2).reshape(3 * chans, 3 * chans)
    back_two = weight_two[::-1, ::-1].transpose(1, 3, 0, 2).reshape(3 * chans, 3 * chans)

    (packed,) = call(pack_kernel, [shape((6, chans, cols), BF)], [x, c])
    gathered = lax.all_gather(packed, "lon", axis=0)
    strip = shape((chans, 3 * cols), BF)
    five = shape((5, chans, cols), BF)
    sx, sc, to1, to2 = call(strip_kernel, [strip, strip, five, five], [x, c, gathered])
    mutual = [[(i, i ^ 1) for i in range(lat_count) if (i ^ 1) < lat_count], []]
    for i in range(1, lat_count - 1, 2):
        mutual[1] += [(i, i + 1), (i + 1, i)]
    got1 = lax.ppermute(to1, "lat", mutual[0])
    got2 = lax.ppermute(to2, "lat", mutual[1])

    conv_flops = 2 * 9 * chans * chans * rows * cols
    taller = shape((rows + 2, chans, cols), BF)
    edges = shape((chans, cols), BF)
    three_wide = shape((3, chans, cols), F32)
    h, d, pole, patch, rim = call(
        interior_kernel,
        [taller, taller, shape((4, chans, cols), BF), three_wide, shape((chans, cols), F32)],
        [north_map, north_code, south_map, south_code, x, c, gathered, sx, sc]
        + [forward_one, back_two, back_one],
        [
            pltpu.VMEM((3, chans, n * cols), BF),
            pltpu.VMEM((n, chans, cols), F32),
            pltpu.VMEM((n, chans, cols), BF),
            pltpu.VMEM((n, chans, cols), BF),
        ],
        flops=2 * conv_flops,
        smem=4,
    )
    h, d, hs, ds, grads = call(
        finish_kernel,
        [taller, taller, edges, edges, shape((3, 3 * chans, cols), F32)],
        [h, d, pole, patch, x, c, sx, sc, got1, got2, forward_one, back_two],
        [
            pltpu.VMEM((rows + 4, chans, cols), BF),
            pltpu.VMEM((rows + 4, chans, cols), BF),
            pltpu.VMEM((chans, 3 * cols), BF),
            pltpu.VMEM((chans, 3 * cols), BF),
            pltpu.VMEM((3 * chans, 3 * chans), F32),
            pltpu.VMEM((3 * chans, 3 * chans), F32),
        ],
        flops=2 * conv_flops,
    )

    flat = grads.reshape(2, -1, cols)
    mine = lax.axis_index("lon") % 2
    swap = [(i, i ^ 1) for i in range(n)]
    kept = lax.dynamic_index_in_dim(flat, mine, 0, keepdims=False)
    given = lax.dynamic_index_in_dim(flat, 1 - mine, 0, keepdims=False)
    half = kept + lax.ppermute(given, "lon", swap)
    bits = [1 << k for k in range((n * lat_count).bit_length() - 1) if 1 << k != lat_count]
    bits = bits[len(bits) // 2 :] + bits[: len(bits) // 2]
    low = shape((rows, chans, cols), BF)
    for k, bit in enumerate(bits):
        other_bit = bits[(k + len(bits) // 2) % len(bits)]
        pairs = [
            (i, i ^ (bit if i // lat_count % 2 == 0 else other_bit)) for i in range(n * lat_count)
        ]
        if k == 0:
            half, h = lax.optimization_barrier((half, h))
        if k == 1:
            half, d = lax.optimization_barrier((half, d))
        arrived = lax.ppermute(half, ("lon", "lat"), pairs)
        half = half + arrived
        if k == 0:
            (out,) = call(out_kernel, [low], [h, hs, forward_two], flops=conv_flops)
            out = out.transpose(1, 0, 2)
            half, out = lax.optimization_barrier((half, out))
        if k == 1:
            (d_fields,) = call(fields_kernel, [low], [d, ds, rim, back_one], flops=conv_flops)
            d_fields = d_fields.transpose(1, 0, 2)
            half, d_fields = lax.optimization_barrier((half, d_fields))
    other = lax.ppermute(half, "lon", swap)
    kernel_shape = shape(weight_one.shape, F32)
    one, two = call(
        functools.partial(unpack_kernel, scale=1.0 / math.sqrt(pixel_total)),
        [kernel_shape, kernel_shape],
        [half, other],
        [pltpu.VMEM((9 * chans, cols), F32)],
    )
    return (out, d_fields, one, two)


def solution(mesh):
    placed = (P(None, "lat", "lon"), P(), P(), P(None, "lat", "lon"), P(), P(), P(), P())
    return jax.shard_map(
        on_device,
        mesh=mesh,
        in_specs=placed,
        out_specs=(P(None, "lat", "lon"), P(None, "lat", "lon"), P(), P()),
        check_vma=False,
    )
```

```python
import functools
import math

import jax
import jax.numpy as jnp
from jax import lax
from jax.experimental import pallas as pl
from jax.experimental.pallas import tpu as pltpu
from jax.experimental.layout import Layout, with_layout_constraint
from jax.sharding import PartitionSpec as P

BF = jnp.bfloat16
F32 = jnp.float32
GELU_K = math.sqrt(2.0 / math.pi)
VMEM_LIMIT = 48 * 1024 * 1024
UNROLL = 5
UNROLL_G = 4
UNROLL_O = 4


def mm(a, b):
    return jnp.dot(a, b, preferred_element_type=F32)


def mm_t(a, b):
    return lax.dot_general(a, b, (((1,), (1,)), ((), ())), preferred_element_type=F32)


def lane_of(like):
    return lax.broadcasted_iota(jnp.int32, like.shape, like.ndim - 1)


def rot(x, by):
    return pltpu.roll(x, by, x.ndim - 1)


def gelu_parts(u):
    square = u * u
    t = jnp.tanh(GELU_K * u * (1.0 + 0.044715 * square))
    half = 0.5 + 0.5 * t
    slope = half + (0.5 * GELU_K) * u * (1.0 - t * t) * (1.0 + (3 * 0.044715) * square)
    return u * half, slope


def arrange(w_ref, forward_ref, back_ref):
    chans = w_ref.shape[2]
    diagonal = lax.broadcasted_iota(jnp.int32, (chans, chans), 0) == lax.broadcasted_iota(
        jnp.int32, (chans, chans), 1
    )
    eye = jnp.where(diagonal, 1.0, 0.0).astype(BF)
    for s in range(3):
        here = slice(s * chans, (s + 1) * chans)
        forward_ref[here] = jnp.concatenate([w_ref[r, s] for r in range(3)], axis=1)
        flipped = jnp.concatenate([w_ref[2 - r, 2 - s] for r in range(3)], axis=0)
        back_ref[here] = mm_t(eye, flipped).astype(BF)


def pack_kernel(x_ref, c_ref, w1_ref, w2_ref, out_ref, f1_ref, b1_ref, f2_ref, b2_ref):
    arrange(w1_ref, f1_ref, b1_ref)
    arrange(w2_ref, f2_ref, b2_ref)
    rows = x_ref.shape[0]
    bottom = jnp.where(lax.axis_index("lat") == 0, 0, 1)
    edge = bottom * (rows - 1)
    beside = 1 + bottom * (rows - 3)
    out_ref[0] = x_ref[edge]
    out_ref[1] = x_ref[beside]
    out_ref[2] = c_ref[edge]
    out_ref[3] = c_ref[beside]
    for at, ref in ((4, x_ref), (5, c_ref)):
        packed = jnp.zeros(ref.shape[1:], F32)
        lane = lane_of(packed)
        for i in range(rows):
            turned = rot(ref[i].astype(F32), (4 * i + 2) % 128)
            packed = jnp.where((lane >= 4 * i) & (lane < 4 * i + 4), turned, packed)
        out_ref[at] = packed.astype(BF)


def strip_kernel(x_ref, c_ref, all_ref, sx_ref, sc_ref, to1_ref, to2_ref):
    rows, chans, cols = x_ref.shape
    n = all_ref.shape[0]
    me = lax.axis_index("lon")
    west = lax.rem(me + n - 1, n)
    east = lax.rem(me + 1, n)
    target = lax.broadcasted_iota(jnp.int32, (3 * cols, 3 * cols), 1)
    source = lax.broadcasted_iota(jnp.int32, (3 * cols, 3 * cols), 0)
    block = target // 128
    side = (target % 128) // 64
    row = target % 64 - 2
    origin = jnp.where(side == 0, block // 2, 1 + (block + 1) // 2)
    wanted = 128 * origin + 4 * row + block + side
    hit = (source == wanted) & (row >= 0) & (row < rows)
    chooser = jnp.where(hit, 1.0, 0.0).astype(BF)
    to_south = jnp.zeros((chans, cols), F32)
    to_north = jnp.zeros((chans, cols), F32)
    lane = lane_of(to_south)
    pair = (lane % 64) // 2
    for at, ref in ((0, sx_ref), (1, sc_ref)):
        taken = jnp.concatenate([all_ref[west, 4 + at], all_ref[me, 4 + at], all_ref[east, 4 + at]], axis=1)
        strip = mm(taken, chooser)
        ref[...] = strip.astype(BF)
        for b in range(3):
            m = 3 * at + b
            piece = strip[:, 128 * b : 128 * b + 128]
            to_south = jnp.where(pair == m, rot(piece, (2 * m - rows) % 128), to_south)
            to_north = jnp.where(pair == m, rot(piece, (2 * m - 2) % 128), to_north)
    odd = lax.rem(lax.axis_index("lat"), 2)
    for ref, northward in ((to1_ref, odd), (to2_ref, 1 - odd)):
        start = (rows - 2) * (1 - northward)
        for k in range(2):
            ref[k] = x_ref[start + k]
            ref[2 + k] = c_ref[start + k]
        ref[4] = jnp.where(northward == 1, to_north, to_south).astype(BF)


def row_stack(strip):
    wide = strip.astype(F32)
    parts = [wide[:, at : at + 128] for at in range(0, wide.shape[1], 128)]
    above = jnp.concatenate([rot(p, 1) for p in parts], axis=1).astype(BF)
    below = jnp.concatenate([rot(p, 127) for p in parts], axis=1).astype(BF)
    return jnp.concatenate([above, strip, below], axis=0)


def joined(z, chans, place, edge_w, edge_e):
    lane = lane_of(edge_w)
    low = jnp.where(lane == 0, rot(edge_w, 128 - place), rot(z[:chans], 1))
    high = jnp.where(lane == 127, rot(edge_e, 63 - place), rot(z[2 * chans :], 127))
    return low + z[chans : 2 * chans] + high


def pair_of_rows(ref, at):
    four = ref[pl.ds(at, 4)]
    _, chans, cols = four.shape
    return jnp.concatenate(
        [four[:3].reshape(3 * chans, cols), four[1:].reshape(3 * chans, cols)], axis=1
    )


def ring_sum(z, chans):
    return rot(z[:chans], 1) + z[chans : 2 * chans] + rot(z[2 * chans :], z.shape[1] - 1)


def interior_kernel(
    nmap_hbm, ncode_hbm, smap_hbm, scode_hbm, x_ref, c_ref, all_ref, sx_ref, sc_ref, a1_ref, a2_ref, a3_ref,
    h_ref, d_ref, pole_ref, patch_ref, rim_ref,
    stack, tiles, hring, dring, nmap, ncode, smap, scode, sems,
):
    tables = [
        pltpu.make_async_copy(src, dst, sems.at[k])
        for k, (src, dst) in enumerate(
            ((nmap_hbm, nmap), (ncode_hbm, ncode), (smap_hbm, smap), (scode_hbm, scode))
        )
    ]
    for table in tables:
        table.start()
    rows, chans, cols = x_ref.shape
    n = all_ref.shape[0]
    lat = lax.axis_index("lat")
    me = lax.axis_index("lon")
    at_top = lat == 0
    at_bottom = lat == lax.axis_size("lat") - 1
    block = (chans, cols)
    lane = lax.broadcasted_iota(jnp.int32, block, 1)
    a1 = a1_ref[...]
    a2 = a2_ref[...]
    zx = mm(a1, row_stack(sx_ref[:, 128:256]))
    zc = mm(a2, row_stack(sc_ref[:, 128:256]))

    def two_rows(step, _):
        y = 1 + 2 * step
        rows_at_once(
            mm(a1, pair_of_rows(x_ref, y - 1)), mm(a2, pair_of_rows(c_ref, y - 1)),
            zx, zc, chans, y + 2, h_ref, d_ref, y + 1,
        )
        return 0

    lax.fori_loop(0, (rows - 2) // 2, two_rows, 0, unroll=UNROLL)
    rim_ref[...] = jnp.zeros(block, F32)
    for table in tables:
        table.wait()

    @pl.when(at_top | at_bottom)
    def _():
        west = lax.rem(me + n - 1, n)
        east = lax.rem(me + 1, n)
        first = jnp.where(at_top, 0, 2)
        last = 2 - first
        place = jnp.where(at_top, 1, rows + 2)
        inner = jnp.where(at_top, 2, rows + 1)
        flip = jnp.where(
            lax.broadcasted_iota(jnp.int32, (cols, cols), 0)
            + lax.broadcasted_iota(jnp.int32, (cols, cols), 1)
            == cols - 1,
            1.0,
            0.0,
        ).astype(BF)

        def partner(b):
            return jnp.where(at_top, nmap[b], smap[b])

        def code(b):
            return jnp.where(at_top, ncode[b], scode[b])

        def turned(tile, b):
            return jnp.where(code(b) == 1, mm(tile, flip), tile.astype(F32))

        def turned_wide(tile, b):
            high = tile.astype(BF)
            low = (tile - high.astype(F32)).astype(BF)
            return jnp.where(code(b) == 1, mm(high, flip) + mm(low, flip), tile)

        def ends(held, at, west_tile, east_tile):
            held = jnp.where(lane == at, rot(west_tile, at + 1), held)
            return jnp.where(lane == 64 + at, rot(east_tile, 64 + at), held)

        for b in range(n):
            span = slice(128 * b, 128 * b + 128)
            across = turned(all_ref[partner(b), 0], b).astype(BF)
            stack[first, :, span] = across
            tiles[b] = across.astype(F32)
            stack[1, :, span] = all_ref[b, 0]
            stack[last, :, span] = all_ref[b, 1]
        u = ring_sum(mm(a1, stack[...].reshape(3 * chans, n * cols)), chans)
        value, slope = gelu_parts(u)
        for b in range(n):
            hring[b] = value[:, 128 * b : 128 * b + 128].astype(BF)
        pole_ref[3] = tiles[me].astype(BF)
        none = jnp.zeros(block, F32)
        patch_ref[2] = ends(none, place, tiles[west], tiles[east])
        empty = jnp.zeros((chans, n * cols), BF)
        stack[first] = empty
        stack[1] = empty
        for b in range(n):
            stack[last, :, 128 * b : 128 * b + 128] = all_ref[b, 2]
        rim = ring_sum(mm(a2, stack[...].reshape(3 * chans, n * cols)), chans)
        for b in range(n):
            tiles[partner(b)] = turned_wide(rim[:, 128 * b : 128 * b + 128], b)
        for b in range(n):
            span = slice(128 * b, 128 * b + 128)
            stack[1, :, span] = all_ref[b, 2]
            stack[last, :, span] = all_ref[b, 3]
        back = ring_sum(mm(a2, stack[...].reshape(3 * chans, n * cols)), chans)
        for b in range(n):
            span = slice(128 * b, 128 * b + 128)
            dring[b] = (slope[:, span] * (back[:, span] + tiles[b])).astype(BF)
        stack[first] = empty
        stack[1] = empty
        origin = 0
        for b in range(n):
            stack[last, :, 128 * b : 128 * b + 128] = dring[b]
            origin = origin + jnp.where(partner(b) == me, b, 0)
        rim = ring_sum(mm(a3_ref[...], stack[...].reshape(3 * chans, n * cols)), chans)
        for b in range(n):
            tiles[b] = rim[:, 128 * b : 128 * b + 128]
        rim_ref[...] = turned_wide(tiles[origin], origin)
        pole_ref[0] = hring[me]
        pole_ref[1] = dring[me]
        pole_ref[2] = turned(hring[partner(me)], me).astype(BF)
        held = ends(none, place, turned(hring[partner(west)], west), turned(hring[partner(east)], east))
        patch_ref[0] = ends(held, inner, hring[west].astype(F32), hring[east].astype(F32))
        patch_ref[1] = ends(none, inner, dring[west].astype(F32), dring[east].astype(F32))


def rows_at_once(z1, z2, zx, zc, chans, place, h_ref, d_ref, at):
    for k in range(2):
        span = slice(128 * k, 128 * k + 128)
        u = joined(z1[:, span], chans, place + k, zx[:chans], zx[2 * chans :])
        back = joined(z2[:, span], chans, place + k, zc[:chans], zc[2 * chans :])
        value, slope = gelu_parts(u)
        h_ref[at + k] = value.astype(BF)
        d_ref[at + k] = (slope * back).astype(BF)


def finish_kernel(
    hin_ref, din_ref, pole_ref, patch_ref, x_ref, c_ref, sx_ref, sc_ref, got1_ref, got2_ref, a1_ref, a2_ref,
    h_ref, d_ref, hs_ref, ds_ref, g_ref,
    xe, ce, sxe, sce, acc1, acc2,
):
    rows, chans, cols = x_ref.shape
    lat = lax.axis_index("lat")
    even = lax.rem(lat, 2) == 0
    at_top = lat == 0
    at_bottom = lat == lax.axis_size("lat") - 1
    block = (chans, cols)
    lane = lax.broadcasted_iota(jnp.int32, block, 1)
    row_lane = lane % 64
    h_ref[2:rows] = hin_ref[2:rows]
    d_ref[2:rows] = din_ref[2:rows]

    xe[2 : rows + 2] = x_ref[...]
    ce[2 : rows + 2] = c_ref[...]
    corner_n = jnp.where(even, got2_ref[4].astype(F32), got1_ref[4].astype(F32))
    corner_s = jnp.where(even, got1_ref[4].astype(F32), got2_ref[4].astype(F32))

    def place_rows(north, south):
        xe[0:2] = north[0:2]
        ce[0:2] = north[2:4]
        xe[rows + 2 : rows + 4] = south[0:2]
        ce[rows + 2 : rows + 4] = south[2:4]

    @pl.when(even)
    def _():
        place_rows(got2_ref, got1_ref)

    @pl.when(jnp.logical_not(even))
    def _():
        place_rows(got1_ref, got2_ref)

    for at, (src, dst) in enumerate(((sx_ref, sxe), (sc_ref, sce))):
        for b in range(3):
            m = 3 * at + b
            piece = src[:, 128 * b : 128 * b + 128].astype(F32)
            piece = jnp.where(row_lane < 2, rot(corner_n, (-2 * m) % 128), piece)
            piece = jnp.where(
                (row_lane >= rows + 2) & (row_lane < rows + 4),
                rot(corner_s, (rows + 2 - 2 * m) % 128),
                piece,
            )
            dst[:, 128 * b : 128 * b + 128] = piece.astype(BF)

    a1 = a1_ref[...]
    a2 = a2_ref[...]
    zx = mm(a1, row_stack(sxe[...]))
    zc = mm(a2, row_stack(sce[...]))

    def three(z):
        return z[:chans, :128] + z[chans : 2 * chans, 128:256] + z[2 * chans :, 256:]

    value, slope = gelu_parts(three(zx))
    hs_ref[...] = value.astype(BF)
    ds_ref[...] = (slope * three(zc)).astype(BF)
    for t in (0, rows):
        rows_at_once(
            mm(a1, pair_of_rows(xe, t)), mm(a2, pair_of_rows(ce, t)),
            zx[:, 128:256], zc[:, 128:256], chans, t + 1, h_ref, d_ref, t,
        )

    @pl.when(at_top | at_bottom)
    def _():
        place = jnp.where(at_top, 1, rows + 2)
        inner = jnp.where(at_top, 2, rows + 1)
        outer_row = jnp.where(at_top, 0, rows + 1)
        inner_row = jnp.where(at_top, 1, rows)
        h_ref[inner_row] = pole_ref[0]
        d_ref[inner_row] = pole_ref[1]
        h_ref[outer_row] = pole_ref[2]
        d_ref[outer_row] = jnp.zeros(block, BF)
        xe[jnp.where(at_top, 1, rows + 2)] = pole_ref[3]
        at_place = row_lane == place
        at_pole = at_place | (row_lane == inner)
        hs_ref[...] = jnp.where(at_pole, patch_ref[0], hs_ref[...].astype(F32)).astype(BF)
        ds_ref[...] = jnp.where(at_pole, patch_ref[1], ds_ref[...].astype(F32)).astype(BF)
        sxe[:, 128:256] = jnp.where(at_place, patch_ref[2], sxe[:, 128:256].astype(F32)).astype(BF)

    own = (row_lane >= 2) & (row_lane < rows + 2)
    none = jnp.zeros(block, F32)

    def rim_terms(west_part, east_part):
        return jnp.concatenate(
            [
                jnp.where(own & (lane < 64), west_part, none),
                none,
                jnp.where(own & (lane >= 64), east_part, none),
            ],
            axis=0,
        ).astype(BF)

    sc = sce[...].astype(F32)
    acc2[...] = mm_t(rim_terms(sc[:, 256:], sc[:, :128]), row_stack(hs_ref[...]))

    def place_column(i, held):
        tile = d_ref[i + 1].astype(F32)
        held = jnp.where(lane == i + 2, rot(tile, i + 2), held)
        return jnp.where(lane == 66 + i, rot(tile, 67 + i), held)

    dcol = lax.fori_loop(0, rows, place_column, none, unroll=8)
    acc1[...] = mm_t(rim_terms(dcol, dcol), row_stack(sxe[:, 128:256]))

    def shifted_rows(ref, at):
        parts = []
        for k in range(2):
            tile = ref[at + k].astype(F32)
            ahead = jnp.where(lane == 127, 0.0, rot(tile, 127))
            behind = jnp.where(lane == 0, 0.0, rot(tile, 1))
            parts.append(jnp.concatenate([ahead, tile, behind], axis=0).astype(BF))
        return jnp.concatenate(parts, axis=1)

    def add_rows(step, _):
        y = 2 * step
        acc2[...] += mm_t(shifted_rows(ce, y + 2), pair_of_rows(h_ref, y))
        acc1[...] += mm_t(shifted_rows(d_ref, y + 1), pair_of_rows(xe, y + 1))
        return 0

    lax.fori_loop(0, rows // 2, add_rows, 0, unroll=UNROLL_G)
    g2 = acc2[...]
    g1 = acc1[...]
    g_ref[0] = g2[:, :128]
    g_ref[1] = g1[:, :128]
    g_ref[2] = jnp.concatenate([g2[:, 128:], g1[:, 128:]], axis=1)


def out_kernel(h_ref, hs_ref, b2_ref, out_ref):
    rows, chans, _ = out_ref.shape
    b2 = b2_ref[...]
    zh = mm(b2, row_stack(hs_ref[...]))

    def two_rows(step, _):
        t = 2 * step
        z = mm(b2, pair_of_rows(h_ref, t))
        for k in range(2):
            row = joined(z[:, 128 * k : 128 * k + 128], chans, t + k + 2, zh[:chans], zh[2 * chans :])
            out_ref[t + k] = row.astype(BF)
        return 0

    lax.fori_loop(0, rows // 2, two_rows, 0, unroll=UNROLL_O)


def fields_kernel(d_ref, ds_ref, rim_ref, b1_ref, out_ref):
    rows, chans, _ = out_ref.shape
    lat = lax.axis_index("lat")
    b1 = b1_ref[...]
    zd = mm(b1, row_stack(ds_ref[...]))

    def two_rows(step, _):
        t = 2 * step
        z = mm(b1, pair_of_rows(d_ref, t))
        for k in range(2):
            row = joined(z[:, 128 * k : 128 * k + 128], chans, t + k + 2, zd[:chans], zd[2 * chans :])
            rim_here = ((t + k == 0) & (lat == 0)) | (
                (t + k == rows - 1) & (lat == lax.axis_size("lat") - 1)
            )
            out_ref[t + k] = (row + jnp.where(rim_here, 1.0, 0.0) * rim_ref[...]).astype(BF)
        return 0

    lax.fori_loop(0, rows // 2, two_rows, 0, unroll=UNROLL_O)


def unpack_kernel(half_ref, other_ref, one_ref, two_ref, whole, *, scale):
    chans = one_ref.shape[2]
    lower = lax.rem(lax.axis_index("lon"), 2) == 0
    count = half_ref.shape[0]
    half = half_ref[...] * scale
    other = other_ref[...] * scale
    whole[:count] = jnp.where(lower, half, other)
    whole[count:] = jnp.where(lower, other, half)
    for at, ref in enumerate((two_ref, one_ref)):
        for s in range(3):
            wide = whole[(3 * at + s) * chans : (3 * at + s + 1) * chans]
            ref[0, s] = wide[:, :chans]
            ref[1, s] = wide[:, chans:]
            ref[2, s] = whole[(6 + s) * chans : (7 + s) * chans][:, chans * at : chans * at + chans]


def call(kernel, outs, args, scratch=(), flops=0, anywhere=0):
    space = [pl.BlockSpec(memory_space=pl.ANY)] * anywhere
    space += [pl.BlockSpec(memory_space=pltpu.VMEM)] * (len(args) - anywhere)
    moved = sum(math.prod(a.shape) * a.dtype.itemsize for a in list(args) + list(outs))
    return pl.pallas_call(
        kernel,
        out_shape=tuple(outs),
        in_specs=space,
        out_specs=tuple(pl.BlockSpec(memory_space=pltpu.VMEM) for _ in outs),
        scratch_shapes=list(scratch),
        compiler_params=pltpu.CompilerParams(vmem_limit_bytes=VMEM_LIMIT),
        cost_estimate=pl.CostEstimate(flops=flops, bytes_accessed=moved, transcendentals=0),
    )(*args)


def native(rows_first):
    return with_layout_constraint(rows_first.transpose(1, 0, 2), Layout((0, 1, 2)))


def on_device(
    fields_in, weight_one, weight_two, cotangent, north_map, north_code, south_map, south_code
):
    chans, rows, cols = fields_in.shape
    n = lax.axis_size("lon")
    lat_count = lax.axis_size("lat")
    pixel_total = rows * cols * n * lat_count
    shape = jax.ShapeDtypeStruct
    x = fields_in.transpose(1, 0, 2)
    c = cotangent.transpose(1, 0, 2)
    square = shape((3 * chans, 3 * chans), BF)
    packed, forward_one, back_one, forward_two, back_two = call(
        pack_kernel, [shape((6, chans, cols), BF)] + [square] * 4, [x, c, weight_one, weight_two]
    )
    gathered = lax.all_gather(packed, "lon", axis=0)
    strip = shape((chans, 3 * cols), BF)
    five = shape((5, chans, cols), BF)
    sx, sc, to1, to2 = call(strip_kernel, [strip, strip, five, five], [x, c, gathered])
    mutual = [[(i, i ^ 1) for i in range(lat_count) if (i ^ 1) < lat_count], []]
    for i in range(1, lat_count - 1, 2):
        mutual[1] += [(i, i + 1), (i + 1, i)]
    got1 = lax.ppermute(to1, "lat", mutual[0])
    got2 = lax.ppermute(to2, "lat", mutual[1])

    conv_flops = 2 * 9 * chans * chans * rows * cols
    taller = shape((rows + 2, chans, cols), BF)
    edges = shape((chans, cols), BF)
    three_wide = shape((3, chans, cols), F32)
    h, d, pole, patch, rim = call(
        interior_kernel,
        [taller, taller, shape((4, chans, cols), BF), three_wide, shape((chans, cols), F32)],
        [north_map, north_code, south_map, south_code, x, c, gathered, sx, sc]
        + [forward_one, back_two, back_one],
        [
            pltpu.VMEM((3, chans, n * cols), BF),
            pltpu.VMEM((n, chans, cols), F32),
            pltpu.VMEM((n, chans, cols), BF),
            pltpu.VMEM((n, chans, cols), BF),
        ]
        + [pltpu.SMEM((n,), jnp.int32)] * 4
        + [pltpu.SemaphoreType.DMA((4,))],
        flops=2 * conv_flops,
        anywhere=4,
    )
    h, d, hs, ds, grads = call(
        finish_kernel,
        [taller, taller, edges, edges, shape((3, 3 * chans, cols), F32)],
        [h, d, pole, patch, x, c, sx, sc, got1, got2, forward_one, back_two],
        [
            pltpu.VMEM((rows + 4, chans, cols), BF),
            pltpu.VMEM((rows + 4, chans, cols), BF),
            pltpu.VMEM((chans, 3 * cols), BF),
            pltpu.VMEM((chans, 3 * cols), BF),
            pltpu.VMEM((3 * chans, 3 * chans), F32),
            pltpu.VMEM((3 * chans, 3 * chans), F32),
        ],
        flops=2 * conv_flops,
    )

    flat = grads.reshape(2, -1, cols)
    mine = lax.axis_index("lon") % 2
    swap = [(i, i ^ 1) for i in range(n)]
    kept = lax.dynamic_index_in_dim(flat, mine, 0, keepdims=False)
    given = lax.dynamic_index_in_dim(flat, 1 - mine, 0, keepdims=False)
    half = kept + lax.ppermute(given, "lon", swap)
    device_count = n * lat_count
    bits = [1 << k for k in range(device_count.bit_length() - 1) if 1 << k != lat_count]
    groups = [bits[k : k + 2] for k in range(0, len(bits) - 1, 2)]
    middle = len(groups) // 2
    left = [bits[-1:]] if len(bits) % 2 else []
    orders = groups[middle:] + groups[:middle] + left, groups + left
    stages = len(orders[0])
    low = shape((rows, chans, cols), BF)
    for k in range(stages):
        sent = half.astype(F32 if k < stages - 1 else BF)
        if k == 0:
            sent, h = lax.optimization_barrier((sent, h))
        if k == 1:
            sent, d = lax.optimization_barrier((sent, d))
        got = [sent]
        for step in range(1, 1 << len(orders[0][k])):
            jumps = [sum(bit for at, bit in enumerate(order[k]) if step >> at & 1) for order in orders]
            pairs = [(i, i ^ jumps[i // lat_count % 2]) for i in range(device_count)]
            got.append(lax.ppermute(sent, ("lon", "lat"), pairs))
        got = [part.astype(F32) for part in got]
        half = (got[0] + got[1]) + (got[2] + got[3]) if len(got) == 4 else got[0] + got[1]
        if k == 0:
            (out,) = call(out_kernel, [low], [h, hs, forward_two], flops=conv_flops)
            out = native(out)
            half, out = lax.optimization_barrier((half, out))
        if k == 1:
            (d_fields,) = call(fields_kernel, [low], [d, ds, rim, back_one], flops=conv_flops)
            d_fields = native(d_fields)
            half, d_fields = lax.optimization_barrier((half, d_fields))
    other = lax.ppermute(half, "lon", swap)
    kernel_shape = shape(weight_one.shape, F32)
    one, two = call(
        functools.partial(unpack_kernel, scale=1.0 / math.sqrt(pixel_total)),
        [kernel_shape, kernel_shape],
        [half, other],
        [pltpu.VMEM((9 * chans, cols), F32)],
    )
    return (out, d_fields, one, two)


def solution(mesh):
    placed = (P(None, "lat", "lon"), P(), P(), P(None, "lat", "lon"), P(), P(), P(), P())
    return jax.shard_map(
        on_device,
        mesh=mesh,
        in_specs=placed,
        out_specs=(P(None, "lat", "lon"), P(None, "lat", "lon"), P(), P()),
        check_vma=False,
    )
```

```python
import functools
import math

import jax
import jax.numpy as jnp
from jax import lax
from jax.experimental import pallas as pl
from jax.experimental.pallas import tpu as pltpu
from jax.experimental.layout import Layout, with_layout_constraint
from jax.sharding import PartitionSpec as P

BF = jnp.bfloat16
F32 = jnp.float32
GELU_K = math.sqrt(2.0 / math.pi)
VMEM_LIMIT = 48 * 1024 * 1024


def mm(a, b):
    return jnp.dot(a, b, preferred_element_type=F32)


def mm_t(a, b):
    return lax.dot_general(a, b, (((1,), (1,)), ((), ())), preferred_element_type=F32)


def lane_of(like):
    return lax.broadcasted_iota(jnp.int32, like.shape, like.ndim - 1)


def rot(x, by):
    return pltpu.roll(x, by, x.ndim - 1)


def gelu_parts(u):
    square = u * u
    t = jnp.tanh(GELU_K * u * (1.0 + 0.044715 * square))
    half = 0.5 + 0.5 * t
    slope = half + (0.5 * GELU_K) * u * (1.0 - t * t) * (1.0 + (3 * 0.044715) * square)
    return u * half, slope


def arrange(w_ref, forward_ref, back_ref):
    chans = w_ref.shape[2]
    diagonal = lax.broadcasted_iota(jnp.int32, (chans, chans), 0) == lax.broadcasted_iota(
        jnp.int32, (chans, chans), 1
    )
    eye = jnp.where(diagonal, 1.0, 0.0).astype(BF)
    for s in range(3):
        here = slice(s * chans, (s + 1) * chans)
        forward_ref[here] = jnp.concatenate([w_ref[r, s] for r in range(3)], axis=1)
        flipped = jnp.concatenate([w_ref[2 - r, 2 - s] for r in range(3)], axis=0)
        back_ref[here] = mm_t(eye, flipped).astype(BF)


def pack_kernel(x_ref, c_ref, out_ref):
    rows = x_ref.shape[0]
    bottom = jnp.where(lax.axis_index("lat") == 0, 0, 1)
    edge = bottom * (rows - 1)
    beside = 1 + bottom * (rows - 3)
    out_ref[0] = x_ref[edge]
    out_ref[1] = x_ref[beside]
    out_ref[2] = c_ref[edge]
    out_ref[3] = c_ref[beside]
    for at, ref in ((4, x_ref), (5, c_ref)):
        packed = jnp.zeros(ref.shape[1:], F32)
        lane = lane_of(packed)
        for i in range(rows):
            turned = rot(ref[i].astype(F32), (4 * i + 2) % 128)
            packed = jnp.where((lane >= 4 * i) & (lane < 4 * i + 4), turned, packed)
        out_ref[at] = packed.astype(BF)


def strip_kernel(
    nmap, ncode, smap, scode, x_ref, c_ref, all_ref, w1_ref, w2_ref,
    table_ref, sx_ref, sc_ref, south_ref, north_ref, f1_ref, b1_ref, f2_ref, b2_ref,
):
    for k, ref in enumerate((nmap, ncode, smap, scode)):
        table_ref[k : k + 1] = ref[...].reshape(1, ref.shape[0])
    arrange(w1_ref, f1_ref, b1_ref)
    arrange(w2_ref, f2_ref, b2_ref)
    rows, chans, cols = x_ref.shape
    n = all_ref.shape[0]
    me = lax.axis_index("lon")
    west = lax.rem(me + n - 1, n)
    east = lax.rem(me + 1, n)
    target = lax.broadcasted_iota(jnp.int32, (3 * cols, 4 * cols), 1)
    source = lax.broadcasted_iota(jnp.int32, (3 * cols, 4 * cols), 0)
    block = target // 128
    side = (target % 128) // 64
    row = target % 64 - 2
    wanted = 128 * (side + block // 2) + 4 * row + block
    hit = (source == wanted) & (row >= 0) & (row < rows)
    chooser = jnp.where(hit, 1.0, 0.0).astype(BF)
    to_south = jnp.zeros((chans, cols), F32)
    to_north = jnp.zeros((chans, cols), F32)
    lane = lane_of(to_south)
    pair = (lane % 64) // 2
    for at, ref in ((0, sx_ref), (1, sc_ref)):
        taken = jnp.concatenate([all_ref[west, 4 + at], all_ref[me, 4 + at], all_ref[east, 4 + at]], axis=1)
        strip = mm(taken, chooser)
        ref[...] = strip.astype(BF)
        for b in range(4):
            m = 4 * at + b
            piece = strip[:, 128 * b : 128 * b + 128]
            to_south = jnp.where(pair == m, rot(piece, (2 * m - rows) % 128), to_south)
            to_north = jnp.where(pair == m, rot(piece, (2 * m - 2) % 128), to_north)
    for ref, start, corner in ((south_ref, rows - 2, to_south), (north_ref, 0, to_north)):
        for k in range(2):
            ref[k] = x_ref[start + k]
            ref[2 + k] = c_ref[start + k]
        ref[4] = corner.astype(BF)


def row_stack(strip):
    wide = strip.astype(F32)
    parts = [wide[:, at : at + 128] for at in range(0, wide.shape[1], 128)]
    above = jnp.concatenate([rot(p, 1) for p in parts], axis=1).astype(BF)
    below = jnp.concatenate([rot(p, 127) for p in parts], axis=1).astype(BF)
    return jnp.concatenate([above, strip, below], axis=0)


def joined(z, chans, place, edge_w, edge_e):
    lane = lane_of(edge_w)
    low = jnp.where(lane == 0, rot(edge_w, 128 - place), rot(z[:chans], 1))
    high = jnp.where(lane == 127, rot(edge_e, 63 - place), rot(z[2 * chans :], 127))
    return low + z[chans : 2 * chans] + high


def pair_of_rows(ref, at):
    four = ref[pl.ds(at, 4)]
    _, chans, cols = four.shape
    return jnp.concatenate(
        [four[:3].reshape(3 * chans, cols), four[1:].reshape(3 * chans, cols)], axis=1
    )


def ring_sum(z, chans):
    return rot(z[:chans], 1) + z[chans : 2 * chans] + rot(z[2 * chans :], z.shape[1] - 1)


def with_edges(a, west, east, group):
    chans = west.shape[0]
    parts = []
    for edge, start in ((west, 16 * group), (east, 64 + 16 * group)):
        term = edge[:, start : start + 16]
        high = term.astype(BF).astype(F32)
        parts += [high, term - high]
    middle = jnp.concatenate(parts, axis=1)
    none = jnp.zeros_like(middle)
    return jnp.concatenate([a, jnp.concatenate([none, middle, none], axis=0).astype(BF)], axis=1)


def interior_kernel(
    table_ref, x_ref, c_ref, all_ref, sx_ref, sc_ref, a1_ref, a2_ref, a3_ref,
    h_ref, d_ref, pole_ref, patch_ref, rim_ref,
    hot, picked, stack, around, slopes, tiles, hring, dring, table, table_sem,
):
    fetch = pltpu.make_async_copy(table_ref, table, table_sem)
    fetch.start()
    rows, chans, cols = x_ref.shape
    a1 = a1_ref[...]
    a2 = a2_ref[...]
    zx = mm(a1, row_stack(sx_ref[:, 128:384]))
    zc = mm(a2, row_stack(sc_ref[:, 128:384]))
    groups = range((rows + 2) // 16 + 1)
    a1_edges = [with_edges(a1, zx[:chans, :128], zx[2 * chans :, 128:], g) for g in groups]
    a2_edges = [with_edges(a2, zc[:chans, :128], zc[2 * chans :, 128:], g) for g in groups]
    lane = lax.broadcasted_iota(jnp.int32, (chans, cols), 1)
    spot = lax.broadcasted_iota(jnp.int32, (chans, cols), 0)
    end = lane == jnp.where(spot < 32, 0, cols - 1)
    for m in range(16):
        hot[m] = jnp.where(end & (spot % 16 == m), 1.0, 0.0).astype(BF)

    def summed(z):
        low = jnp.where(lane == 0, 0.0, rot(z[:chans], 1))
        high = jnp.where(lane == cols - 1, 0.0, rot(z[2 * chans :], 127))
        return low + z[chans : 2 * chans] + high

    def product(choices, ref, y):
        four = ref[y - 1 : y + 3]
        halves = [
            jnp.concatenate([four[k : k + 3].reshape(3 * chans, cols), hot[(y + 2 + k) % 16]], axis=0)
            for k in range(2)
        ]
        if (y + 2) // 16 == (y + 3) // 16:
            z = mm(choices[(y + 2) // 16], jnp.concatenate(halves, axis=1))
            return z[:, :cols], z[:, cols:]
        return [mm(choices[(y + 2 + k) // 16], halves[k]) for k in range(2)]

    def two_rows(y):
        for k, (z1, z2) in enumerate(zip(product(a1_edges, x_ref, y), product(a2_edges, c_ref, y))):
            value, slope = gelu_parts(summed(z1))
            h_ref[y + 1 + k] = value.astype(BF)
            d_ref[y + 1 + k] = (slope * summed(z2)).astype(BF)

    todo = list(range(1, rows - 1, 2))
    for y in todo[:4]:
        two_rows(y)
    fetch.wait()
    parts = pole_ring(
        rows, all_ref, a1, a2, a3_ref, pole_ref, patch_ref, rim_ref,
        picked, stack, around, slopes, tiles, hring, dring, table,
    )
    for y in todo[4:]:
        next(parts, None)
        two_rows(y)
    for _ in parts:
        pass


def pole_ring(
    rows, all_ref, a1, a2, a3_ref, pole_ref, patch_ref, rim_ref,
    picked, stack, around, slopes, tiles, hring, dring, table,
):
    n, _, chans, cols = all_ref.shape
    lat = lax.axis_index("lat")
    me = lax.axis_index("lon")
    at_top = lat == 0
    at_pole = at_top | (lat == lax.axis_size("lat") - 1)
    block = (chans, cols)
    lane = lax.broadcasted_iota(jnp.int32, block, 1)
    west = lax.rem(me + n - 1, n)
    east = lax.rem(me + 1, n)
    first = jnp.where(at_top, 0, 2)
    last = 2 - first
    place = jnp.where(at_top, 1, rows + 2)
    inner = jnp.where(at_top, 2, rows + 1)
    flip = jnp.where(
        lax.broadcasted_iota(jnp.int32, (cols, cols), 0)
        + lax.broadcasted_iota(jnp.int32, (cols, cols), 1)
        == cols - 1,
        1.0,
        0.0,
    ).astype(BF)
    spans = [slice(128 * b, 128 * b + 128) for b in range(n)]
    partner = [table[jnp.where(at_top, 0, 2), b] for b in range(n)]
    code = [table[jnp.where(at_top, 1, 3), b] for b in range(n)]

    def partner_of(b):
        return table[jnp.where(at_top, 0, 2), b]

    def code_of(b):
        return table[jnp.where(at_top, 1, 3), b]

    def halves(wide):
        high = wide.astype(BF)
        return high, (wide - high.astype(F32)).astype(BF)

    for b in range(n):
        picked[b * chans : (b + 1) * chans] = all_ref[partner[b], 0]
    turned = mm(picked[...], flip)
    for b in range(n):
        here = slice(b * chans, (b + 1) * chans)
        across = jnp.where(code[b] == 1, turned[here], picked[here].astype(F32))
        tiles[b] = across
        stack[first, :, spans[b]] = across.astype(BF)
        stack[1, :, spans[b]] = all_ref[b, 0]
        stack[last, :, spans[b]] = all_ref[b, 1]
    yield

    def ends(held, at, west_tile, east_tile):
        held = jnp.where(lane == at, rot(west_tile, at + 1), held)
        return jnp.where(lane == 64 + at, rot(east_tile, 64 + at), held)

    none = jnp.zeros(block, F32)
    pole_ref[3] = tiles[me].astype(BF)
    patch_ref[2] = ends(none, place, tiles[west], tiles[east])
    u = ring_sum(mm(a1, stack[...].reshape(3 * chans, n * cols)), chans)
    value, slope = gelu_parts(u)
    slopes[...] = slope
    for b in range(n):
        hring[b] = value[:, spans[b]].astype(BF)
    yield

    wide = a2.astype(F32)
    empty = jnp.zeros((3 * chans, chans), F32)
    over = jnp.where(
        at_top,
        jnp.concatenate([wide[:, 2 * chans :], empty], axis=1),
        jnp.concatenate([empty, wide[:, :chans]], axis=1),
    )
    rest = jnp.where(at_top, wide[:, chans:], wide[:, : 2 * chans])
    near = jnp.where(at_top, 0, 1)
    for b in range(n):
        around[near, :, spans[b]] = all_ref[b, 2]
        around[1 - near, :, spans[b]] = all_ref[b, 3]
    both = around[...].reshape(2 * chans, n * cols)
    rim = ring_sum(mm(over.astype(BF), both), chans)
    yield
    tall = jnp.concatenate([rim[:, span] for span in spans], axis=0)
    high, low = halves(tall)
    turned = mm(high, flip) + mm(low, flip)
    for b in range(n):
        here = slice(b * chans, (b + 1) * chans)
        tiles[partner[b]] = jnp.where(code[b] == 1, turned[here], tall[here])
    yield
    back = ring_sum(mm(rest.astype(BF), both), chans)
    for b in range(n):
        dring[b] = (slopes[:, spans[b]] * (back[:, spans[b]] + tiles[b])).astype(BF)
    yield

    origin = 0
    for b in range(n):
        origin = origin + jnp.where(partner[b] == me, b, 0)
    three = jnp.concatenate(
        [dring[lax.rem(origin + n - 1, n)], dring[origin], dring[lax.rem(origin + 1, n)]], axis=1
    )
    wide = a3_ref[...].astype(F32)
    over = jnp.where(at_top, wide[:, 2 * chans :], wide[:, :chans])
    rim = ring_sum(mm(over.astype(BF), three), chans)[:, cols : 2 * cols]
    high, low = halves(rim)
    rim = jnp.where(code_of(origin) == 1, mm(high, flip) + mm(low, flip), rim)
    rim_ref[...] = jnp.where(at_pole, rim, none)
    yield

    pole_ref[0] = hring[me]
    pole_ref[1] = dring[me]
    whose = (me, west, east)
    found = jnp.concatenate([hring[partner_of(b)] for b in whose], axis=0)
    turned = mm(found, flip)
    own, beyond_west, beyond_east = (
        jnp.where(
            code_of(b) == 1,
            turned[k * chans : (k + 1) * chans],
            found[k * chans : (k + 1) * chans].astype(F32),
        )
        for k, b in enumerate(whose)
    )
    pole_ref[2] = own.astype(BF)
    held = ends(none, place, beyond_west, beyond_east)
    patch_ref[0] = ends(held, inner, hring[west].astype(F32), hring[east].astype(F32))
    patch_ref[1] = ends(none, inner, dring[west].astype(F32), dring[east].astype(F32))
    mine = dring[me].astype(F32)
    patch_ref[3] = jnp.where(lane < 64, rot(mine, inner), rot(mine, 65 + inner))


def rows_at_once(z1, z2, xw, xeast, cw, ceast, chans, place, h_ref, d_ref, at):
    for k in range(2):
        span = slice(128 * k, 128 * k + 128)
        u = joined(z1[:, span], chans, place + k, xw, xeast)
        back = joined(z2[:, span], chans, place + k, cw, ceast)
        value, slope = gelu_parts(u)
        h_ref[at + k] = value.astype(BF)
        d_ref[at + k] = (slope * back).astype(BF)


def finish_kernel(
    hin_ref, din_ref, pole_ref, patch_ref, x_ref, c_ref, sx_ref, sc_ref, fn_ref, fs_ref, a1_ref, a2_ref,
    h_ref, d_ref, hs_ref, ds_ref, g_ref,
    xe, ce, sxe, sce, dcol, xrim, acc1, acc2,
):
    rows, chans, cols = x_ref.shape
    lat = lax.axis_index("lat")
    at_top = lat == 0
    at_bottom = lat == lax.axis_size("lat") - 1
    block = (chans, cols)
    lane = lax.broadcasted_iota(jnp.int32, block, 1)
    row_lane = lane % 64
    h_ref[2:rows] = hin_ref[2:rows]
    d_ref[2:rows] = din_ref[2:rows]

    xe[2 : rows + 2] = x_ref[...]
    ce[2 : rows + 2] = c_ref[...]
    xe[0:2] = fn_ref[0:2]
    ce[0:2] = fn_ref[2:4]
    xe[rows + 2 : rows + 4] = fs_ref[0:2]
    ce[rows + 2 : rows + 4] = fs_ref[2:4]
    corner_n = fn_ref[4].astype(F32)
    corner_s = fs_ref[4].astype(F32)
    for at, (src, dst) in enumerate(((sx_ref, sxe), (sc_ref, sce))):
        for b in range(4):
            m = 4 * at + b
            piece = src[:, 128 * b : 128 * b + 128].astype(F32)
            piece = jnp.where(row_lane < 2, rot(corner_n, (-2 * m) % 128), piece)
            piece = jnp.where(
                (row_lane >= rows + 2) & (row_lane < rows + 4),
                rot(corner_s, (rows + 2 - 2 * m) % 128),
                piece,
            )
            dst[:, 128 * b : 128 * b + 128] = piece.astype(BF)

    a1 = a1_ref[...]
    a2 = a2_ref[...]
    zx = mm(a1, row_stack(sxe[...]))
    zc = mm(a2, row_stack(sce[...]))

    def both_ends(z):
        return [
            z[:chans, at : at + 128] + z[chans : 2 * chans, at + 128 : at + 256] + z[2 * chans :, at + 256 : at + 384]
            for at in (0, 128)
        ]

    west_side = lane < 64
    found = [(value, slope * back) for (value, slope), back in zip(map(gelu_parts, both_ends(zx)), both_ends(zc))]
    hs_ref[...] = jnp.where(west_side, found[0][0], found[1][0]).astype(BF)
    ds_ref[...] = jnp.where(west_side, found[0][1], found[1][1]).astype(BF)
    dcol[...] = jnp.where(west_side, found[1][1], found[0][1])
    xrim[...] = jnp.where(west_side, sxe[:, 128:256].astype(F32), sxe[:, 256:384].astype(F32))
    xw, xeast = zx[:chans, 128:256], zx[2 * chans :, 256:384]
    cw, ceast = zc[:chans, 128:256], zc[2 * chans :, 256:384]
    for t in (0, rows):
        rows_at_once(
            mm(a1, pair_of_rows(xe, t)), mm(a2, pair_of_rows(ce, t)),
            xw, xeast, cw, ceast, chans, t + 1, h_ref, d_ref, t,
        )

    @pl.when(at_top | at_bottom)
    def _():
        place = jnp.where(at_top, 1, rows + 2)
        inner = jnp.where(at_top, 2, rows + 1)
        outer_row = jnp.where(at_top, 0, rows + 1)
        inner_row = jnp.where(at_top, 1, rows)
        h_ref[inner_row] = pole_ref[0]
        d_ref[inner_row] = pole_ref[1]
        h_ref[outer_row] = pole_ref[2]
        d_ref[outer_row] = jnp.zeros(block, BF)
        xe[jnp.where(at_top, 1, rows + 2)] = pole_ref[3]
        at_place = row_lane == place
        at_pole = at_place | (row_lane == inner)
        hs_ref[...] = jnp.where(at_pole, patch_ref[0], hs_ref[...].astype(F32)).astype(BF)
        ds_ref[...] = jnp.where(at_pole, patch_ref[1], ds_ref[...].astype(F32)).astype(BF)
        xrim[...] = jnp.where(at_place, patch_ref[2], xrim[...])
        dcol[...] = jnp.where(row_lane == inner, patch_ref[3], dcol[...])

    own = (row_lane >= 2) & (row_lane < rows + 2)
    none = jnp.zeros(block, F32)

    def rim_terms(west_part, east_part):
        return jnp.concatenate(
            [
                jnp.where(own & (lane < 64), west_part, none),
                none,
                jnp.where(own & (lane >= 64), east_part, none),
            ],
            axis=0,
        ).astype(BF)

    west_cot = sce[:, 256:384].astype(F32)
    east_cot = sce[:, 128:256].astype(F32)
    acc2[...] = mm_t(rim_terms(west_cot, east_cot), row_stack(hs_ref[...]))
    acc1[...] = mm_t(rim_terms(dcol[...], dcol[...]), row_stack(xrim[...].astype(BF)))
    zero = jnp.zeros(block, BF)

    def shifted_rows(ref, at):
        parts = []
        for k in range(2):
            tile = ref[at + k]
            ahead = jnp.where(lane == cols - 1, zero, rot(tile, cols - 1))
            behind = jnp.where(lane == 0, zero, rot(tile, 1))
            parts.append(jnp.concatenate([ahead, tile, behind], axis=0))
        return jnp.concatenate(parts, axis=1)

    def add_rows(step, _):
        y = 2 * step
        acc2[...] += mm_t(shifted_rows(ce, y + 2), pair_of_rows(h_ref, y))
        acc1[...] += mm_t(shifted_rows(d_ref, y + 1), pair_of_rows(xe, y + 1))
        return 0

    lax.fori_loop(0, rows // 2, add_rows, 0, unroll=True)
    g2 = acc2[...]
    g1 = acc1[...]
    g_ref[0] = g2[:, :128]
    g_ref[1] = g1[:, :128]
    g_ref[2] = jnp.concatenate([g2[:, 128:], g1[:, 128:]], axis=1)


def out_kernel(h_ref, hs_ref, b2_ref, out_ref):
    rows, chans, _ = out_ref.shape
    b2 = b2_ref[...]
    zh = mm(b2, row_stack(hs_ref[...]))

    def two_rows(step, _):
        t = 2 * step
        z = mm(b2, pair_of_rows(h_ref, t))
        for k in range(2):
            row = joined(z[:, 128 * k : 128 * k + 128], chans, t + k + 2, zh[:chans], zh[2 * chans :])
            out_ref[t + k] = row.astype(BF)
        return 0

    lax.fori_loop(0, rows // 2, two_rows, 0, unroll=True)


def fields_kernel(d_ref, ds_ref, rim_ref, b1_ref, out_ref):
    rows, chans, _ = out_ref.shape
    lat = lax.axis_index("lat")
    b1 = b1_ref[...]
    zd = mm(b1, row_stack(ds_ref[...]))

    def two_rows(step, _):
        t = 2 * step
        z = mm(b1, pair_of_rows(d_ref, t))
        for k in range(2):
            row = joined(z[:, 128 * k : 128 * k + 128], chans, t + k + 2, zd[:chans], zd[2 * chans :])
            rim_here = ((t + k == 0) & (lat == 0)) | (
                (t + k == rows - 1) & (lat == lax.axis_size("lat") - 1)
            )
            out_ref[t + k] = (row + jnp.where(rim_here, 1.0, 0.0) * rim_ref[...]).astype(BF)
        return 0

    lax.fori_loop(0, rows // 2, two_rows, 0, unroll=True)


def unpack_kernel(half_ref, other_ref, one_ref, two_ref, whole, *, scale):
    chans = one_ref.shape[2]
    lower = lax.rem(lax.axis_index("lon"), 2) == 0
    count = half_ref.shape[0]
    half = half_ref[...] * scale
    other = other_ref[...] * scale
    whole[:count] = jnp.where(lower, half, other)
    whole[count:] = jnp.where(lower, other, half)
    for at, ref in enumerate((two_ref, one_ref)):
        for s in range(3):
            wide = whole[(3 * at + s) * chans : (3 * at + s + 1) * chans]
            ref[0, s] = wide[:, :chans]
            ref[1, s] = wide[:, chans:]
            ref[2, s] = whole[(6 + s) * chans : (7 + s) * chans][:, chans * at : chans * at + chans]


def call(kernel, outs, args, scratch=(), flops=0):
    space = [pl.BlockSpec(memory_space=pltpu.VMEM)] * len(args)
    moved = sum(math.prod(a.shape) * a.dtype.itemsize for a in list(args) + list(outs))
    return pl.pallas_call(
        kernel,
        out_shape=tuple(outs),
        in_specs=space,
        out_specs=tuple(pl.BlockSpec(memory_space=pltpu.VMEM) for _ in outs),
        scratch_shapes=list(scratch),
        compiler_params=pltpu.CompilerParams(vmem_limit_bytes=VMEM_LIMIT),
        cost_estimate=pl.CostEstimate(flops=flops, bytes_accessed=moved, transcendentals=0),
    )(*args)


def native(rows_first):
    return with_layout_constraint(rows_first.transpose(1, 0, 2), Layout((0, 1, 2)))


def on_device(
    fields_in, weight_one, weight_two, cotangent, north_map, north_code, south_map, south_code
):
    chans, rows, cols = fields_in.shape
    n = lax.axis_size("lon")
    lat_count = lax.axis_size("lat")
    pixel_total = rows * cols * n * lat_count
    shape = jax.ShapeDtypeStruct
    x = fields_in.transpose(1, 0, 2)
    c = cotangent.transpose(1, 0, 2)
    square = shape((3 * chans, 3 * chans), BF)
    (packed,) = call(pack_kernel, [shape((6, chans, cols), BF)], [x, c])
    gathered = lax.all_gather(packed, "lon", axis=0)
    strip = shape((chans, 4 * cols), BF)
    five = shape((5, chans, cols), BF)
    table, sx, sc, to_south, to_north, forward_one, back_one, forward_two, back_two = call(
        strip_kernel,
        [shape((4, n), jnp.int32), strip, strip, five, five] + [square] * 4,
        [north_map, north_code, south_map, south_code, x, c, gathered, weight_one, weight_two],
    )
    southward = [(i, (i + 1) % lat_count) for i in range(lat_count)]
    northward = [(target, source) for source, target in southward]
    from_north = lax.ppermute(to_south, "lat", southward)
    from_south = lax.ppermute(to_north, "lat", northward)

    conv_flops = 2 * 9 * chans * chans * rows * cols
    taller = shape((rows + 2, chans, cols), BF)
    edges = shape((chans, cols), BF)
    patches = shape((4, chans, cols), F32)
    h, d, pole, patch, rim = call(
        interior_kernel,
        [taller, taller, shape((4, chans, cols), BF), patches, shape((chans, cols), F32)],
        [table, x, c, gathered, sx, sc]
        + [forward_one, back_two, back_one],
        [
            pltpu.VMEM((16, chans, cols), BF),
            pltpu.VMEM((n * chans, cols), BF),
            pltpu.VMEM((3, chans, n * cols), BF),
            pltpu.VMEM((2, chans, n * cols), BF),
            pltpu.VMEM((chans, n * cols), F32),
            pltpu.VMEM((n, chans, cols), F32),
            pltpu.VMEM((n, chans, cols), BF),
            pltpu.VMEM((n, chans, cols), BF),
        ]
        + [pltpu.SMEM((4, n), jnp.int32), pltpu.SemaphoreType.DMA],
        flops=2 * conv_flops,
    )
    h, d, hs, ds, grads = call(
        finish_kernel,
        [taller, taller, edges, edges, shape((3, 3 * chans, cols), F32)],
        [h, d, pole, patch, x, c, sx, sc, from_north, from_south, forward_one, back_two],
        [
            pltpu.VMEM((rows + 4, chans, cols), BF),
            pltpu.VMEM((rows + 4, chans, cols), BF),
            pltpu.VMEM((chans, 4 * cols), BF),
            pltpu.VMEM((chans, 4 * cols), BF),
            pltpu.VMEM((chans, cols), F32),
            pltpu.VMEM((chans, cols), F32),
            pltpu.VMEM((3 * chans, 3 * chans), F32),
            pltpu.VMEM((3 * chans, 3 * chans), F32),
        ],
        flops=2 * conv_flops,
    )

    flat = grads.reshape(2, -1, cols)
    mine = lax.axis_index("lon") % 2
    swap = [(i, i ^ 1) for i in range(n)]
    kept = lax.dynamic_index_in_dim(flat, mine, 0, keepdims=False)
    given = lax.dynamic_index_in_dim(flat, 1 - mine, 0, keepdims=False)
    half = kept + lax.ppermute(given, "lon", swap)
    device_count = n * lat_count
    bits = [1 << k for k in range(device_count.bit_length() - 1) if 1 << k != lat_count]
    groups = [bits[k : k + 2] for k in range(0, len(bits) - 1, 2)]
    middle = len(groups) // 2
    left = [bits[-1:]] if len(bits) % 2 else []
    orders = groups[middle:] + groups[:middle] + left, groups + left
    stages = len(orders[0])
    low = shape((rows, chans, cols), BF)
    for k in range(stages):
        sent = half.astype(BF)
        if k == 0:
            sent, h = lax.optimization_barrier((sent, h))
        if k == 1:
            sent, d = lax.optimization_barrier((sent, d))
        got = [sent]
        for step in range(1, 1 << len(orders[0][k])):
            jumps = [sum(bit for at, bit in enumerate(order[k]) if step >> at & 1) for order in orders]
            pairs = [(i, i ^ jumps[i // lat_count % 2]) for i in range(device_count)]
            got.append(lax.ppermute(sent, ("lon", "lat"), pairs))
        got = [part.astype(F32) for part in got]
        half = (got[0] + got[1]) + (got[2] + got[3]) if len(got) == 4 else got[0] + got[1]
        if k == 0:
            (out,) = call(out_kernel, [low], [h, hs, forward_two], flops=conv_flops)
            out = native(out)
            half, out = lax.optimization_barrier((half, out))
        if k == 1:
            (d_fields,) = call(fields_kernel, [low], [d, ds, rim, back_one], flops=conv_flops)
            d_fields = native(d_fields)
            half, d_fields = lax.optimization_barrier((half, d_fields))
    other = lax.ppermute(half, "lon", swap)
    kernel_shape = shape(weight_one.shape, F32)
    one, two = call(
        functools.partial(unpack_kernel, scale=1.0 / math.sqrt(pixel_total)),
        [kernel_shape, kernel_shape],
        [half, other],
        [pltpu.VMEM((9 * chans, cols), F32)],
    )
    return (out, d_fields, one, two)


def solution(mesh):
    placed = (P(None, "lat", "lon"), P(), P(), P(None, "lat", "lon"), P(), P(), P(), P())
    return jax.shard_map(
        on_device,
        mesh=mesh,
        in_specs=placed,
        out_specs=(P(None, "lat", "lon"), P(None, "lat", "lon"), P(), P()),
        check_vma=False,
    )
```

```python
import functools
import math

import jax
import jax.numpy as jnp
import ml_dtypes
import numpy as np
from jax import lax
from jax.experimental import pallas as pl
from jax.experimental.pallas import tpu as pltpu
from jax.experimental.layout import Layout, with_layout_constraint
from jax.sharding import PartitionSpec as P

BF = jnp.bfloat16
F32 = jnp.float32
GELU_K = math.sqrt(2.0 / math.pi)
VMEM_LIMIT = 48 * 1024 * 1024


def mm(a, b):
    return jnp.dot(a, b, preferred_element_type=F32)


def mm_t(a, b):
    return lax.dot_general(a, b, (((1,), (1,)), ((), ())), preferred_element_type=F32)


def lane_of(like):
    return lax.broadcasted_iota(jnp.int32, like.shape, like.ndim - 1)


def rot(x, by):
    return pltpu.roll(x, by, x.ndim - 1)


def gelu_parts(u):
    square = u * u
    t = jnp.tanh(GELU_K * u * (1.0 + 0.044715 * square))
    half = 0.5 + 0.5 * t
    slope = half + (0.5 * GELU_K) * u * (1.0 - t * t) * (1.0 + (3 * 0.044715) * square)
    return u * half, slope


def arrange(w_ref, forward_ref, back_ref):
    chans = w_ref.shape[2]
    diagonal = lax.broadcasted_iota(jnp.int32, (chans, chans), 0) == lax.broadcasted_iota(
        jnp.int32, (chans, chans), 1
    )
    eye = jnp.where(diagonal, 1.0, 0.0).astype(BF)
    for s in range(3):
        here = slice(s * chans, (s + 1) * chans)
        forward_ref[here] = jnp.concatenate([w_ref[r, s] for r in range(3)], axis=1)
        flipped = jnp.concatenate([w_ref[2 - r, 2 - s] for r in range(3)], axis=0)
        back_ref[here] = mm_t(eye, flipped).astype(BF)


def pack_kernel(x_ref, c_ref, out_ref):
    rows = x_ref.shape[0]
    bottom = jnp.where(lax.axis_index("lat") == 0, 0, 1)
    edge = bottom * (rows - 1)
    beside = 1 + bottom * (rows - 3)
    out_ref[0] = x_ref[edge]
    out_ref[1] = x_ref[beside]
    out_ref[2] = c_ref[edge]
    out_ref[3] = c_ref[beside]
    for at, ref in ((4, x_ref), (5, c_ref)):
        packed = jnp.zeros(ref.shape[1:], F32)
        lane = lane_of(packed)
        for i in range(rows):
            turned = rot(ref[i].astype(F32), (4 * i + 2) % 128)
            packed = jnp.where((lane >= 4 * i) & (lane < 4 * i + 4), turned, packed)
        out_ref[at] = packed.astype(BF)


def strip_chooser(rows, cols):
    target = np.arange(4 * cols)[None]
    source = np.arange(3 * cols)[:, None]
    block, side, row = target // 128, target % 128 // 64, target % 64 - 2
    wanted = 128 * (side + block // 2) + 4 * row + block
    return ((source == wanted) & (row >= 0) & (row < rows)).astype(ml_dtypes.bfloat16)


def end_choosers(chans, cols):
    m = np.arange(16)[:, None, None]
    spot = np.arange(chans)[None, :, None]
    lane = np.arange(cols)[None, None]
    return ((lane == np.where(spot < 32, 0, cols - 1)) & (spot % 16 == m)).astype(ml_dtypes.bfloat16)


def strip_kernel(
    chooser_ref, x_ref, c_ref, all_ref, w1_ref, w2_ref,
    sx_ref, sc_ref, south_ref, north_ref, f1_ref, b1_ref, f2_ref, b2_ref,
):
    arrange(w1_ref, f1_ref, b1_ref)
    arrange(w2_ref, f2_ref, b2_ref)
    rows, chans, cols = x_ref.shape
    n = all_ref.shape[0]
    me = lax.axis_index("lon")
    west = lax.rem(me + n - 1, n)
    east = lax.rem(me + 1, n)
    to_south = jnp.zeros((chans, cols), F32)
    to_north = jnp.zeros((chans, cols), F32)
    lane = lane_of(to_south)
    pair = (lane % 64) // 2
    for at, ref in ((0, sx_ref), (1, sc_ref)):
        taken = jnp.concatenate([all_ref[west, 4 + at], all_ref[me, 4 + at], all_ref[east, 4 + at]], axis=1)
        strip = mm(taken, chooser_ref[...])
        ref[...] = strip.astype(BF)
        for b in range(4):
            m = 4 * at + b
            piece = strip[:, 128 * b : 128 * b + 128]
            to_south = jnp.where(pair == m, rot(piece, (2 * m - rows) % 128), to_south)
            to_north = jnp.where(pair == m, rot(piece, (2 * m - 2) % 128), to_north)
    for ref, start, corner in ((south_ref, rows - 2, to_south), (north_ref, 0, to_north)):
        for k in range(2):
            ref[k] = x_ref[start + k]
            ref[2 + k] = c_ref[start + k]
        ref[4] = corner.astype(BF)


def shifted_rows(ref, at):
    both = ref[pl.ds(at, 2)]
    lane = lane_of(both[0])
    zero = jnp.zeros_like(both[0])
    parts = []
    for k in range(2):
        ahead = jnp.where(lane == lane.shape[1] - 1, zero, rot(both[k], lane.shape[1] - 1))
        behind = jnp.where(lane == 0, zero, rot(both[k], 1))
        parts.append(jnp.concatenate([ahead, both[k], behind], axis=0))
    return jnp.concatenate(parts, axis=1)


def row_stack(strip):
    wide = strip.astype(F32)
    parts = [wide[:, at : at + 128] for at in range(0, wide.shape[1], 128)]
    above = jnp.concatenate([rot(p, 1) for p in parts], axis=1).astype(BF)
    below = jnp.concatenate([rot(p, 127) for p in parts], axis=1).astype(BF)
    return jnp.concatenate([above, strip, below], axis=0)


def joined(z, chans, place, edge_w, edge_e):
    lane = lane_of(edge_w)
    low = jnp.where(lane == 0, rot(edge_w, 128 - place), rot(z[:chans], 1))
    high = jnp.where(lane == 127, rot(edge_e, 63 - place), rot(z[2 * chans :], 127))
    return low + z[chans : 2 * chans] + high


def pair_of_rows(ref, at):
    four = ref[pl.ds(at, 4)]
    _, chans, cols = four.shape
    return jnp.concatenate(
        [four[:3].reshape(3 * chans, cols), four[1:].reshape(3 * chans, cols)], axis=1
    )


def ring_sum(z, chans):
    return rot(z[:chans], 1) + z[chans : 2 * chans] + rot(z[2 * chans :], z.shape[1] - 1)


def with_edges(a, west, east, group):
    chans = west.shape[0]
    parts = []
    for edge, start in ((west, 16 * group), (east, 64 + 16 * group)):
        term = edge[:, start : start + 16]
        high = term.astype(BF).astype(F32)
        parts += [high, term - high]
    middle = jnp.concatenate(parts, axis=1)
    none = jnp.zeros_like(middle)
    return jnp.concatenate([a, jnp.concatenate([none, middle, none], axis=0).astype(BF)], axis=1)


def interior_kernel(
    nmap_hbm, ncode_hbm, smap_hbm, scode_hbm, hot, x_ref, c_ref, all_ref, sx_ref, sc_ref, a1_ref, a2_ref, a3_ref,
    h_ref, d_ref, pole_ref, patch_ref, rim_ref, acc1, acc2,
    picked, stack, around, slopes, tiles, hring, dring, nmap, ncode, smap, scode, sems,
):
    tables = [
        pltpu.make_async_copy(src, dst, sems.at[k])
        for k, (src, dst) in enumerate(
            ((nmap_hbm, nmap), (ncode_hbm, ncode), (smap_hbm, smap), (scode_hbm, scode))
        )
    ]
    for table in tables:
        table.start()
    rows, chans, cols = x_ref.shape
    a1 = a1_ref[...]
    a2 = a2_ref[...]
    zx = mm(a1, row_stack(sx_ref[:, 128:384]))
    zc = mm(a2, row_stack(sc_ref[:, 128:384]))
    groups = range((rows + 2) // 16 + 1)
    a1_edges = [with_edges(a1, zx[:chans, :128], zx[2 * chans :, 128:], g) for g in groups]
    a2_edges = [with_edges(a2, zc[:chans, :128], zc[2 * chans :, 128:], g) for g in groups]
    lane = lax.broadcasted_iota(jnp.int32, (chans, cols), 1)
    def summed(z):
        low = jnp.where(lane == 0, 0.0, rot(z[:chans], 1))
        high = jnp.where(lane == cols - 1, 0.0, rot(z[2 * chans :], 127))
        return low + z[chans : 2 * chans] + high

    def product(choices, ref, y):
        four = ref[y - 1 : y + 3]
        halves = [
            jnp.concatenate([four[k : k + 3].reshape(3 * chans, cols), hot[(y + 2 + k) % 16]], axis=0)
            for k in range(2)
        ]
        if (y + 2) // 16 == (y + 3) // 16:
            z = mm(choices[(y + 2) // 16], jnp.concatenate(halves, axis=1))
            return z[:, :cols], z[:, cols:]
        return [mm(choices[(y + 2 + k) // 16], halves[k]) for k in range(2)]

    def two_rows(y):
        for k, (z1, z2) in enumerate(zip(product(a1_edges, x_ref, y), product(a2_edges, c_ref, y))):
            value, slope = gelu_parts(summed(z1))
            h_ref[y + 1 + k] = value.astype(BF)
            d_ref[y + 1 + k] = (slope * summed(z2)).astype(BF)

    def gradients(y):
        two = mm_t(shifted_rows(c_ref, y), pair_of_rows(h_ref, y))
        one = mm_t(shifted_rows(d_ref, y + 1), pair_of_rows(x_ref, y - 1))
        acc2[...] = two if y == 2 else acc2[...] + two
        acc1[...] = one if y == 2 else acc1[...] + one

    todo = list(range(1, rows - 1, 2))
    for y in todo[:4]:
        two_rows(y)
    for table in tables:
        table.wait()
    parts = pole_ring(
        rows, all_ref, a1, a2, a3_ref, pole_ref, patch_ref, rim_ref,
        picked, stack, around, slopes, tiles, hring, dring, nmap, ncode, smap, scode,
    )
    for y in todo[4:]:
        next(parts, None)
        two_rows(y)
    for _ in parts:
        pass
    for y in range(2, rows - 2, 2):
        gradients(y)


def pole_ring(
    rows, all_ref, a1, a2, a3_ref, pole_ref, patch_ref, rim_ref,
    picked, stack, around, slopes, tiles, hring, dring, nmap, ncode, smap, scode,
):
    n, _, chans, cols = all_ref.shape
    lat = lax.axis_index("lat")
    me = lax.axis_index("lon")
    at_top = lat == 0
    at_pole = at_top | (lat == lax.axis_size("lat") - 1)
    block = (chans, cols)
    lane = lax.broadcasted_iota(jnp.int32, block, 1)
    west = lax.rem(me + n - 1, n)
    east = lax.rem(me + 1, n)
    first = jnp.where(at_top, 0, 2)
    last = 2 - first
    place = jnp.where(at_top, 1, rows + 2)
    inner = jnp.where(at_top, 2, rows + 1)
    flip = jnp.where(
        lax.broadcasted_iota(jnp.int32, (cols, cols), 0)
        + lax.broadcasted_iota(jnp.int32, (cols, cols), 1)
        == cols - 1,
        1.0,
        0.0,
    ).astype(BF)
    spans = [slice(128 * b, 128 * b + 128) for b in range(n)]
    partner = [jnp.where(at_top, nmap[b], smap[b]) for b in range(n)]
    code = [jnp.where(at_top, ncode[b], scode[b]) for b in range(n)]

    def partner_of(b):
        return jnp.where(at_top, nmap[b], smap[b])

    def code_of(b):
        return jnp.where(at_top, ncode[b], scode[b])

    def halves(wide):
        high = wide.astype(BF)
        return high, (wide - high.astype(F32)).astype(BF)

    for b in range(n):
        picked[b * chans : (b + 1) * chans] = all_ref[partner[b], 0]
    turned = mm(picked[...], flip)
    for b in range(n):
        here = slice(b * chans, (b + 1) * chans)
        across = jnp.where(code[b] == 1, turned[here], picked[here].astype(F32))
        tiles[b] = across
        stack[first, :, spans[b]] = across.astype(BF)
        stack[1, :, spans[b]] = all_ref[b, 0]
        stack[last, :, spans[b]] = all_ref[b, 1]
    yield

    def ends(held, at, west_tile, east_tile):
        held = jnp.where(lane == at, rot(west_tile, at + 1), held)
        return jnp.where(lane == 64 + at, rot(east_tile, 64 + at), held)

    none = jnp.zeros(block, F32)
    pole_ref[3] = tiles[me].astype(BF)
    patch_ref[2] = ends(none, place, tiles[west], tiles[east])
    u = ring_sum(mm(a1, stack[...].reshape(3 * chans, n * cols)), chans)
    value, slope = gelu_parts(u)
    slopes[...] = slope
    for b in range(n):
        hring[b] = value[:, spans[b]].astype(BF)
    yield

    wide = a2.astype(F32)
    empty = jnp.zeros((3 * chans, chans), F32)
    over = jnp.where(
        at_top,
        jnp.concatenate([wide[:, 2 * chans :], empty], axis=1),
        jnp.concatenate([empty, wide[:, :chans]], axis=1),
    )
    rest = jnp.where(at_top, wide[:, chans:], wide[:, : 2 * chans])
    near = jnp.where(at_top, 0, 1)
    for b in range(n):
        around[near, :, spans[b]] = all_ref[b, 2]
        around[1 - near, :, spans[b]] = all_ref[b, 3]
    both = around[...].reshape(2 * chans, n * cols)
    rim = ring_sum(mm(over.astype(BF), both), chans)
    yield
    tall = jnp.concatenate([rim[:, span] for span in spans], axis=0)
    high, low = halves(tall)
    turned = mm(high, flip) + mm(low, flip)
    for b in range(n):
        here = slice(b * chans, (b + 1) * chans)
        tiles[partner[b]] = jnp.where(code[b] == 1, turned[here], tall[here])
    yield
    back = ring_sum(mm(rest.astype(BF), both), chans)
    for b in range(n):
        dring[b] = (slopes[:, spans[b]] * (back[:, spans[b]] + tiles[b])).astype(BF)
    yield

    origin = 0
    for b in range(n):
        origin = origin + jnp.where(partner[b] == me, b, 0)
    three = jnp.concatenate(
        [dring[lax.rem(origin + n - 1, n)], dring[origin], dring[lax.rem(origin + 1, n)]], axis=1
    )
    wide = a3_ref[...].astype(F32)
    over = jnp.where(at_top, wide[:, 2 * chans :], wide[:, :chans])
    rim = ring_sum(mm(over.astype(BF), three), chans)[:, cols : 2 * cols]
    high, low = halves(rim)
    rim = jnp.where(code_of(origin) == 1, mm(high, flip) + mm(low, flip), rim)
    rim_ref[...] = jnp.where(at_pole, rim, none)
    yield

    pole_ref[0] = hring[me]
    pole_ref[1] = dring[me]
    whose = (me, west, east)
    found = jnp.concatenate([hring[partner_of(b)] for b in whose], axis=0)
    turned = mm(found, flip)
    own, beyond_west, beyond_east = (
        jnp.where(
            code_of(b) == 1,
            turned[k * chans : (k + 1) * chans],
            found[k * chans : (k + 1) * chans].astype(F32),
        )
        for k, b in enumerate(whose)
    )
    pole_ref[2] = own.astype(BF)
    held = ends(none, place, beyond_west, beyond_east)
    patch_ref[0] = ends(held, inner, hring[west].astype(F32), hring[east].astype(F32))
    patch_ref[1] = ends(none, inner, dring[west].astype(F32), dring[east].astype(F32))
    mine = dring[me].astype(F32)
    patch_ref[3] = jnp.where(lane < 64, rot(mine, inner), rot(mine, 65 + inner))


def rows_at_once(z1, z2, xw, xeast, cw, ceast, chans, place, h_ref, d_ref, at):
    for k in range(2):
        span = slice(128 * k, 128 * k + 128)
        u = joined(z1[:, span], chans, place + k, xw, xeast)
        back = joined(z2[:, span], chans, place + k, cw, ceast)
        value, slope = gelu_parts(u)
        h_ref[at + k] = value.astype(BF)
        d_ref[at + k] = (slope * back).astype(BF)


def finish_kernel(
    hin_ref, din_ref, in1_ref, in2_ref, pole_ref, patch_ref, x_ref, c_ref, sx_ref, sc_ref, fn_ref, fs_ref, a1_ref, a2_ref,
    h_ref, d_ref, hs_ref, ds_ref, g_ref,
    xe, ce, sxe, sce, dcol, xrim, acc1, acc2,
):
    rows, chans, cols = x_ref.shape
    lat = lax.axis_index("lat")
    at_top = lat == 0
    at_bottom = lat == lax.axis_size("lat") - 1
    block = (chans, cols)
    lane = lax.broadcasted_iota(jnp.int32, block, 1)
    row_lane = lane % 64
    h_ref[2:rows] = hin_ref[2:rows]
    d_ref[2:rows] = din_ref[2:rows]

    xe[2 : rows + 2] = x_ref[...]
    ce[2 : rows + 2] = c_ref[...]
    xe[0:2] = fn_ref[0:2]
    ce[0:2] = fn_ref[2:4]
    xe[rows + 2 : rows + 4] = fs_ref[0:2]
    ce[rows + 2 : rows + 4] = fs_ref[2:4]
    corner_n = fn_ref[4].astype(F32)
    corner_s = fs_ref[4].astype(F32)
    for at, (src, dst) in enumerate(((sx_ref, sxe), (sc_ref, sce))):
        for b in range(4):
            m = 4 * at + b
            piece = src[:, 128 * b : 128 * b + 128].astype(F32)
            piece = jnp.where(row_lane < 2, rot(corner_n, (-2 * m) % 128), piece)
            piece = jnp.where(
                (row_lane >= rows + 2) & (row_lane < rows + 4),
                rot(corner_s, (rows + 2 - 2 * m) % 128),
                piece,
            )
            dst[:, 128 * b : 128 * b + 128] = piece.astype(BF)

    a1 = a1_ref[...]
    a2 = a2_ref[...]
    zx = mm(a1, row_stack(sxe[...]))
    zc = mm(a2, row_stack(sce[...]))

    def both_ends(z):
        return [
            z[:chans, at : at + 128] + z[chans : 2 * chans, at + 128 : at + 256] + z[2 * chans :, at + 256 : at + 384]
            for at in (0, 128)
        ]

    west_side = lane < 64
    found = [(value, slope * back) for (value, slope), back in zip(map(gelu_parts, both_ends(zx)), both_ends(zc))]
    hs_ref[...] = jnp.where(west_side, found[0][0], found[1][0]).astype(BF)
    ds_ref[...] = jnp.where(west_side, found[0][1], found[1][1]).astype(BF)
    dcol[...] = jnp.where(west_side, found[1][1], found[0][1])
    xrim[...] = jnp.where(west_side, sxe[:, 128:256].astype(F32), sxe[:, 256:384].astype(F32))
    xw, xeast = zx[:chans, 128:256], zx[2 * chans :, 256:384]
    cw, ceast = zc[:chans, 128:256], zc[2 * chans :, 256:384]
    for t in (0, rows):
        rows_at_once(
            mm(a1, pair_of_rows(xe, t)), mm(a2, pair_of_rows(ce, t)),
            xw, xeast, cw, ceast, chans, t + 1, h_ref, d_ref, t,
        )

    @pl.when(at_top | at_bottom)
    def _():
        place = jnp.where(at_top, 1, rows + 2)
        inner = jnp.where(at_top, 2, rows + 1)
        outer_row = jnp.where(at_top, 0, rows + 1)
        inner_row = jnp.where(at_top, 1, rows)
        h_ref[inner_row] = pole_ref[0]
        d_ref[inner_row] = pole_ref[1]
        h_ref[outer_row] = pole_ref[2]
        d_ref[outer_row] = jnp.zeros(block, BF)
        xe[jnp.where(at_top, 1, rows + 2)] = pole_ref[3]
        at_place = row_lane == place
        at_pole = at_place | (row_lane == inner)
        hs_ref[...] = jnp.where(at_pole, patch_ref[0], hs_ref[...].astype(F32)).astype(BF)
        ds_ref[...] = jnp.where(at_pole, patch_ref[1], ds_ref[...].astype(F32)).astype(BF)
        xrim[...] = jnp.where(at_place, patch_ref[2], xrim[...])
        dcol[...] = jnp.where(row_lane == inner, patch_ref[3], dcol[...])

    own = (row_lane >= 2) & (row_lane < rows + 2)
    none = jnp.zeros(block, F32)

    def rim_terms(west_part, east_part):
        return jnp.concatenate(
            [
                jnp.where(own & (lane < 64), west_part, none),
                none,
                jnp.where(own & (lane >= 64), east_part, none),
            ],
            axis=0,
        ).astype(BF)

    west_cot = sce[:, 256:384].astype(F32)
    east_cot = sce[:, 128:256].astype(F32)
    acc2[...] = in2_ref[...] + mm_t(rim_terms(west_cot, east_cot), row_stack(hs_ref[...]))
    acc1[...] = in1_ref[...] + mm_t(rim_terms(dcol[...], dcol[...]), row_stack(xrim[...].astype(BF)))
    for y in (0, rows - 2):
        acc2[...] += mm_t(shifted_rows(ce, y + 2), pair_of_rows(h_ref, y))
        acc1[...] += mm_t(shifted_rows(d_ref, y + 1), pair_of_rows(xe, y + 1))
    g2 = acc2[...]
    g1 = acc1[...]
    g_ref[0] = g2[:, :128]
    g_ref[1] = g1[:, :128]
    g_ref[2] = jnp.concatenate([g2[:, 128:], g1[:, 128:]], axis=1)


def out_kernel(h_ref, hs_ref, b2_ref, out_ref):
    rows, chans, _ = out_ref.shape
    b2 = b2_ref[...]
    zh = mm(b2, row_stack(hs_ref[...]))

    def two_rows(step, _):
        t = 2 * step
        z = mm(b2, pair_of_rows(h_ref, t))
        for k in range(2):
            row = joined(z[:, 128 * k : 128 * k + 128], chans, t + k + 2, zh[:chans], zh[2 * chans :])
            out_ref[t + k] = row.astype(BF)
        return 0

    lax.fori_loop(0, rows // 2, two_rows, 0, unroll=True)


def fields_kernel(d_ref, ds_ref, rim_ref, b1_ref, out_ref):
    rows, chans, _ = out_ref.shape
    lat = lax.axis_index("lat")
    b1 = b1_ref[...]
    zd = mm(b1, row_stack(ds_ref[...]))

    def two_rows(step, _):
        t = 2 * step
        z = mm(b1, pair_of_rows(d_ref, t))
        for k in range(2):
            row = joined(z[:, 128 * k : 128 * k + 128], chans, t + k + 2, zd[:chans], zd[2 * chans :])
            rim_here = ((t + k == 0) & (lat == 0)) | (
                (t + k == rows - 1) & (lat == lax.axis_size("lat") - 1)
            )
            out_ref[t + k] = (row + jnp.where(rim_here, 1.0, 0.0) * rim_ref[...]).astype(BF)
        return 0

    lax.fori_loop(0, rows // 2, two_rows, 0, unroll=True)


def unpack_kernel(half_ref, other_ref, one_ref, two_ref, whole, *, scale):
    chans = one_ref.shape[2]
    lower = lax.rem(lax.axis_index("lon"), 2) == 0
    count = half_ref.shape[0]
    half = half_ref[...] * scale
    other = other_ref[...] * scale
    whole[:count] = jnp.where(lower, half, other)
    whole[count:] = jnp.where(lower, other, half)
    for at, ref in enumerate((two_ref, one_ref)):
        for s in range(3):
            wide = whole[(3 * at + s) * chans : (3 * at + s + 1) * chans]
            ref[0, s] = wide[:, :chans]
            ref[1, s] = wide[:, chans:]
            ref[2, s] = whole[(6 + s) * chans : (7 + s) * chans][:, chans * at : chans * at + chans]


def call(kernel, outs, args, scratch=(), flops=0, pinned=0):
    args = [pltpu.with_memory_space_constraint(a, pltpu.HBM) for a in args[:pinned]] + args[pinned:]
    space = [pl.BlockSpec(memory_space=pltpu.HBM)] * pinned
    space += [pl.BlockSpec(memory_space=pltpu.VMEM)] * (len(args) - pinned)
    moved = sum(math.prod(a.shape) * a.dtype.itemsize for a in list(args) + list(outs))
    return pl.pallas_call(
        kernel,
        out_shape=tuple(outs),
        in_specs=space,
        out_specs=tuple(pl.BlockSpec(memory_space=pltpu.VMEM) for _ in outs),
        scratch_shapes=list(scratch),
        compiler_params=pltpu.CompilerParams(vmem_limit_bytes=VMEM_LIMIT),
        cost_estimate=pl.CostEstimate(flops=flops, bytes_accessed=moved, transcendentals=0),
    )(*args)


def native(rows_first):
    return with_layout_constraint(rows_first.transpose(1, 0, 2), Layout((0, 1, 2)))


def on_device(
    fields_in, weight_one, weight_two, cotangent, north_map, north_code, south_map, south_code
):
    chans, rows, cols = fields_in.shape
    n = lax.axis_size("lon")
    lat_count = lax.axis_size("lat")
    pixel_total = rows * cols * n * lat_count
    shape = jax.ShapeDtypeStruct
    x = fields_in.transpose(1, 0, 2)
    c = cotangent.transpose(1, 0, 2)
    square = shape((3 * chans, 3 * chans), BF)
    (packed,) = call(pack_kernel, [shape((6, chans, cols), BF)], [x, c])
    gathered = lax.all_gather(packed, "lon", axis=0)
    strip = shape((chans, 4 * cols), BF)
    five = shape((5, chans, cols), BF)
    sx, sc, to_south, to_north, forward_one, back_one, forward_two, back_two = call(
        strip_kernel,
        [strip, strip, five, five] + [square] * 4,
        [jnp.asarray(strip_chooser(rows, cols)), x, c, gathered, weight_one, weight_two],
    )
    southward = [(i, (i + 1) % lat_count) for i in range(lat_count)]
    northward = [(target, source) for source, target in southward]
    from_north = lax.ppermute(to_south, "lat", southward)
    from_south = lax.ppermute(to_north, "lat", northward)

    conv_flops = 2 * 9 * chans * chans * rows * cols
    taller = shape((rows + 2, chans, cols), BF)
    edges = shape((chans, cols), BF)
    patches = shape((4, chans, cols), F32)
    partial = shape((3 * chans, 3 * chans), F32)
    h, d, pole, patch, rim, part_one, part_two = call(
        interior_kernel,
        [taller, taller, shape((4, chans, cols), BF), patches, shape((chans, cols), F32)] + [partial] * 2,
        [north_map, north_code, south_map, south_code, jnp.asarray(end_choosers(chans, cols))]
        + [x, c, gathered, sx, sc]
        + [forward_one, back_two, back_one],
        [
            pltpu.VMEM((n * chans, cols), BF),
            pltpu.VMEM((3, chans, n * cols), BF),
            pltpu.VMEM((2, chans, n * cols), BF),
            pltpu.VMEM((chans, n * cols), F32),
            pltpu.VMEM((n, chans, cols), F32),
            pltpu.VMEM((n, chans, cols), BF),
            pltpu.VMEM((n, chans, cols), BF),
        ]
        + [pltpu.SMEM((n,), jnp.int32)] * 4
        + [pltpu.SemaphoreType.DMA((4,))],
        pinned=4,
        flops=2 * conv_flops,
    )
    h, d, hs, ds, grads = call(
        finish_kernel,
        [taller, taller, edges, edges, shape((3, 3 * chans, cols), F32)],
        [h, d, part_one, part_two, pole, patch, x, c, sx, sc, from_north, from_south, forward_one, back_two],
        [
            pltpu.VMEM((rows + 4, chans, cols), BF),
            pltpu.VMEM((rows + 4, chans, cols), BF),
            pltpu.VMEM((chans, 4 * cols), BF),
            pltpu.VMEM((chans, 4 * cols), BF),
            pltpu.VMEM((chans, cols), F32),
            pltpu.VMEM((chans, cols), F32),
            pltpu.VMEM((3 * chans, 3 * chans), F32),
            pltpu.VMEM((3 * chans, 3 * chans), F32),
        ],
        flops=2 * conv_flops,
    )

    flat = grads.reshape(2, -1, cols)
    mine = lax.axis_index("lon") % 2
    swap = [(i, i ^ 1) for i in range(n)]
    kept = lax.dynamic_index_in_dim(flat, mine, 0, keepdims=False)
    given = lax.dynamic_index_in_dim(flat, 1 - mine, 0, keepdims=False)
    half = kept + lax.ppermute(given, "lon", swap)
    device_count = n * lat_count
    bits = [1 << k for k in range(device_count.bit_length() - 1) if 1 << k != lat_count]
    groups = [bits[k : k + 2] for k in range(0, len(bits) - 1, 2)]
    middle = len(groups) // 2
    left = [bits[-1:]] if len(bits) % 2 else []
    orders = groups[middle:] + groups[:middle] + left, groups + left
    stages = len(orders[0])
    low = shape((rows, chans, cols), BF)
    for k in range(stages):
        sent = half.astype(BF)
        if k == 0:
            sent, h = lax.optimization_barrier((sent, h))
        if k == 1:
            sent, d = lax.optimization_barrier((sent, d))
        got = [sent]
        for step in range(1, 1 << len(orders[0][k])):
            jumps = [sum(bit for at, bit in enumerate(order[k]) if step >> at & 1) for order in orders]
            pairs = [(i, i ^ jumps[i // lat_count % 2]) for i in range(device_count)]
            got.append(lax.ppermute(sent, ("lon", "lat"), pairs))
        got = [part.astype(F32) for part in got]
        half = (got[0] + got[1]) + (got[2] + got[3]) if len(got) == 4 else got[0] + got[1]
        if k == 0:
            (out,) = call(out_kernel, [low], [h, hs, forward_two], flops=conv_flops)
            out = native(out)
            half, out = lax.optimization_barrier((half, out))
        if k == 1:
            (d_fields,) = call(fields_kernel, [low], [d, ds, rim, back_one], flops=conv_flops)
            d_fields = native(d_fields)
            half, d_fields = lax.optimization_barrier((half, d_fields))
    other = lax.ppermute(half, "lon", swap)
    kernel_shape = shape(weight_one.shape, F32)
    one, two = call(
        functools.partial(unpack_kernel, scale=1.0 / math.sqrt(pixel_total)),
        [kernel_shape, kernel_shape],
        [half, other],
        [pltpu.VMEM((9 * chans, cols), F32)],
    )
    return (out, d_fields, one, two)


def solution(mesh):
    placed = (P(None, "lat", "lon"), P(), P(), P(None, "lat", "lon"), P(), P(), P(), P())
    return jax.shard_map(
        on_device,
        mesh=mesh,
        in_specs=placed,
        out_specs=(P(None, "lat", "lon"), P(None, "lat", "lon"), P(), P()),
        check_vma=False,
    )
```

```python
import functools
import math

import jax
import jax.numpy as jnp
from jax import lax
from jax.experimental import pallas as pl
from jax.experimental.pallas import tpu as pltpu
from jax.experimental.layout import Layout, with_layout_constraint
from jax.sharding import PartitionSpec as P

BF = jnp.bfloat16
F32 = jnp.float32
GELU_K = math.sqrt(2.0 / math.pi)
VMEM_LIMIT = 48 * 1024 * 1024


def mm(a, b):
    return jnp.dot(a, b, preferred_element_type=F32)


def mm_t(a, b):
    return lax.dot_general(a, b, (((1,), (1,)), ((), ())), preferred_element_type=F32)


def lane_of(like):
    return lax.broadcasted_iota(jnp.int32, like.shape, like.ndim - 1)


def rot(x, by):
    return pltpu.roll(x, by, x.ndim - 1)


def gelu_parts(u):
    square = u * u
    t = jnp.tanh(GELU_K * u * (1.0 + 0.044715 * square))
    half = 0.5 + 0.5 * t
    slope = half + (0.5 * GELU_K) * u * (1.0 - t * t) * (1.0 + (3 * 0.044715) * square)
    return u * half, slope


def arrange(w_ref, forward_ref, back_ref):
    chans = w_ref.shape[2]
    diagonal = lax.broadcasted_iota(jnp.int32, (chans, chans), 0) == lax.broadcasted_iota(
        jnp.int32, (chans, chans), 1
    )
    eye = jnp.where(diagonal, 1.0, 0.0).astype(BF)
    for s in range(3):
        here = slice(s * chans, (s + 1) * chans)
        forward_ref[here] = jnp.concatenate([w_ref[r, s] for r in range(3)], axis=1)
        flipped = jnp.concatenate([w_ref[2 - r, 2 - s] for r in range(3)], axis=0)
        back_ref[here] = mm_t(eye, flipped).astype(BF)


def strip_chooser(rows, out_ref):
    source = lax.broadcasted_iota(jnp.int32, out_ref.shape, 0)
    target = lax.broadcasted_iota(jnp.int32, (1, out_ref.shape[1]), 1)
    block, side, row = target // 128, target % 128 // 64, target % 64 - 2
    wanted = 128 * (side + block // 2) + 4 * row + block
    wanted = jnp.where((row >= 0) & (row < rows), wanted, -1)
    out_ref[...] = jnp.where(source == wanted, 1.0, 0.0).astype(BF)


def end_choosers(out_ref):
    _, chans, cols = out_ref.shape
    lane = lax.broadcasted_iota(jnp.int32, (chans, cols), 1)
    spot = lax.broadcasted_iota(jnp.int32, (chans, cols), 0)
    at_end = jnp.where(lane == jnp.where(spot < 32, 0, cols - 1), spot % 16, -1)
    for m in range(16):
        out_ref[m] = jnp.where(at_end == m, 1.0, 0.0).astype(BF)


def pack_kernel(
    x_hbm, c_hbm, w1_hbm, w2_hbm,
    x_ref, c_ref, out_ref, f1_ref, b1_ref, f2_ref, b2_ref, chooser_ref, hot_ref,
    xin, cin, w1_ref, w2_ref, sems, weight_sems,
):
    rows, chans, _ = x_ref.shape
    pieces = []
    for k, start in enumerate(range(0, chans, 16)):
        here = pl.ds(start, 16)
        for side, (src, held, dst) in enumerate(((x_hbm, xin, x_ref), (c_hbm, cin, c_ref))):
            copy = pltpu.make_async_copy(src.at[here], held.at[here], sems.at[side, k])
            copy.start()
            pieces.append((copy, held, dst, here))
    weights = [
        pltpu.make_async_copy(src, dst, weight_sems.at[k])
        for k, (src, dst) in enumerate(((w1_hbm, w1_ref), (w2_hbm, w2_ref)))
    ]
    for copy in weights:
        copy.start()
    strip_chooser(rows, chooser_ref)
    end_choosers(hot_ref)
    for copy, held, dst, here in pieces:
        copy.wait()
        dst[:, here] = jnp.swapaxes(held[here], 0, 1)
    bottom = jnp.where(lax.axis_index("lat") == 0, 0, 1)
    edge = bottom * (rows - 1)
    beside = 1 + bottom * (rows - 3)
    out_ref[0] = x_ref[edge]
    out_ref[1] = x_ref[beside]
    out_ref[2] = c_ref[edge]
    out_ref[3] = c_ref[beside]
    for copy in weights:
        copy.wait()
    arrange(w1_ref, f1_ref, b1_ref)
    arrange(w2_ref, f2_ref, b2_ref)
    for at, ref in ((4, x_ref), (5, c_ref)):
        packed = jnp.zeros(ref.shape[1:], F32)
        lane = lane_of(packed)
        for i in range(rows):
            turned = rot(ref[i].astype(F32), (4 * i + 2) % 128)
            packed = jnp.where((lane >= 4 * i) & (lane < 4 * i + 4), turned, packed)
        out_ref[at] = packed.astype(BF)


def strip_kernel(
    chooser_ref, x_ref, c_ref, all_ref,
    sx_ref, sc_ref, south_ref, north_ref,
):
    rows, chans, cols = x_ref.shape
    n = all_ref.shape[0]
    me = lax.axis_index("lon")
    west = lax.rem(me + n - 1, n)
    east = lax.rem(me + 1, n)
    to_south = jnp.zeros((chans, cols), F32)
    to_north = jnp.zeros((chans, cols), F32)
    lane = lane_of(to_south)
    pair = (lane % 64) // 2
    for at, ref in ((0, sx_ref), (1, sc_ref)):
        taken = jnp.concatenate([all_ref[west, 4 + at], all_ref[me, 4 + at], all_ref[east, 4 + at]], axis=1)
        strip = mm(taken, chooser_ref[...])
        ref[...] = strip.astype(BF)
        for b in range(4):
            m = 4 * at + b
            piece = strip[:, 128 * b : 128 * b + 128]
            to_south = jnp.where(pair == m, rot(piece, (2 * m - rows) % 128), to_south)
            to_north = jnp.where(pair == m, rot(piece, (2 * m - 2) % 128), to_north)
    for ref, start, corner in ((south_ref, rows - 2, to_south), (north_ref, 0, to_north)):
        for k in range(2):
            ref[k] = x_ref[start + k]
            ref[2 + k] = c_ref[start + k]
        ref[4] = corner.astype(BF)


def shifted_rows(ref, at):
    both = ref[pl.ds(at, 2)]
    lane = lane_of(both[0])
    zero = jnp.zeros_like(both[0])
    parts = []
    for k in range(2):
        ahead = jnp.where(lane == lane.shape[1] - 1, zero, rot(both[k], lane.shape[1] - 1))
        behind = jnp.where(lane == 0, zero, rot(both[k], 1))
        parts.append(jnp.concatenate([ahead, both[k], behind], axis=0))
    return jnp.concatenate(parts, axis=1)


def row_stack(strip):
    wide = strip.astype(F32)
    parts = [wide[:, at : at + 128] for at in range(0, wide.shape[1], 128)]
    above = jnp.concatenate([rot(p, 1) for p in parts], axis=1).astype(BF)
    below = jnp.concatenate([rot(p, 127) for p in parts], axis=1).astype(BF)
    return jnp.concatenate([above, strip, below], axis=0)


def joined(z, chans, place, edge_w, edge_e):
    lane = lane_of(edge_w)
    low = jnp.where(lane == 0, rot(edge_w, 128 - place), rot(z[:chans], 1))
    high = jnp.where(lane == 127, rot(edge_e, 63 - place), rot(z[2 * chans :], 127))
    return low + z[chans : 2 * chans] + high


def pair_of_rows(ref, at):
    four = ref[pl.ds(at, 4)]
    _, chans, cols = four.shape
    return jnp.concatenate(
        [four[:3].reshape(3 * chans, cols), four[1:].reshape(3 * chans, cols)], axis=1
    )


def ring_sum(z, chans):
    return rot(z[:chans], 1) + z[chans : 2 * chans] + rot(z[2 * chans :], z.shape[1] - 1)


def with_edges(a, west, east, group):
    chans = west.shape[0]
    parts = []
    for edge, start in ((west, 16 * group), (east, 64 + 16 * group)):
        term = edge[:, start : start + 16]
        high = term.astype(BF).astype(F32)
        parts += [high, term - high]
    middle = jnp.concatenate(parts, axis=1)
    none = jnp.zeros_like(middle)
    return jnp.concatenate([a, jnp.concatenate([none, middle, none], axis=0).astype(BF)], axis=1)


def interior_kernel(
    nmap_hbm, ncode_hbm, smap_hbm, scode_hbm, hot, x_ref, c_ref, all_ref, sx_ref, sc_ref, a1_ref, a2_ref, a3_ref,
    h_ref, d_ref, pole_ref, patch_ref, rim_ref, acc1, acc2,
    picked, stack, around, slopes, tiles, hring, dring, nmap, ncode, smap, scode, sems,
):
    tables = [
        pltpu.make_async_copy(src, dst, sems.at[k])
        for k, (src, dst) in enumerate(
            ((nmap_hbm, nmap), (ncode_hbm, ncode), (smap_hbm, smap), (scode_hbm, scode))
        )
    ]
    for table in tables:
        table.start()
    rows, chans, cols = x_ref.shape
    a1 = a1_ref[...]
    a2 = a2_ref[...]
    zx = mm(a1, row_stack(sx_ref[:, 128:384]))
    zc = mm(a2, row_stack(sc_ref[:, 128:384]))
    groups = range((rows + 2) // 16 + 1)
    a1_edges = [with_edges(a1, zx[:chans, :128], zx[2 * chans :, 128:], g) for g in groups]
    a2_edges = [with_edges(a2, zc[:chans, :128], zc[2 * chans :, 128:], g) for g in groups]
    lane = lax.broadcasted_iota(jnp.int32, (chans, cols), 1)
    def summed(z):
        low = jnp.where(lane == 0, 0.0, rot(z[:chans], 1))
        high = jnp.where(lane == cols - 1, 0.0, rot(z[2 * chans :], 127))
        return low + z[chans : 2 * chans] + high

    def product(choices, ref, y):
        four = ref[y - 1 : y + 3]
        halves = [
            jnp.concatenate([four[k : k + 3].reshape(3 * chans, cols), hot[(y + 2 + k) % 16]], axis=0)
            for k in range(2)
        ]
        if (y + 2) // 16 == (y + 3) // 16:
            z = mm(choices[(y + 2) // 16], jnp.concatenate(halves, axis=1))
            return z[:, :cols], z[:, cols:]
        return [mm(choices[(y + 2 + k) // 16], halves[k]) for k in range(2)]

    def two_rows(y):
        for k, (z1, z2) in enumerate(zip(product(a1_edges, x_ref, y), product(a2_edges, c_ref, y))):
            value, slope = gelu_parts(summed(z1))
            h_ref[y + 1 + k] = value.astype(BF)
            d_ref[y + 1 + k] = (slope * summed(z2)).astype(BF)

    def gradients(y):
        two = mm_t(shifted_rows(c_ref, y), pair_of_rows(h_ref, y))
        one = mm_t(shifted_rows(d_ref, y + 1), pair_of_rows(x_ref, y - 1))
        acc2[...] = two if y == 2 else acc2[...] + two
        acc1[...] = one if y == 2 else acc1[...] + one

    todo = list(range(1, rows - 1, 2))
    for y in todo[:4]:
        two_rows(y)
    for table in tables:
        table.wait()
    parts = pole_ring(
        rows, all_ref, a1, a2, a3_ref, pole_ref, patch_ref, rim_ref,
        picked, stack, around, slopes, tiles, hring, dring, nmap, ncode, smap, scode,
    )
    for y in todo[4:]:
        next(parts, None)
        two_rows(y)
    for _ in parts:
        pass
    for y in range(2, rows - 2, 2):
        gradients(y)


def pole_ring(
    rows, all_ref, a1, a2, a3_ref, pole_ref, patch_ref, rim_ref,
    picked, stack, around, slopes, tiles, hring, dring, nmap, ncode, smap, scode,
):
    n, _, chans, cols = all_ref.shape
    lat = lax.axis_index("lat")
    me = lax.axis_index("lon")
    at_top = lat == 0
    at_pole = at_top | (lat == lax.axis_size("lat") - 1)
    block = (chans, cols)
    lane = lax.broadcasted_iota(jnp.int32, block, 1)
    west = lax.rem(me + n - 1, n)
    east = lax.rem(me + 1, n)
    first = jnp.where(at_top, 0, 2)
    last = 2 - first
    place = jnp.where(at_top, 1, rows + 2)
    inner = jnp.where(at_top, 2, rows + 1)
    flip = jnp.where(
        lax.broadcasted_iota(jnp.int32, (cols, cols), 0)
        + lax.broadcasted_iota(jnp.int32, (cols, cols), 1)
        == cols - 1,
        1.0,
        0.0,
    ).astype(BF)
    spans = [slice(128 * b, 128 * b + 128) for b in range(n)]
    partner = [jnp.where(at_top, nmap[b], smap[b]) for b in range(n)]
    code = [jnp.where(at_top, ncode[b], scode[b]) for b in range(n)]

    def partner_of(b):
        return jnp.where(at_top, nmap[b], smap[b])

    def code_of(b):
        return jnp.where(at_top, ncode[b], scode[b])

    def halves(wide):
        high = wide.astype(BF)
        return high, (wide - high.astype(F32)).astype(BF)

    for b in range(n):
        picked[b * chans : (b + 1) * chans] = all_ref[partner[b], 0]
    turned = mm(picked[...], flip)
    for b in range(n):
        here = slice(b * chans, (b + 1) * chans)
        across = jnp.where(code[b] == 1, turned[here], picked[here].astype(F32))
        tiles[b] = across
        stack[first, :, spans[b]] = across.astype(BF)
        stack[1, :, spans[b]] = all_ref[b, 0]
        stack[last, :, spans[b]] = all_ref[b, 1]
    yield

    def ends(held, at, west_tile, east_tile):
        held = jnp.where(lane == at, rot(west_tile, at + 1), held)
        return jnp.where(lane == 64 + at, rot(east_tile, 64 + at), held)

    none = jnp.zeros(block, F32)
    pole_ref[3] = tiles[me].astype(BF)
    patch_ref[2] = ends(none, place, tiles[west], tiles[east])
    u = ring_sum(mm(a1, stack[...].reshape(3 * chans, n * cols)), chans)
    value, slope = gelu_parts(u)
    slopes[...] = slope
    for b in range(n):
        hring[b] = value[:, spans[b]].astype(BF)
    yield

    wide = a2.astype(F32)
    empty = jnp.zeros((3 * chans, chans), F32)
    over = jnp.where(
        at_top,
        jnp.concatenate([wide[:, 2 * chans :], empty], axis=1),
        jnp.concatenate([empty, wide[:, :chans]], axis=1),
    )
    rest = jnp.where(at_top, wide[:, chans:], wide[:, : 2 * chans])
    near = jnp.where(at_top, 0, 1)
    for b in range(n):
        around[near, :, spans[b]] = all_ref[b, 2]
        around[1 - near, :, spans[b]] = all_ref[b, 3]
    both = around[...].reshape(2 * chans, n * cols)
    rim = ring_sum(mm(over.astype(BF), both), chans)
    yield
    tall = jnp.concatenate([rim[:, span] for span in spans], axis=0)
    high, low = halves(tall)
    turned = mm(high, flip) + mm(low, flip)
    for b in range(n):
        here = slice(b * chans, (b + 1) * chans)
        tiles[partner[b]] = jnp.where(code[b] == 1, turned[here], tall[here])
    yield
    back = ring_sum(mm(rest.astype(BF), both), chans)
    for b in range(n):
        dring[b] = (slopes[:, spans[b]] * (back[:, spans[b]] + tiles[b])).astype(BF)
    yield

    origin = 0
    for b in range(n):
        origin = origin + jnp.where(partner[b] == me, b, 0)
    three = jnp.concatenate(
        [dring[lax.rem(origin + n - 1, n)], dring[origin], dring[lax.rem(origin + 1, n)]], axis=1
    )
    wide = a3_ref[...].astype(F32)
    over = jnp.where(at_top, wide[:, 2 * chans :], wide[:, :chans])
    rim = ring_sum(mm(over.astype(BF), three), chans)[:, cols : 2 * cols]
    high, low = halves(rim)
    rim = jnp.where(code_of(origin) == 1, mm(high, flip) + mm(low, flip), rim)
    rim_ref[...] = jnp.where(at_pole, rim, none)
    yield

    pole_ref[0] = hring[me]
    pole_ref[1] = dring[me]
    whose = (me, west, east)
    found = jnp.concatenate([hring[partner_of(b)] for b in whose], axis=0)
    turned = mm(found, flip)
    own, beyond_west, beyond_east = (
        jnp.where(
            code_of(b) == 1,
            turned[k * chans : (k + 1) * chans],
            found[k * chans : (k + 1) * chans].astype(F32),
        )
        for k, b in enumerate(whose)
    )
    pole_ref[2] = own.astype(BF)
    held = ends(none, place, beyond_west, beyond_east)
    patch_ref[0] = ends(held, inner, hring[west].astype(F32), hring[east].astype(F32))
    patch_ref[1] = ends(none, inner, dring[west].astype(F32), dring[east].astype(F32))
    mine = dring[me].astype(F32)
    patch_ref[3] = jnp.where(lane < 64, rot(mine, inner), rot(mine, 65 + inner))


def rows_at_once(z1, z2, xw, xeast, cw, ceast, chans, place, h_ref, d_ref, at):
    for k in range(2):
        span = slice(128 * k, 128 * k + 128)
        u = joined(z1[:, span], chans, place + k, xw, xeast)
        back = joined(z2[:, span], chans, place + k, cw, ceast)
        value, slope = gelu_parts(u)
        h_ref[at + k] = value.astype(BF)
        d_ref[at + k] = (slope * back).astype(BF)


def finish_kernel(
    hin_ref, din_ref, in1_ref, in2_ref, pole_ref, patch_ref, x_ref, c_ref, sx_ref, sc_ref, fn_ref, fs_ref, a1_ref, a2_ref,
    h_ref, d_ref, hs_ref, ds_ref, g_ref,
    xe, ce, sxe, sce, dcol, xrim, acc1, acc2,
):
    rows, chans, cols = x_ref.shape
    lat = lax.axis_index("lat")
    at_top = lat == 0
    at_bottom = lat == lax.axis_size("lat") - 1
    block = (chans, cols)
    lane = lax.broadcasted_iota(jnp.int32, block, 1)
    row_lane = lane % 64
    h_ref[2:rows] = hin_ref[2:rows]
    d_ref[2:rows] = din_ref[2:rows]

    xe[2 : rows + 2] = x_ref[...]
    ce[2 : rows + 2] = c_ref[...]
    xe[0:2] = fn_ref[0:2]
    ce[0:2] = fn_ref[2:4]
    xe[rows + 2 : rows + 4] = fs_ref[0:2]
    ce[rows + 2 : rows + 4] = fs_ref[2:4]
    corner_n = fn_ref[4].astype(F32)
    corner_s = fs_ref[4].astype(F32)
    for at, (src, dst) in enumerate(((sx_ref, sxe), (sc_ref, sce))):
        for b in range(4):
            m = 4 * at + b
            piece = src[:, 128 * b : 128 * b + 128].astype(F32)
            piece = jnp.where(row_lane < 2, rot(corner_n, (-2 * m) % 128), piece)
            piece = jnp.where(
                (row_lane >= rows + 2) & (row_lane < rows + 4),
                rot(corner_s, (rows + 2 - 2 * m) % 128),
                piece,
            )
            dst[:, 128 * b : 128 * b + 128] = piece.astype(BF)

    a1 = a1_ref[...]
    a2 = a2_ref[...]
    zx = mm(a1, row_stack(sxe[...]))
    zc = mm(a2, row_stack(sce[...]))

    def both_ends(z):
        return [
            z[:chans, at : at + 128] + z[chans : 2 * chans, at + 128 : at + 256] + z[2 * chans :, at + 256 : at + 384]
            for at in (0, 128)
        ]

    west_side = lane < 64
    found = [(value, slope * back) for (value, slope), back in zip(map(gelu_parts, both_ends(zx)), both_ends(zc))]
    hs_ref[...] = jnp.where(west_side, found[0][0], found[1][0]).astype(BF)
    ds_ref[...] = jnp.where(west_side, found[0][1], found[1][1]).astype(BF)
    dcol[...] = jnp.where(west_side, found[1][1], found[0][1])
    xrim[...] = jnp.where(west_side, sxe[:, 128:256].astype(F32), sxe[:, 256:384].astype(F32))
    xw, xeast = zx[:chans, 128:256], zx[2 * chans :, 256:384]
    cw, ceast = zc[:chans, 128:256], zc[2 * chans :, 256:384]
    for t in (0, rows):
        rows_at_once(
            mm(a1, pair_of_rows(xe, t)), mm(a2, pair_of_rows(ce, t)),
            xw, xeast, cw, ceast, chans, t + 1, h_ref, d_ref, t,
        )

    @pl.when(at_top | at_bottom)
    def _():
        place = jnp.where(at_top, 1, rows + 2)
        inner = jnp.where(at_top, 2, rows + 1)
        outer_row = jnp.where(at_top, 0, rows + 1)
        inner_row = jnp.where(at_top, 1, rows)
        h_ref[inner_row] = pole_ref[0]
        d_ref[inner_row] = pole_ref[1]
        h_ref[outer_row] = pole_ref[2]
        d_ref[outer_row] = jnp.zeros(block, BF)
        xe[jnp.where(at_top, 1, rows + 2)] = pole_ref[3]
        at_place = row_lane == place
        at_pole = at_place | (row_lane == inner)
        hs_ref[...] = jnp.where(at_pole, patch_ref[0], hs_ref[...].astype(F32)).astype(BF)
        ds_ref[...] = jnp.where(at_pole, patch_ref[1], ds_ref[...].astype(F32)).astype(BF)
        xrim[...] = jnp.where(at_place, patch_ref[2], xrim[...])
        dcol[...] = jnp.where(row_lane == inner, patch_ref[3], dcol[...])

    own = (row_lane >= 2) & (row_lane < rows + 2)
    none = jnp.zeros(block, F32)

    def rim_terms(west_part, east_part):
        return jnp.concatenate(
            [
                jnp.where(own & (lane < 64), west_part, none),
                none,
                jnp.where(own & (lane >= 64), east_part, none),
            ],
            axis=0,
        ).astype(BF)

    west_cot = sce[:, 256:384].astype(F32)
    east_cot = sce[:, 128:256].astype(F32)
    acc2[...] = in2_ref[...] + mm_t(rim_terms(west_cot, east_cot), row_stack(hs_ref[...]))
    acc1[...] = in1_ref[...] + mm_t(rim_terms(dcol[...], dcol[...]), row_stack(xrim[...].astype(BF)))
    for y in (0, rows - 2):
        acc2[...] += mm_t(shifted_rows(ce, y + 2), pair_of_rows(h_ref, y))
        acc1[...] += mm_t(shifted_rows(d_ref, y + 1), pair_of_rows(xe, y + 1))
    g2 = acc2[...]
    g1 = acc1[...]
    g_ref[0] = g2[:, :128]
    g_ref[1] = g1[:, :128]
    g_ref[2] = jnp.concatenate([g2[:, 128:], g1[:, 128:]], axis=1)


def out_kernel(h_ref, hs_ref, b2_ref, out_ref):
    rows, chans, _ = out_ref.shape
    b2 = b2_ref[...]
    zh = mm(b2, row_stack(hs_ref[...]))

    def two_rows(step, _):
        t = 2 * step
        z = mm(b2, pair_of_rows(h_ref, t))
        for k in range(2):
            row = joined(z[:, 128 * k : 128 * k + 128], chans, t + k + 2, zh[:chans], zh[2 * chans :])
            out_ref[t + k] = row.astype(BF)
        return 0

    lax.fori_loop(0, rows // 2, two_rows, 0, unroll=True)


def fields_kernel(d_ref, ds_ref, rim_ref, b1_ref, out_ref):
    rows, chans, _ = out_ref.shape
    lat = lax.axis_index("lat")
    b1 = b1_ref[...]
    zd = mm(b1, row_stack(ds_ref[...]))

    def two_rows(step, _):
        t = 2 * step
        z = mm(b1, pair_of_rows(d_ref, t))
        for k in range(2):
            row = joined(z[:, 128 * k : 128 * k + 128], chans, t + k + 2, zd[:chans], zd[2 * chans :])
            rim_here = ((t + k == 0) & (lat == 0)) | (
                (t + k == rows - 1) & (lat == lax.axis_size("lat") - 1)
            )
            out_ref[t + k] = (row + jnp.where(rim_here, 1.0, 0.0) * rim_ref[...]).astype(BF)
        return 0

    lax.fori_loop(0, rows // 2, two_rows, 0, unroll=True)


def unpack_kernel(half_ref, other_ref, one_ref, two_ref, whole, *, scale):
    chans = one_ref.shape[2]
    lower = lax.rem(lax.axis_index("lon"), 2) == 0
    count = half_ref.shape[0]
    half = half_ref[...] * scale
    other = other_ref[...] * scale
    whole[:count] = jnp.where(lower, half, other)
    whole[count:] = jnp.where(lower, other, half)
    for at, ref in enumerate((two_ref, one_ref)):
        for s in range(3):
            wide = whole[(3 * at + s) * chans : (3 * at + s + 1) * chans]
            ref[0, s] = wide[:, :chans]
            ref[1, s] = wide[:, chans:]
            ref[2, s] = whole[(6 + s) * chans : (7 + s) * chans][:, chans * at : chans * at + chans]


def call(kernel, outs, args, scratch=(), flops=0, pinned=0):
    args = [pltpu.with_memory_space_constraint(a, pltpu.HBM) for a in args[:pinned]] + args[pinned:]
    space = [pl.BlockSpec(memory_space=pltpu.HBM)] * pinned
    space += [pl.BlockSpec(memory_space=pltpu.VMEM)] * (len(args) - pinned)
    moved = sum(math.prod(a.shape) * a.dtype.itemsize for a in list(args) + list(outs))
    return pl.pallas_call(
        kernel,
        out_shape=tuple(outs),
        in_specs=space,
        out_specs=tuple(pl.BlockSpec(memory_space=pltpu.VMEM) for _ in outs),
        scratch_shapes=list(scratch),
        compiler_params=pltpu.CompilerParams(vmem_limit_bytes=VMEM_LIMIT),
        cost_estimate=pl.CostEstimate(flops=flops, bytes_accessed=moved, transcendentals=0),
    )(*args)


def native(rows_first):
    return with_layout_constraint(rows_first.transpose(1, 0, 2), Layout((0, 1, 2)))


def on_device(
    fields_in, weight_one, weight_two, cotangent, north_map, north_code, south_map, south_code
):
    chans, rows, cols = fields_in.shape
    n = lax.axis_size("lon")
    lat_count = lax.axis_size("lat")
    pixel_total = rows * cols * n * lat_count
    shape = jax.ShapeDtypeStruct
    square = shape((3 * chans, 3 * chans), BF)
    low = shape((rows, chans, cols), BF)
    chooser = shape((3 * cols, 4 * cols), BF)
    x, c, packed, forward_one, back_one, forward_two, back_two, chooser, hot = call(
        pack_kernel,
        [low, low, shape((6, chans, cols), BF)] + [square] * 4 + [chooser, shape((16, chans, cols), BF)],
        [fields_in, cotangent, weight_one, weight_two],
        [
            pltpu.VMEM((chans, rows, cols), BF),
            pltpu.VMEM((chans, rows, cols), BF),
            pltpu.VMEM(weight_one.shape, BF),
            pltpu.VMEM(weight_two.shape, BF),
            pltpu.SemaphoreType.DMA((2, chans // 16)),
            pltpu.SemaphoreType.DMA((2,)),
        ],
        pinned=4,
    )
    gathered = lax.all_gather(packed, "lon", axis=0)
    strip = shape((chans, 4 * cols), BF)
    five = shape((5, chans, cols), BF)
    sx, sc, to_south, to_north = call(
        strip_kernel, [strip, strip, five, five], [chooser, x, c, gathered]
    )
    southward = [(i, (i + 1) % lat_count) for i in range(lat_count)]
    northward = [(target, source) for source, target in southward]
    from_north = lax.ppermute(to_south, "lat", southward)
    from_south = lax.ppermute(to_north, "lat", northward)

    conv_flops = 2 * 9 * chans * chans * rows * cols
    taller = shape((rows + 2, chans, cols), BF)
    edges = shape((chans, cols), BF)
    patches = shape((4, chans, cols), F32)
    partial = shape((3 * chans, 3 * chans), F32)
    h, d, pole, patch, rim, part_one, part_two = call(
        interior_kernel,
        [taller, taller, shape((4, chans, cols), BF), patches, shape((chans, cols), F32)] + [partial] * 2,
        [north_map, north_code, south_map, south_code, hot]
        + [x, c, gathered, sx, sc]
        + [forward_one, back_two, back_one],
        [
            pltpu.VMEM((n * chans, cols), BF),
            pltpu.VMEM((3, chans, n * cols), BF),
            pltpu.VMEM((2, chans, n * cols), BF),
            pltpu.VMEM((chans, n * cols), F32),
            pltpu.VMEM((n, chans, cols), F32),
            pltpu.VMEM((n, chans, cols), BF),
            pltpu.VMEM((n, chans, cols), BF),
        ]
        + [pltpu.SMEM((n,), jnp.int32)] * 4
        + [pltpu.SemaphoreType.DMA((4,))],
        pinned=4,
        flops=2 * conv_flops,
    )
    h, d, hs, ds, grads = call(
        finish_kernel,
        [taller, taller, edges, edges, shape((3, 3 * chans, cols), F32)],
        [h, d, part_one, part_two, pole, patch, x, c, sx, sc, from_north, from_south, forward_one, back_two],
        [
            pltpu.VMEM((rows + 4, chans, cols), BF),
            pltpu.VMEM((rows + 4, chans, cols), BF),
            pltpu.VMEM((chans, 4 * cols), BF),
            pltpu.VMEM((chans, 4 * cols), BF),
            pltpu.VMEM((chans, cols), F32),
            pltpu.VMEM((chans, cols), F32),
            pltpu.VMEM((3 * chans, 3 * chans), F32),
            pltpu.VMEM((3 * chans, 3 * chans), F32),
        ],
        flops=2 * conv_flops,
    )

    flat = grads.reshape(2, -1, cols)
    mine = lax.axis_index("lon") % 2
    swap = [(i, i ^ 1) for i in range(n)]
    kept = lax.dynamic_index_in_dim(flat, mine, 0, keepdims=False)
    given = lax.dynamic_index_in_dim(flat, 1 - mine, 0, keepdims=False)
    half = kept + lax.ppermute(given, "lon", swap)
    device_count = n * lat_count
    bits = [1 << k for k in range(device_count.bit_length() - 1) if 1 << k != lat_count]
    groups = [bits[k : k + 2] for k in range(0, len(bits) - 1, 2)]
    middle = len(groups) // 2
    left = [bits[-1:]] if len(bits) % 2 else []
    orders = groups[middle:] + groups[:middle] + left, groups + left
    stages = len(orders[0])
    for k in range(stages):
        sent = half.astype(BF)
        if k == 0:
            sent, h = lax.optimization_barrier((sent, h))
        if k == 1:
            sent, d = lax.optimization_barrier((sent, d))
        got = [sent]
        for step in range(1, 1 << len(orders[0][k])):
            jumps = [sum(bit for at, bit in enumerate(order[k]) if step >> at & 1) for order in orders]
            pairs = [(i, i ^ jumps[i // lat_count % 2]) for i in range(device_count)]
            got.append(lax.ppermute(sent, ("lon", "lat"), pairs))
        got = [part.astype(F32) for part in got]
        half = (got[0] + got[1]) + (got[2] + got[3]) if len(got) == 4 else got[0] + got[1]
        if k == 0:
            (out,) = call(out_kernel, [low], [h, hs, forward_two], flops=conv_flops)
            out = native(out)
            half, out = lax.optimization_barrier((half, out))
        if k == 1:
            (d_fields,) = call(fields_kernel, [low], [d, ds, rim, back_one], flops=conv_flops)
            d_fields = native(d_fields)
            half, d_fields = lax.optimization_barrier((half, d_fields))
    other = lax.ppermute(half, "lon", swap)
    kernel_shape = shape(weight_one.shape, F32)
    one, two = call(
        functools.partial(unpack_kernel, scale=1.0 / math.sqrt(pixel_total)),
        [kernel_shape, kernel_shape],
        [half, other],
        [pltpu.VMEM((9 * chans, cols), F32)],
    )
    return (out, d_fields, one, two)


def solution(mesh):
    placed = (P(None, "lat", "lon"), P(), P(), P(None, "lat", "lon"), P(), P(), P(), P())
    return jax.shard_map(
        on_device,
        mesh=mesh,
        in_specs=placed,
        out_specs=(P(None, "lat", "lon"), P(None, "lat", "lon"), P(), P()),
        check_vma=False,
    )
```

```python
import functools
import math

import jax
import jax.numpy as jnp
from jax import lax
from jax.experimental import pallas as pl
from jax.experimental.pallas import tpu as pltpu
from jax.experimental.layout import Layout, with_layout_constraint
from jax.sharding import PartitionSpec as P

BF = jnp.bfloat16
F32 = jnp.float32
GELU_K = math.sqrt(2.0 / math.pi)
VMEM_LIMIT = 48 * 1024 * 1024


def mm(a, b):
    return jnp.dot(a, b, preferred_element_type=F32)


def mm_t(a, b):
    return lax.dot_general(a, b, (((1,), (1,)), ((), ())), preferred_element_type=F32)


def lane_of(like):
    return lax.broadcasted_iota(jnp.int32, like.shape, like.ndim - 1)


def rot(x, by):
    return pltpu.roll(x, by, x.ndim - 1)


def gelu_parts(u):
    square = u * u
    t = jnp.tanh(GELU_K * u * (1.0 + 0.044715 * square))
    half = 0.5 + 0.5 * t
    slope = half + (0.5 * GELU_K) * u * (1.0 - t * t) * (1.0 + (3 * 0.044715) * square)
    return u * half, slope


def arrange(w_ref, forward_ref, back_ref):
    chans = w_ref.shape[2]
    diagonal = lax.broadcasted_iota(jnp.int32, (chans, chans), 0) == lax.broadcasted_iota(
        jnp.int32, (chans, chans), 1
    )
    eye = jnp.where(diagonal, 1.0, 0.0).astype(BF)
    for s in range(3):
        here = slice(s * chans, (s + 1) * chans)
        forward_ref[here] = jnp.concatenate([w_ref[r, s] for r in range(3)], axis=1)
        flipped = jnp.concatenate([w_ref[2 - r, 2 - s] for r in range(3)], axis=0)
        back_ref[here] = mm_t(eye, flipped).astype(BF)


def strip_chooser(rows, out_ref):
    source = lax.broadcasted_iota(jnp.int32, out_ref.shape, 0)
    target = lax.broadcasted_iota(jnp.int32, (1, out_ref.shape[1]), 1)
    block, side, row = target // 128, target % 128 // 64, target % 64 - 2
    wanted = 128 * (side + block // 2) + 4 * row + block
    wanted = jnp.where((row >= 0) & (row < rows), wanted, -1)
    out_ref[...] = jnp.where(source == wanted, 1.0, 0.0).astype(BF)


def end_choosers(out_ref):
    _, chans, cols = out_ref.shape
    lane = lax.broadcasted_iota(jnp.int32, (chans, cols), 1)
    spot = lax.broadcasted_iota(jnp.int32, (chans, cols), 0)
    at_end = jnp.where(lane == jnp.where(spot < 32, 0, cols - 1), spot % 16, -1)
    for m in range(16):
        out_ref[m] = jnp.where(at_end == m, 1.0, 0.0).astype(BF)


def pack_kernel(
    x_hbm, c_hbm, w1_hbm, w2_hbm,
    x_ref, c_ref, out_ref, f1_ref, b1_ref, f2_ref, b2_ref, chooser_ref, hot_ref,
    xin, cin, w1_ref, w2_ref, sems, weight_sems,
):
    rows, chans, _ = x_ref.shape
    pieces = []
    for k, start in enumerate(range(0, chans, 16)):
        here = pl.ds(start, 16)
        for side, (src, held, dst) in enumerate(((x_hbm, xin, x_ref), (c_hbm, cin, c_ref))):
            copy = pltpu.make_async_copy(src.at[here], held.at[here], sems.at[side, k])
            copy.start()
            pieces.append((copy, held, dst, here))
    weights = [
        pltpu.make_async_copy(src, dst, weight_sems.at[k])
        for k, (src, dst) in enumerate(((w1_hbm, w1_ref), (w2_hbm, w2_ref)))
    ]
    for copy in weights:
        copy.start()
    strip_chooser(rows, chooser_ref)
    end_choosers(hot_ref)
    for copy, held, dst, here in pieces:
        copy.wait()
        dst[:, here] = jnp.swapaxes(held[here], 0, 1)
    bottom = jnp.where(lax.axis_index("lat") == 0, 0, 1)
    edge = bottom * (rows - 1)
    beside = 1 + bottom * (rows - 3)
    out_ref[0] = x_ref[edge]
    out_ref[1] = x_ref[beside]
    out_ref[2] = c_ref[edge]
    out_ref[3] = c_ref[beside]
    for copy in weights:
        copy.wait()
    arrange(w1_ref, f1_ref, b1_ref)
    arrange(w2_ref, f2_ref, b2_ref)
    for at, ref in ((4, x_ref), (5, c_ref)):
        packed = jnp.zeros(ref.shape[1:], F32)
        lane = lane_of(packed)
        for i in range(rows):
            turned = rot(ref[i].astype(F32), (4 * i + 2) % 128)
            packed = jnp.where((lane >= 4 * i) & (lane < 4 * i + 4), turned, packed)
        out_ref[at] = packed.astype(BF)


def strip_kernel(
    chooser_ref, x_ref, c_ref, all_ref,
    sx_ref, sc_ref, south_ref, north_ref,
):
    rows, chans, cols = x_ref.shape
    n = all_ref.shape[0]
    me = lax.axis_index("lon")
    west = lax.rem(me + n - 1, n)
    east = lax.rem(me + 1, n)
    to_south = jnp.zeros((chans, cols), F32)
    to_north = jnp.zeros((chans, cols), F32)
    lane = lane_of(to_south)
    pair = (lane % 64) // 2
    for at, ref in ((0, sx_ref), (1, sc_ref)):
        taken = jnp.concatenate([all_ref[west, 4 + at], all_ref[me, 4 + at], all_ref[east, 4 + at]], axis=1)
        strip = mm(taken, chooser_ref[...])
        ref[...] = strip.astype(BF)
        for b in range(4):
            m = 4 * at + b
            piece = strip[:, 128 * b : 128 * b + 128]
            to_south = jnp.where(pair == m, rot(piece, (2 * m - rows) % 128), to_south)
            to_north = jnp.where(pair == m, rot(piece, (2 * m - 2) % 128), to_north)
    for ref, start, corner in ((south_ref, rows - 2, to_south), (north_ref, 0, to_north)):
        for k in range(2):
            ref[k] = x_ref[start + k]
            ref[2 + k] = c_ref[start + k]
        ref[4] = corner.astype(BF)


def shifted_rows(ref, at):
    both = ref[pl.ds(at, 2)]
    lane = lane_of(both[0])
    zero = jnp.zeros_like(both[0])
    parts = []
    for k in range(2):
        ahead = jnp.where(lane == lane.shape[1] - 1, zero, rot(both[k], lane.shape[1] - 1))
        behind = jnp.where(lane == 0, zero, rot(both[k], 1))
        parts.append(jnp.concatenate([ahead, both[k], behind], axis=0))
    return jnp.concatenate(parts, axis=1)


def row_stack(strip):
    wide = strip.astype(F32)
    parts = [wide[:, at : at + 128] for at in range(0, wide.shape[1], 128)]
    above = jnp.concatenate([rot(p, 1) for p in parts], axis=1).astype(BF)
    below = jnp.concatenate([rot(p, 127) for p in parts], axis=1).astype(BF)
    return jnp.concatenate([above, strip, below], axis=0)


def joined(z, chans, place, edge_w, edge_e):
    lane = lane_of(edge_w)
    low = jnp.where(lane == 0, rot(edge_w, 128 - place), rot(z[:chans], 1))
    high = jnp.where(lane == 127, rot(edge_e, 63 - place), rot(z[2 * chans :], 127))
    return low + z[chans : 2 * chans] + high


def pair_of_rows(ref, at):
    four = ref[pl.ds(at, 4)]
    _, chans, cols = four.shape
    return jnp.concatenate(
        [four[:3].reshape(3 * chans, cols), four[1:].reshape(3 * chans, cols)], axis=1
    )


def ring_sum(z, chans):
    return rot(z[:chans], 1) + z[chans : 2 * chans] + rot(z[2 * chans :], z.shape[1] - 1)


def with_edges(a, west, east, group):
    chans = west.shape[0]
    parts = []
    for edge, start in ((west, 16 * group), (east, 64 + 16 * group)):
        term = edge[:, start : start + 16]
        high = term.astype(BF).astype(F32)
        parts += [high, term - high]
    middle = jnp.concatenate(parts, axis=1)
    none = jnp.zeros_like(middle)
    return jnp.concatenate([a, jnp.concatenate([none, middle, none], axis=0).astype(BF)], axis=1)


def interior_kernel(
    nmap_hbm, ncode_hbm, smap_hbm, scode_hbm, hot, x_ref, c_ref, all_ref, sx_ref, sc_ref, a1_ref, a2_ref, a3_ref,
    h_ref, d_ref, pole_ref, patch_ref, rim_ref, acc1, acc2,
    picked, stack, around, slopes, tiles, hring, dring, nmap, ncode, smap, scode, sems,
):
    tables = [
        pltpu.make_async_copy(src, dst, sems.at[k])
        for k, (src, dst) in enumerate(
            ((nmap_hbm, nmap), (ncode_hbm, ncode), (smap_hbm, smap), (scode_hbm, scode))
        )
    ]
    for table in tables:
        table.start()
    rows, chans, cols = x_ref.shape
    a1 = a1_ref[...]
    a2 = a2_ref[...]
    zx = mm(a1, row_stack(sx_ref[:, 128:384]))
    zc = mm(a2, row_stack(sc_ref[:, 128:384]))
    groups = range((rows + 2) // 16 + 1)
    a1_edges = [with_edges(a1, zx[:chans, :128], zx[2 * chans :, 128:], g) for g in groups]
    a2_edges = [with_edges(a2, zc[:chans, :128], zc[2 * chans :, 128:], g) for g in groups]
    lane = lax.broadcasted_iota(jnp.int32, (chans, cols), 1)
    def summed(z):
        low = jnp.where(lane == 0, 0.0, rot(z[:chans], 1))
        high = jnp.where(lane == cols - 1, 0.0, rot(z[2 * chans :], 127))
        return low + z[chans : 2 * chans] + high

    def product(choices, ref, y):
        four = ref[y - 1 : y + 3]
        halves = [
            jnp.concatenate([four[k : k + 3].reshape(3 * chans, cols), hot[(y + 2 + k) % 16]], axis=0)
            for k in range(2)
        ]
        if (y + 2) // 16 == (y + 3) // 16:
            z = mm(choices[(y + 2) // 16], jnp.concatenate(halves, axis=1))
            return z[:, :cols], z[:, cols:]
        return [mm(choices[(y + 2 + k) // 16], halves[k]) for k in range(2)]

    def two_rows(y):
        for k, (z1, z2) in enumerate(zip(product(a1_edges, x_ref, y), product(a2_edges, c_ref, y))):
            value, slope = gelu_parts(summed(z1))
            h_ref[y + 1 + k] = value.astype(BF)
            d_ref[y + 1 + k] = (slope * summed(z2)).astype(BF)

    def gradients(y):
        two = mm_t(shifted_rows(c_ref, y), pair_of_rows(h_ref, y))
        one = mm_t(shifted_rows(d_ref, y + 1), pair_of_rows(x_ref, y - 1))
        acc2[...] = two if y == 2 else acc2[...] + two
        acc1[...] = one if y == 2 else acc1[...] + one

    todo = list(range(1, rows - 1, 2))
    for y in todo[:4]:
        two_rows(y)
    for table in tables:
        table.wait()
    parts = pole_ring(
        rows, all_ref, a1, a2, a3_ref, pole_ref, patch_ref, rim_ref,
        picked, stack, around, slopes, tiles, hring, dring, nmap, ncode, smap, scode,
    )
    for y in todo[4:]:
        next(parts, None)
        two_rows(y)
    for _ in parts:
        pass
    for y in range(2, rows - 2, 2):
        gradients(y)


def pole_ring(
    rows, all_ref, a1, a2, a3_ref, pole_ref, patch_ref, rim_ref,
    picked, stack, around, slopes, tiles, hring, dring, nmap, ncode, smap, scode,
):
    n, _, chans, cols = all_ref.shape
    lat = lax.axis_index("lat")
    me = lax.axis_index("lon")
    at_top = lat == 0
    at_pole = at_top | (lat == lax.axis_size("lat") - 1)
    block = (chans, cols)
    lane = lax.broadcasted_iota(jnp.int32, block, 1)
    west = lax.rem(me + n - 1, n)
    east = lax.rem(me + 1, n)
    first = jnp.where(at_top, 0, 2)
    last = 2 - first
    place = jnp.where(at_top, 1, rows + 2)
    inner = jnp.where(at_top, 2, rows + 1)
    flip = jnp.where(
        lax.broadcasted_iota(jnp.int32, (cols, cols), 0)
        + lax.broadcasted_iota(jnp.int32, (cols, cols), 1)
        == cols - 1,
        1.0,
        0.0,
    ).astype(BF)
    spans = [slice(128 * b, 128 * b + 128) for b in range(n)]
    partner = [jnp.where(at_top, nmap[b], smap[b]) for b in range(n)]
    code = [jnp.where(at_top, ncode[b], scode[b]) for b in range(n)]

    def partner_of(b):
        return jnp.where(at_top, nmap[b], smap[b])

    def code_of(b):
        return jnp.where(at_top, ncode[b], scode[b])

    def halves(wide):
        high = wide.astype(BF)
        return high, (wide - high.astype(F32)).astype(BF)

    for b in range(n):
        picked[b * chans : (b + 1) * chans] = all_ref[partner[b], 0]
    turned = mm(picked[...], flip)
    for b in range(n):
        here = slice(b * chans, (b + 1) * chans)
        across = jnp.where(code[b] == 1, turned[here], picked[here].astype(F32))
        tiles[b] = across
        stack[first, :, spans[b]] = across.astype(BF)
        stack[1, :, spans[b]] = all_ref[b, 0]
        stack[last, :, spans[b]] = all_ref[b, 1]
    yield

    def ends(held, at, west_tile, east_tile):
        held = jnp.where(lane == at, rot(west_tile, at + 1), held)
        return jnp.where(lane == 64 + at, rot(east_tile, 64 + at), held)

    none = jnp.zeros(block, F32)
    pole_ref[3] = tiles[me].astype(BF)
    patch_ref[2] = ends(none, place, tiles[west], tiles[east])
    u = ring_sum(mm(a1, stack[...].reshape(3 * chans, n * cols)), chans)
    value, slope = gelu_parts(u)
    slopes[...] = slope
    for b in range(n):
        hring[b] = value[:, spans[b]].astype(BF)
    yield

    wide = a2.astype(F32)
    empty = jnp.zeros((3 * chans, chans), F32)
    over = jnp.where(
        at_top,
        jnp.concatenate([wide[:, 2 * chans :], empty], axis=1),
        jnp.concatenate([empty, wide[:, :chans]], axis=1),
    )
    rest = jnp.where(at_top, wide[:, chans:], wide[:, : 2 * chans])
    near = jnp.where(at_top, 0, 1)
    for b in range(n):
        around[near, :, spans[b]] = all_ref[b, 2]
        around[1 - near, :, spans[b]] = all_ref[b, 3]
    both = around[...].reshape(2 * chans, n * cols)
    rim = ring_sum(mm(over.astype(BF), both), chans)
    yield
    tall = jnp.concatenate([rim[:, span] for span in spans], axis=0)
    high, low = halves(tall)
    turned = mm(high, flip) + mm(low, flip)
    for b in range(n):
        here = slice(b * chans, (b + 1) * chans)
        tiles[partner[b]] = jnp.where(code[b] == 1, turned[here], tall[here])
    yield
    back = ring_sum(mm(rest.astype(BF), both), chans)
    for b in range(n):
        dring[b] = (slopes[:, spans[b]] * (back[:, spans[b]] + tiles[b])).astype(BF)
    yield

    origin = 0
    for b in range(n):
        origin = origin + jnp.where(partner[b] == me, b, 0)
    three = jnp.concatenate(
        [dring[lax.rem(origin + n - 1, n)], dring[origin], dring[lax.rem(origin + 1, n)]], axis=1
    )
    wide = a3_ref[...].astype(F32)
    over = jnp.where(at_top, wide[:, 2 * chans :], wide[:, :chans])
    rim = ring_sum(mm(over.astype(BF), three), chans)[:, cols : 2 * cols]
    high, low = halves(rim)
    rim = jnp.where(code_of(origin) == 1, mm(high, flip) + mm(low, flip), rim)
    rim_ref[...] = jnp.where(at_pole, rim, none)
    yield

    pole_ref[0] = hring[me]
    pole_ref[1] = dring[me]
    whose = (me, west, east)
    found = jnp.concatenate([hring[partner_of(b)] for b in whose], axis=0)
    turned = mm(found, flip)
    own, beyond_west, beyond_east = (
        jnp.where(
            code_of(b) == 1,
            turned[k * chans : (k + 1) * chans],
            found[k * chans : (k + 1) * chans].astype(F32),
        )
        for k, b in enumerate(whose)
    )
    pole_ref[2] = own.astype(BF)
    held = ends(none, place, beyond_west, beyond_east)
    patch_ref[0] = ends(held, inner, hring[west].astype(F32), hring[east].astype(F32))
    patch_ref[1] = ends(none, inner, dring[west].astype(F32), dring[east].astype(F32))
    mine = dring[me].astype(F32)
    patch_ref[3] = jnp.where(lane < 64, rot(mine, inner), rot(mine, 65 + inner))


def rows_at_once(z1, z2, xw, xeast, cw, ceast, chans, place, h_ref, d_ref, at):
    for k in range(2):
        span = slice(128 * k, 128 * k + 128)
        u = joined(z1[:, span], chans, place + k, xw, xeast)
        back = joined(z2[:, span], chans, place + k, cw, ceast)
        value, slope = gelu_parts(u)
        h_ref[at + k] = value.astype(BF)
        d_ref[at + k] = (slope * back).astype(BF)


def finish_kernel(
    hin_ref, din_ref, in1_ref, in2_ref, pole_ref, patch_ref, x_ref, c_ref, sx_ref, sc_ref, fn_ref, fs_ref, a1_ref, a2_ref,
    h_ref, d_ref, hs_ref, ds_ref, g_ref,
    xe, ce, sxe, sce, dcol, xrim, acc1, acc2,
):
    rows, chans, cols = x_ref.shape
    lat = lax.axis_index("lat")
    at_top = lat == 0
    at_bottom = lat == lax.axis_size("lat") - 1
    block = (chans, cols)
    lane = lax.broadcasted_iota(jnp.int32, block, 1)
    row_lane = lane % 64
    h_ref[2:rows] = hin_ref[2:rows]
    d_ref[2:rows] = din_ref[2:rows]

    xe[2 : rows + 2] = x_ref[...]
    ce[2 : rows + 2] = c_ref[...]
    xe[0:2] = fn_ref[0:2]
    ce[0:2] = fn_ref[2:4]
    xe[rows + 2 : rows + 4] = fs_ref[0:2]
    ce[rows + 2 : rows + 4] = fs_ref[2:4]
    corner_n = fn_ref[4].astype(F32)
    corner_s = fs_ref[4].astype(F32)
    for at, (src, dst) in enumerate(((sx_ref, sxe), (sc_ref, sce))):
        for b in range(4):
            m = 4 * at + b
            piece = src[:, 128 * b : 128 * b + 128].astype(F32)
            piece = jnp.where(row_lane < 2, rot(corner_n, (-2 * m) % 128), piece)
            piece = jnp.where(
                (row_lane >= rows + 2) & (row_lane < rows + 4),
                rot(corner_s, (rows + 2 - 2 * m) % 128),
                piece,
            )
            dst[:, 128 * b : 128 * b + 128] = piece.astype(BF)

    a1 = a1_ref[...]
    a2 = a2_ref[...]
    zx = mm(a1, row_stack(sxe[...]))
    zc = mm(a2, row_stack(sce[...]))

    def both_ends(z):
        return [
            z[:chans, at : at + 128] + z[chans : 2 * chans, at + 128 : at + 256] + z[2 * chans :, at + 256 : at + 384]
            for at in (0, 128)
        ]

    west_side = lane < 64
    found = [(value, slope * back) for (value, slope), back in zip(map(gelu_parts, both_ends(zx)), both_ends(zc))]
    hs_ref[...] = jnp.where(west_side, found[0][0], found[1][0]).astype(BF)
    ds_ref[...] = jnp.where(west_side, found[0][1], found[1][1]).astype(BF)
    dcol[...] = jnp.where(west_side, found[1][1], found[0][1])
    xrim[...] = jnp.where(west_side, sxe[:, 128:256].astype(F32), sxe[:, 256:384].astype(F32))
    xw, xeast = zx[:chans, 128:256], zx[2 * chans :, 256:384]
    cw, ceast = zc[:chans, 128:256], zc[2 * chans :, 256:384]
    for t in (0, rows):
        rows_at_once(
            mm(a1, pair_of_rows(xe, t)), mm(a2, pair_of_rows(ce, t)),
            xw, xeast, cw, ceast, chans, t + 1, h_ref, d_ref, t,
        )

    @pl.when(at_top | at_bottom)
    def _():
        place = jnp.where(at_top, 1, rows + 2)
        inner = jnp.where(at_top, 2, rows + 1)
        outer_row = jnp.where(at_top, 0, rows + 1)
        inner_row = jnp.where(at_top, 1, rows)
        h_ref[inner_row] = pole_ref[0]
        d_ref[inner_row] = pole_ref[1]
        h_ref[outer_row] = pole_ref[2]
        d_ref[outer_row] = jnp.zeros(block, BF)
        xe[jnp.where(at_top, 1, rows + 2)] = pole_ref[3]
        at_place = row_lane == place
        at_pole = at_place | (row_lane == inner)
        hs_ref[...] = jnp.where(at_pole, patch_ref[0], hs_ref[...].astype(F32)).astype(BF)
        ds_ref[...] = jnp.where(at_pole, patch_ref[1], ds_ref[...].astype(F32)).astype(BF)
        xrim[...] = jnp.where(at_place, patch_ref[2], xrim[...])
        dcol[...] = jnp.where(row_lane == inner, patch_ref[3], dcol[...])

    own = (row_lane >= 2) & (row_lane < rows + 2)
    none = jnp.zeros(block, F32)

    def rim_terms(west_part, east_part):
        return jnp.concatenate(
            [
                jnp.where(own & (lane < 64), west_part, none),
                none,
                jnp.where(own & (lane >= 64), east_part, none),
            ],
            axis=0,
        ).astype(BF)

    west_cot = sce[:, 256:384].astype(F32)
    east_cot = sce[:, 128:256].astype(F32)
    acc2[...] = in2_ref[...] + mm_t(rim_terms(west_cot, east_cot), row_stack(hs_ref[...]))
    acc1[...] = in1_ref[...] + mm_t(rim_terms(dcol[...], dcol[...]), row_stack(xrim[...].astype(BF)))
    for y in (0, rows - 2):
        acc2[...] += mm_t(shifted_rows(ce, y + 2), pair_of_rows(h_ref, y))
        acc1[...] += mm_t(shifted_rows(d_ref, y + 1), pair_of_rows(xe, y + 1))
    g2 = acc2[...]
    g1 = acc1[...]
    g_ref[0] = g2[:, :128]
    g_ref[1] = g1[:, :128]
    g_ref[2] = jnp.concatenate([g2[:, 128:], g1[:, 128:]], axis=1)


def out_kernel(h_ref, hs_ref, b2_ref, out_ref):
    rows, chans, _ = out_ref.shape
    b2 = b2_ref[...]
    zh = mm(b2, row_stack(hs_ref[...]))

    def two_rows(step, _):
        t = 2 * step
        z = mm(b2, pair_of_rows(h_ref, t))
        for k in range(2):
            row = joined(z[:, 128 * k : 128 * k + 128], chans, t + k + 2, zh[:chans], zh[2 * chans :])
            out_ref[t + k] = row.astype(BF)
        return 0

    lax.fori_loop(0, rows // 2, two_rows, 0, unroll=True)


def fields_kernel(d_ref, ds_ref, rim_ref, b1_ref, out_ref):
    rows, chans, _ = out_ref.shape
    lat = lax.axis_index("lat")
    b1 = b1_ref[...]
    zd = mm(b1, row_stack(ds_ref[...]))

    def two_rows(step, _):
        t = 2 * step
        z = mm(b1, pair_of_rows(d_ref, t))
        for k in range(2):
            row = joined(z[:, 128 * k : 128 * k + 128], chans, t + k + 2, zd[:chans], zd[2 * chans :])
            rim_here = ((t + k == 0) & (lat == 0)) | (
                (t + k == rows - 1) & (lat == lax.axis_size("lat") - 1)
            )
            out_ref[t + k] = (row + jnp.where(rim_here, 1.0, 0.0) * rim_ref[...]).astype(BF)
        return 0

    lax.fori_loop(0, rows // 2, two_rows, 0, unroll=True)


def unpack_kernel(half_ref, other_ref, one_ref, two_ref, whole, *, scale):
    chans = one_ref.shape[2]
    lower = lax.rem(lax.axis_index("lon"), 2) == 0
    count = half_ref.shape[0]
    half = half_ref[...] * scale
    other = other_ref[...] * scale
    whole[:count] = jnp.where(lower, half, other)
    whole[count:] = jnp.where(lower, other, half)
    for at, ref in enumerate((two_ref, one_ref)):
        for s in range(3):
            wide = whole[(3 * at + s) * chans : (3 * at + s + 1) * chans]
            ref[0, s] = wide[:, :chans]
            ref[1, s] = wide[:, chans:]
            ref[2, s] = whole[(6 + s) * chans : (7 + s) * chans][:, chans * at : chans * at + chans]


def call(kernel, outs, args, scratch=(), flops=0, pinned=0):
    args = [pltpu.with_memory_space_constraint(a, pltpu.HBM) for a in args[:pinned]] + args[pinned:]
    space = [pl.BlockSpec(memory_space=pltpu.HBM)] * pinned
    space += [pl.BlockSpec(memory_space=pltpu.VMEM)] * (len(args) - pinned)
    moved = sum(math.prod(a.shape) * a.dtype.itemsize for a in list(args) + list(outs))
    return pl.pallas_call(
        kernel,
        out_shape=tuple(outs),
        in_specs=space,
        out_specs=tuple(pl.BlockSpec(memory_space=pltpu.VMEM) for _ in outs),
        scratch_shapes=list(scratch),
        compiler_params=pltpu.CompilerParams(vmem_limit_bytes=VMEM_LIMIT),
        cost_estimate=pl.CostEstimate(flops=flops, bytes_accessed=moved, transcendentals=0),
    )(*args)


def native(rows_first):
    return with_layout_constraint(rows_first.transpose(1, 0, 2), Layout((0, 1, 2)))


def on_device(
    fields_in, weight_one, weight_two, cotangent, north_map, north_code, south_map, south_code
):
    chans, rows, cols = fields_in.shape
    n = lax.axis_size("lon")
    lat_count = lax.axis_size("lat")
    pixel_total = rows * cols * n * lat_count
    shape = jax.ShapeDtypeStruct
    square = shape((3 * chans, 3 * chans), BF)
    low = shape((rows, chans, cols), BF)
    chooser = shape((3 * cols, 4 * cols), BF)
    x, c, packed, forward_one, back_one, forward_two, back_two, chooser, hot = call(
        pack_kernel,
        [low, low, shape((6, chans, cols), BF)] + [square] * 4 + [chooser, shape((16, chans, cols), BF)],
        [fields_in, cotangent, weight_one, weight_two],
        [
            pltpu.VMEM((chans, rows, cols), BF),
            pltpu.VMEM((chans, rows, cols), BF),
            pltpu.VMEM(weight_one.shape, BF),
            pltpu.VMEM(weight_two.shape, BF),
            pltpu.SemaphoreType.DMA((2, chans // 16)),
            pltpu.SemaphoreType.DMA((2,)),
        ],
        pinned=4,
    )
    gathered = lax.all_gather(packed, "lon", axis=0)
    strip = shape((chans, 4 * cols), BF)
    five = shape((5, chans, cols), BF)
    sx, sc, to_south, to_north = call(
        strip_kernel, [strip, strip, five, five], [chooser, x, c, gathered]
    )
    southward = [(i, (i + 1) % lat_count) for i in range(lat_count)]
    northward = [(target, source) for source, target in southward]
    from_north = lax.ppermute(to_south, "lat", southward)
    from_south = lax.ppermute(to_north, "lat", northward)

    conv_flops = 2 * 9 * chans * chans * rows * cols
    taller = shape((rows + 2, chans, cols), BF)
    edges = shape((chans, cols), BF)
    patches = shape((4, chans, cols), F32)
    partial = shape((3 * chans, 3 * chans), F32)
    h, d, pole, patch, rim, part_one, part_two = call(
        interior_kernel,
        [taller, taller, shape((4, chans, cols), BF), patches, shape((chans, cols), F32)] + [partial] * 2,
        [north_map, north_code, south_map, south_code, hot]
        + [x, c, gathered, sx, sc]
        + [forward_one, back_two, back_one],
        [
            pltpu.VMEM((n * chans, cols), BF),
            pltpu.VMEM((3, chans, n * cols), BF),
            pltpu.VMEM((2, chans, n * cols), BF),
            pltpu.VMEM((chans, n * cols), F32),
            pltpu.VMEM((n, chans, cols), F32),
            pltpu.VMEM((n, chans, cols), BF),
            pltpu.VMEM((n, chans, cols), BF),
        ]
        + [pltpu.SMEM((n,), jnp.int32)] * 4
        + [pltpu.SemaphoreType.DMA((4,))],
        pinned=4,
        flops=2 * conv_flops,
    )
    h, d, hs, ds, grads = call(
        finish_kernel,
        [taller, taller, edges, edges, shape((3, 3 * chans, cols), F32)],
        [h, d, part_one, part_two, pole, patch, x, c, sx, sc, from_north, from_south, forward_one, back_two],
        [
            pltpu.VMEM((rows + 4, chans, cols), BF),
            pltpu.VMEM((rows + 4, chans, cols), BF),
            pltpu.VMEM((chans, 4 * cols), BF),
            pltpu.VMEM((chans, 4 * cols), BF),
            pltpu.VMEM((chans, cols), F32),
            pltpu.VMEM((chans, cols), F32),
            pltpu.VMEM((3 * chans, 3 * chans), F32),
            pltpu.VMEM((3 * chans, 3 * chans), F32),
        ],
        flops=2 * conv_flops,
    )

    flat = grads.reshape(2, -1, cols)
    mine = lax.axis_index("lon") % 2
    swap = [(i, i ^ 1) for i in range(n)]
    kept = lax.dynamic_index_in_dim(flat, mine, 0, keepdims=False)
    given = lax.dynamic_index_in_dim(flat, 1 - mine, 0, keepdims=False)
    half = kept + lax.ppermute(given, "lon", swap)
    device_count = n * lat_count
    bits = [1 << k for k in range(device_count.bit_length() - 1) if 1 << k != lat_count]
    groups = [bits[k : k + 2] for k in range(0, len(bits) - 1, 2)]
    middle = len(groups) // 2
    left = [bits[-1:]] if len(bits) % 2 else []
    orders = groups[middle:] + groups[:middle] + left, groups + left
    stages = len(orders[0])
    for k in range(stages):
        sent = half.astype(BF)
        if k == 0:
            sent, h = lax.optimization_barrier((sent, h))
        if k == 1:
            sent, d = lax.optimization_barrier((sent, d))
        got = [sent]
        for step in range(1, 1 << len(orders[0][k])):
            jumps = [sum(bit for at, bit in enumerate(order[k]) if step >> at & 1) for order in orders]
            pairs = [(i, i ^ jumps[i // lat_count % 2]) for i in range(device_count)]
            got.append(lax.ppermute(sent, ("lon", "lat"), pairs))
        got = [part.astype(F32) for part in got]
        half = (got[0] + got[3]) + (got[2] + got[1]) if len(got) == 4 else got[0] + got[1]
        if k == 0:
            (out,) = call(out_kernel, [low], [h, hs, forward_two], flops=conv_flops)
            out = native(out)
            half, out = lax.optimization_barrier((half, out))
        if k == 1:
            (d_fields,) = call(fields_kernel, [low], [d, ds, rim, back_one], flops=conv_flops)
            d_fields = native(d_fields)
            half, d_fields = lax.optimization_barrier((half, d_fields))
    other = lax.ppermute(half, "lon", swap)
    kernel_shape = shape(weight_one.shape, F32)
    one, two = call(
        functools.partial(unpack_kernel, scale=1.0 / math.sqrt(pixel_total)),
        [kernel_shape, kernel_shape],
        [half, other],
        [pltpu.VMEM((9 * chans, cols), F32)],
    )
    return (out, d_fields, one, two)


def solution(mesh):
    placed = (P(None, "lat", "lon"), P(), P(), P(None, "lat", "lon"), P(), P(), P(), P())
    return jax.shard_map(
        on_device,
        mesh=mesh,
        in_specs=placed,
        out_specs=(P(None, "lat", "lon"), P(None, "lat", "lon"), P(), P()),
        check_vma=False,
    )
```

```python
import functools
import math

import jax
import jax.numpy as jnp
from jax import lax
from jax.experimental import pallas as pl
from jax.experimental.pallas import tpu as pltpu
from jax.experimental.layout import Layout, with_layout_constraint
from jax.sharding import PartitionSpec as P

BF = jnp.bfloat16
F32 = jnp.float32
GELU_K = math.sqrt(2.0 / math.pi)
VMEM_LIMIT = 48 * 1024 * 1024


def mm(a, b):
    return jnp.dot(a, b, preferred_element_type=F32)


def mm_t(a, b):
    return lax.dot_general(a, b, (((1,), (1,)), ((), ())), preferred_element_type=F32)


def lane_of(like):
    return lax.broadcasted_iota(jnp.int32, like.shape, like.ndim - 1)


def rot(x, by):
    return pltpu.roll(x, by, x.ndim - 1)


def gelu_parts(u):
    square = u * u
    t = jnp.tanh(GELU_K * u * (1.0 + 0.044715 * square))
    half = 0.5 + 0.5 * t
    slope = half + (0.5 * GELU_K) * u * (1.0 - t * t) * (1.0 + (3 * 0.044715) * square)
    return u * half, slope


def arrange(w_ref, forward_ref, back_ref):
    chans = w_ref.shape[2]
    diagonal = lax.broadcasted_iota(jnp.int32, (chans, chans), 0) == lax.broadcasted_iota(
        jnp.int32, (chans, chans), 1
    )
    eye = jnp.where(diagonal, 1.0, 0.0).astype(BF)
    for s in range(3):
        here = slice(s * chans, (s + 1) * chans)
        forward_ref[here] = jnp.concatenate([w_ref[r, s] for r in range(3)], axis=1)
        flipped = jnp.concatenate([w_ref[2 - r, 2 - s] for r in range(3)], axis=0)
        back_ref[here] = mm_t(eye, flipped).astype(BF)


def strip_chooser(rows, out_ref):
    source = lax.broadcasted_iota(jnp.int32, out_ref.shape, 0)
    target = lax.broadcasted_iota(jnp.int32, (1, out_ref.shape[1]), 1)
    block, side, row = target // 128, target % 128 // 64, target % 64 - 2
    wanted = 128 * (side + block // 2) + 4 * row + block
    wanted = jnp.where((row >= 0) & (row < rows), wanted, -1)
    out_ref[...] = jnp.where(source == wanted, 1.0, 0.0).astype(BF)


def end_choosers(out_ref):
    _, chans, cols = out_ref.shape
    lane = lax.broadcasted_iota(jnp.int32, (chans, cols), 1)
    spot = lax.broadcasted_iota(jnp.int32, (chans, cols), 0)
    at_end = jnp.where(lane == jnp.where(spot < 32, 0, cols - 1), spot % 16, -1)
    for m in range(16):
        out_ref[m] = jnp.where(at_end == m, 1.0, 0.0).astype(BF)


def pack_kernel(
    x_hbm, c_hbm, w1_hbm, w2_hbm,
    x_ref, c_ref, out_ref, f1_ref, b1_ref, f2_ref, b2_ref, chooser_ref, hot_ref,
    xin, cin, w1_ref, w2_ref, sems, weight_sems,
):
    rows, chans, _ = x_ref.shape
    pieces = []
    for k, start in enumerate(range(0, chans, 32)):
        here = pl.ds(start, 32)
        for side, (src, held, dst) in enumerate(((x_hbm, xin, x_ref), (c_hbm, cin, c_ref))):
            copy = pltpu.make_async_copy(src.at[here], held.at[here], sems.at[side, k])
            copy.start()
            pieces.append((copy, held, dst, here))
    weights = [
        pltpu.make_async_copy(src, dst, weight_sems.at[k])
        for k, (src, dst) in enumerate(((w1_hbm, w1_ref), (w2_hbm, w2_ref)))
    ]
    for copy in weights:
        copy.start()
    strip_chooser(rows, chooser_ref)
    end_choosers(hot_ref)
    for copy, held, dst, here in pieces:
        copy.wait()
        dst[:, here] = jnp.swapaxes(held[here], 0, 1)
    bottom = jnp.where(lax.axis_index("lat") == 0, 0, 1)
    edge = bottom * (rows - 1)
    beside = 1 + bottom * (rows - 3)
    out_ref[0] = x_ref[edge]
    out_ref[1] = x_ref[beside]
    out_ref[2] = c_ref[edge]
    out_ref[3] = c_ref[beside]
    for copy in weights:
        copy.wait()
    arrange(w1_ref, f1_ref, b1_ref)
    arrange(w2_ref, f2_ref, b2_ref)
    for at, ref in ((4, x_ref), (5, c_ref)):
        packed = jnp.zeros(ref.shape[1:], F32)
        lane = lane_of(packed)
        for i in range(rows):
            turned = rot(ref[i].astype(F32), (4 * i + 2) % 128)
            packed = jnp.where((lane >= 4 * i) & (lane < 4 * i + 4), turned, packed)
        out_ref[at] = packed.astype(BF)


def strip_kernel(
    chooser_ref, x_ref, c_ref, all_ref,
    sx_ref, sc_ref, south_ref, north_ref,
):
    rows, chans, cols = x_ref.shape
    n = all_ref.shape[0]
    me = lax.axis_index("lon")
    west = lax.rem(me + n - 1, n)
    east = lax.rem(me + 1, n)
    to_south = jnp.zeros((chans, cols), F32)
    to_north = jnp.zeros((chans, cols), F32)
    lane = lane_of(to_south)
    pair = (lane % 64) // 2
    for at, ref in ((0, sx_ref), (1, sc_ref)):
        taken = jnp.concatenate([all_ref[west, 4 + at], all_ref[me, 4 + at], all_ref[east, 4 + at]], axis=1)
        strip = mm(taken, chooser_ref[...])
        ref[...] = strip.astype(BF)
        for b in range(4):
            m = 4 * at + b
            piece = strip[:, 128 * b : 128 * b + 128]
            to_south = jnp.where(pair == m, rot(piece, (2 * m - rows) % 128), to_south)
            to_north = jnp.where(pair == m, rot(piece, (2 * m - 2) % 128), to_north)
    for ref, start, corner in ((south_ref, rows - 2, to_south), (north_ref, 0, to_north)):
        for k in range(2):
            ref[k] = x_ref[start + k]
            ref[2 + k] = c_ref[start + k]
        ref[4] = corner.astype(BF)


def shifted_rows(ref, at):
    both = ref[pl.ds(at, 2)]
    lane = lane_of(both[0])
    zero = jnp.zeros_like(both[0])
    parts = []
    for k in range(2):
        ahead = jnp.where(lane == lane.shape[1] - 1, zero, rot(both[k], lane.shape[1] - 1))
        behind = jnp.where(lane == 0, zero, rot(both[k], 1))
        parts.append(jnp.concatenate([ahead, both[k], behind], axis=0))
    return jnp.concatenate(parts, axis=1)


def row_stack(strip):
    wide = strip.astype(F32)
    parts = [wide[:, at : at + 128] for at in range(0, wide.shape[1], 128)]
    above = jnp.concatenate([rot(p, 1) for p in parts], axis=1).astype(BF)
    below = jnp.concatenate([rot(p, 127) for p in parts], axis=1).astype(BF)
    return jnp.concatenate([above, strip, below], axis=0)


def joined(z, chans, place, edge_w, edge_e):
    lane = lane_of(edge_w)
    low = jnp.where(lane == 0, rot(edge_w, 128 - place), rot(z[:chans], 1))
    high = jnp.where(lane == 127, rot(edge_e, 63 - place), rot(z[2 * chans :], 127))
    return low + z[chans : 2 * chans] + high


def pair_of_rows(ref, at):
    four = ref[pl.ds(at, 4)]
    _, chans, cols = four.shape
    return jnp.concatenate(
        [four[:3].reshape(3 * chans, cols), four[1:].reshape(3 * chans, cols)], axis=1
    )


def ring_sum(z, chans):
    return rot(z[:chans], 1) + z[chans : 2 * chans] + rot(z[2 * chans :], z.shape[1] - 1)


def with_edges(a, west, east, group):
    chans = west.shape[0]
    parts = []
    for edge, start in ((west, 16 * group), (east, 64 + 16 * group)):
        term = edge[:, start : start + 16]
        high = term.astype(BF).astype(F32)
        parts += [high, term - high]
    middle = jnp.concatenate(parts, axis=1)
    none = jnp.zeros_like(middle)
    return jnp.concatenate([a, jnp.concatenate([none, middle, none], axis=0).astype(BF)], axis=1)


def interior_kernel(
    nmap_hbm, ncode_hbm, smap_hbm, scode_hbm, hot, x_ref, c_ref, all_ref, sx_ref, sc_ref, a1_ref, a2_ref, a3_ref,
    h_ref, d_ref, pole_ref, patch_ref, rim_ref, acc1, acc2,
    picked, stack, around, slopes, tiles, hring, dring, nmap, ncode, smap, scode, sems,
):
    tables = [
        pltpu.make_async_copy(src, dst, sems.at[k])
        for k, (src, dst) in enumerate(
            ((nmap_hbm, nmap), (ncode_hbm, ncode), (smap_hbm, smap), (scode_hbm, scode))
        )
    ]
    for table in tables:
        table.start()
    rows, chans, cols = x_ref.shape
    a1 = a1_ref[...]
    a2 = a2_ref[...]
    zx = mm(a1, row_stack(sx_ref[:, 128:384]))
    zc = mm(a2, row_stack(sc_ref[:, 128:384]))
    groups = range((rows + 2) // 16 + 1)
    a1_edges = [with_edges(a1, zx[:chans, :128], zx[2 * chans :, 128:], g) for g in groups]
    a2_edges = [with_edges(a2, zc[:chans, :128], zc[2 * chans :, 128:], g) for g in groups]
    lane = lax.broadcasted_iota(jnp.int32, (chans, cols), 1)
    def summed(z):
        low = jnp.where(lane == 0, 0.0, rot(z[:chans], 1))
        high = jnp.where(lane == cols - 1, 0.0, rot(z[2 * chans :], 127))
        return low + z[chans : 2 * chans] + high

    def product(choices, ref, y):
        four = ref[y - 1 : y + 3]
        halves = [
            jnp.concatenate([four[k : k + 3].reshape(3 * chans, cols), hot[(y + 2 + k) % 16]], axis=0)
            for k in range(2)
        ]
        if (y + 2) // 16 == (y + 3) // 16:
            z = mm(choices[(y + 2) // 16], jnp.concatenate(halves, axis=1))
            return z[:, :cols], z[:, cols:]
        return [mm(choices[(y + 2 + k) // 16], halves[k]) for k in range(2)]

    def two_rows(y):
        for k, (z1, z2) in enumerate(zip(product(a1_edges, x_ref, y), product(a2_edges, c_ref, y))):
            value, slope = gelu_parts(summed(z1))
            h_ref[y + 1 + k] = value.astype(BF)
            d_ref[y + 1 + k] = (slope * summed(z2)).astype(BF)

    def gradients(y):
        two = mm_t(shifted_rows(c_ref, y), pair_of_rows(h_ref, y))
        one = mm_t(shifted_rows(d_ref, y + 1), pair_of_rows(x_ref, y - 1))
        acc2[...] = two if y == 2 else acc2[...] + two
        acc1[...] = one if y == 2 else acc1[...] + one

    todo = list(range(1, rows - 1, 2))
    for y in todo[:4]:
        two_rows(y)
    for table in tables:
        table.wait()
    parts = pole_ring(
        rows, all_ref, a1, a2, a3_ref, pole_ref, patch_ref, rim_ref,
        picked, stack, around, slopes, tiles, hring, dring, nmap, ncode, smap, scode,
    )
    for y in todo[4:]:
        next(parts, None)
        two_rows(y)
    for _ in parts:
        pass
    for y in range(2, rows - 2, 2):
        gradients(y)


def pole_ring(
    rows, all_ref, a1, a2, a3_ref, pole_ref, patch_ref, rim_ref,
    picked, stack, around, slopes, tiles, hring, dring, nmap, ncode, smap, scode,
):
    n, _, chans, cols = all_ref.shape
    lat = lax.axis_index("lat")
    me = lax.axis_index("lon")
    at_top = lat == 0
    at_pole = at_top | (lat == lax.axis_size("lat") - 1)
    block = (chans, cols)
    lane = lax.broadcasted_iota(jnp.int32, block, 1)
    west = lax.rem(me + n - 1, n)
    east = lax.rem(me + 1, n)
    first = jnp.where(at_top, 0, 2)
    last = 2 - first
    place = jnp.where(at_top, 1, rows + 2)
    inner = jnp.where(at_top, 2, rows + 1)
    flip = jnp.where(
        lax.broadcasted_iota(jnp.int32, (cols, cols), 0)
        + lax.broadcasted_iota(jnp.int32, (cols, cols), 1)
        == cols - 1,
        1.0,
        0.0,
    ).astype(BF)
    spans = [slice(128 * b, 128 * b + 128) for b in range(n)]
    partner = [jnp.where(at_top, nmap[b], smap[b]) for b in range(n)]
    code = [jnp.where(at_top, ncode[b], scode[b]) for b in range(n)]

    def partner_of(b):
        return jnp.where(at_top, nmap[b], smap[b])

    def code_of(b):
        return jnp.where(at_top, ncode[b], scode[b])

    def halves(wide):
        high = wide.astype(BF)
        return high, (wide - high.astype(F32)).astype(BF)

    for b in range(n):
        picked[b * chans : (b + 1) * chans] = all_ref[partner[b], 0]
    turned = mm(picked[...], flip)
    for b in range(n):
        here = slice(b * chans, (b + 1) * chans)
        across = jnp.where(code[b] == 1, turned[here], picked[here].astype(F32))
        tiles[b] = across
        stack[first, :, spans[b]] = across.astype(BF)
        stack[1, :, spans[b]] = all_ref[b, 0]
        stack[last, :, spans[b]] = all_ref[b, 1]
    yield

    def ends(held, at, west_tile, east_tile):
        held = jnp.where(lane == at, rot(west_tile, at + 1), held)
        return jnp.where(lane == 64 + at, rot(east_tile, 64 + at), held)

    none = jnp.zeros(block, F32)
    pole_ref[3] = tiles[me].astype(BF)
    patch_ref[2] = ends(none, place, tiles[west], tiles[east])
    u = ring_sum(mm(a1, stack[...].reshape(3 * chans, n * cols)), chans)
    value, slope = gelu_parts(u)
    slopes[...] = slope
    for b in range(n):
        hring[b] = value[:, spans[b]].astype(BF)
    yield

    wide = a2.astype(F32)
    empty = jnp.zeros((3 * chans, chans), F32)
    over = jnp.where(
        at_top,
        jnp.concatenate([wide[:, 2 * chans :], empty], axis=1),
        jnp.concatenate([empty, wide[:, :chans]], axis=1),
    )
    rest = jnp.where(at_top, wide[:, chans:], wide[:, : 2 * chans])
    near = jnp.where(at_top, 0, 1)
    for b in range(n):
        around[near, :, spans[b]] = all_ref[b, 2]
        around[1 - near, :, spans[b]] = all_ref[b, 3]
    both = around[...].reshape(2 * chans, n * cols)
    rim = ring_sum(mm(over.astype(BF), both), chans)
    yield
    tall = jnp.concatenate([rim[:, span] for span in spans], axis=0)
    high, low = halves(tall)
    turned = mm(high, flip) + mm(low, flip)
    for b in range(n):
        here = slice(b * chans, (b + 1) * chans)
        tiles[partner[b]] = jnp.where(code[b] == 1, turned[here], tall[here])
    yield
    back = ring_sum(mm(rest.astype(BF), both), chans)
    for b in range(n):
        dring[b] = (slopes[:, spans[b]] * (back[:, spans[b]] + tiles[b])).astype(BF)
    yield

    origin = 0
    for b in range(n):
        origin = origin + jnp.where(partner[b] == me, b, 0)
    three = jnp.concatenate(
        [dring[lax.rem(origin + n - 1, n)], dring[origin], dring[lax.rem(origin + 1, n)]], axis=1
    )
    wide = a3_ref[...].astype(F32)
    over = jnp.where(at_top, wide[:, 2 * chans :], wide[:, :chans])
    rim = ring_sum(mm(over.astype(BF), three), chans)[:, cols : 2 * cols]
    high, low = halves(rim)
    rim = jnp.where(code_of(origin) == 1, mm(high, flip) + mm(low, flip), rim)
    rim_ref[...] = jnp.where(at_pole, rim, none)
    yield

    pole_ref[0] = hring[me]
    pole_ref[1] = dring[me]
    whose = (me, west, east)
    found = jnp.concatenate([hring[partner_of(b)] for b in whose], axis=0)
    turned = mm(found, flip)
    own, beyond_west, beyond_east = (
        jnp.where(
            code_of(b) == 1,
            turned[k * chans : (k + 1) * chans],
            found[k * chans : (k + 1) * chans].astype(F32),
        )
        for k, b in enumerate(whose)
    )
    pole_ref[2] = own.astype(BF)
    held = ends(none, place, beyond_west, beyond_east)
    patch_ref[0] = ends(held, inner, hring[west].astype(F32), hring[east].astype(F32))
    patch_ref[1] = ends(none, inner, dring[west].astype(F32), dring[east].astype(F32))
    mine = dring[me].astype(F32)
    patch_ref[3] = jnp.where(lane < 64, rot(mine, inner), rot(mine, 65 + inner))


def rows_at_once(z1, z2, xw, xeast, cw, ceast, chans, place, h_ref, d_ref, at):
    for k in range(2):
        span = slice(128 * k, 128 * k + 128)
        u = joined(z1[:, span], chans, place + k, xw, xeast)
        back = joined(z2[:, span], chans, place + k, cw, ceast)
        value, slope = gelu_parts(u)
        h_ref[at + k] = value.astype(BF)
        d_ref[at + k] = (slope * back).astype(BF)


def finish_kernel(
    hin_ref, din_ref, in1_ref, in2_ref, pole_ref, patch_ref, x_ref, c_ref, sx_ref, sc_ref, fn_ref, fs_ref, a1_ref, a2_ref,
    h_ref, d_ref, hs_ref, ds_ref, g_ref,
    xe, ce, sxe, sce, dcol, xrim, acc1, acc2,
):
    rows, chans, cols = x_ref.shape
    lat = lax.axis_index("lat")
    at_top = lat == 0
    at_bottom = lat == lax.axis_size("lat") - 1
    block = (chans, cols)
    lane = lax.broadcasted_iota(jnp.int32, block, 1)
    row_lane = lane % 64
    h_ref[2:rows] = hin_ref[2:rows]
    d_ref[2:rows] = din_ref[2:rows]

    xe[2 : rows + 2] = x_ref[...]
    ce[2 : rows + 2] = c_ref[...]
    xe[0:2] = fn_ref[0:2]
    ce[0:2] = fn_ref[2:4]
    xe[rows + 2 : rows + 4] = fs_ref[0:2]
    ce[rows + 2 : rows + 4] = fs_ref[2:4]
    corner_n = fn_ref[4].astype(F32)
    corner_s = fs_ref[4].astype(F32)
    for at, (src, dst) in enumerate(((sx_ref, sxe), (sc_ref, sce))):
        for b in range(4):
            m = 4 * at + b
            piece = src[:, 128 * b : 128 * b + 128].astype(F32)
            piece = jnp.where(row_lane < 2, rot(corner_n, (-2 * m) % 128), piece)
            piece = jnp.where(
                (row_lane >= rows + 2) & (row_lane < rows + 4),
                rot(corner_s, (rows + 2 - 2 * m) % 128),
                piece,
            )
            dst[:, 128 * b : 128 * b + 128] = piece.astype(BF)

    a1 = a1_ref[...]
    a2 = a2_ref[...]
    zx = mm(a1, row_stack(sxe[...]))
    zc = mm(a2, row_stack(sce[...]))

    def both_ends(z):
        return [
            z[:chans, at : at + 128] + z[chans : 2 * chans, at + 128 : at + 256] + z[2 * chans :, at + 256 : at + 384]
            for at in (0, 128)
        ]

    west_side = lane < 64
    found = [(value, slope * back) for (value, slope), back in zip(map(gelu_parts, both_ends(zx)), both_ends(zc))]
    hs_ref[...] = jnp.where(west_side, found[0][0], found[1][0]).astype(BF)
    ds_ref[...] = jnp.where(west_side, found[0][1], found[1][1]).astype(BF)
    dcol[...] = jnp.where(west_side, found[1][1], found[0][1])
    xrim[...] = jnp.where(west_side, sxe[:, 128:256].astype(F32), sxe[:, 256:384].astype(F32))
    xw, xeast = zx[:chans, 128:256], zx[2 * chans :, 256:384]
    cw, ceast = zc[:chans, 128:256], zc[2 * chans :, 256:384]
    for t in (0, rows):
        rows_at_once(
            mm(a1, pair_of_rows(xe, t)), mm(a2, pair_of_rows(ce, t)),
            xw, xeast, cw, ceast, chans, t + 1, h_ref, d_ref, t,
        )

    @pl.when(at_top | at_bottom)
    def _():
        place = jnp.where(at_top, 1, rows + 2)
        inner = jnp.where(at_top, 2, rows + 1)
        outer_row = jnp.where(at_top, 0, rows + 1)
        inner_row = jnp.where(at_top, 1, rows)
        h_ref[inner_row] = pole_ref[0]
        d_ref[inner_row] = pole_ref[1]
        h_ref[outer_row] = pole_ref[2]
        d_ref[outer_row] = jnp.zeros(block, BF)
        xe[jnp.where(at_top, 1, rows + 2)] = pole_ref[3]
        at_place = row_lane == place
        at_pole = at_place | (row_lane == inner)
        hs_ref[...] = jnp.where(at_pole, patch_ref[0], hs_ref[...].astype(F32)).astype(BF)
        ds_ref[...] = jnp.where(at_pole, patch_ref[1], ds_ref[...].astype(F32)).astype(BF)
        xrim[...] = jnp.where(at_place, patch_ref[2], xrim[...])
        dcol[...] = jnp.where(row_lane == inner, patch_ref[3], dcol[...])

    own = (row_lane >= 2) & (row_lane < rows + 2)
    none = jnp.zeros(block, F32)

    def rim_terms(west_part, east_part):
        return jnp.concatenate(
            [
                jnp.where(own & (lane < 64), west_part, none),
                none,
                jnp.where(own & (lane >= 64), east_part, none),
            ],
            axis=0,
        ).astype(BF)

    west_cot = sce[:, 256:384].astype(F32)
    east_cot = sce[:, 128:256].astype(F32)
    acc2[...] = in2_ref[...] + mm_t(rim_terms(west_cot, east_cot), row_stack(hs_ref[...]))
    acc1[...] = in1_ref[...] + mm_t(rim_terms(dcol[...], dcol[...]), row_stack(xrim[...].astype(BF)))
    for y in (0, rows - 2):
        acc2[...] += mm_t(shifted_rows(ce, y + 2), pair_of_rows(h_ref, y))
        acc1[...] += mm_t(shifted_rows(d_ref, y + 1), pair_of_rows(xe, y + 1))
    g2 = acc2[...]
    g1 = acc1[...]
    middle = 3 * chans // 2
    for k, g in enumerate((g2, g1)):
        g_ref[k, : 3 * chans] = g[:, :cols]
        g_ref[k, 3 * chans :] = jnp.concatenate([g[:middle, cols:], g[middle:, cols:]], axis=1)


def out_kernel(h_ref, hs_ref, b2_ref, out_ref):
    rows, chans, _ = out_ref.shape
    b2 = b2_ref[...]
    zh = mm(b2, row_stack(hs_ref[...]))

    def two_rows(step, _):
        t = 2 * step
        z = mm(b2, pair_of_rows(h_ref, t))
        for k in range(2):
            row = joined(z[:, 128 * k : 128 * k + 128], chans, t + k + 2, zh[:chans], zh[2 * chans :])
            out_ref[t + k] = row.astype(BF)
        return 0

    lax.fori_loop(0, rows // 2, two_rows, 0, unroll=True)


def fields_kernel(d_ref, ds_ref, rim_ref, b1_ref, out_ref):
    rows, chans, _ = out_ref.shape
    lat = lax.axis_index("lat")
    b1 = b1_ref[...]
    zd = mm(b1, row_stack(ds_ref[...]))

    def two_rows(step, _):
        t = 2 * step
        z = mm(b1, pair_of_rows(d_ref, t))
        for k in range(2):
            row = joined(z[:, 128 * k : 128 * k + 128], chans, t + k + 2, zd[:chans], zd[2 * chans :])
            rim_here = ((t + k == 0) & (lat == 0)) | (
                (t + k == rows - 1) & (lat == lax.axis_size("lat") - 1)
            )
            out_ref[t + k] = (row + jnp.where(rim_here, 1.0, 0.0) * rim_ref[...]).astype(BF)
        return 0

    lax.fori_loop(0, rows // 2, two_rows, 0, unroll=True)


def unpacked(packed_ref, staged, scale):
    chans = staged.shape[2]
    low, high = slice(0, chans), slice(chans, 2 * chans)
    base, half = 3 * chans, chans // 2
    for s in range(3):
        wide = packed_ref[s * chans : (s + 1) * chans] * scale
        staged[0, s] = wide[:, low]
        staged[1, s] = wide[:, high]
    staged[2, 0] = packed_ref[base : base + chans, low] * scale
    staged[2, 1, :half] = packed_ref[base + chans : base + 3 * half, low] * scale
    staged[2, 1, half:] = packed_ref[base : base + half, high] * scale
    staged[2, 2] = packed_ref[base + half : base + 3 * half, high] * scale


def written(staged, sem, one_ref, two_ref, to_two):
    for ref, here in ((two_ref, to_two), (one_ref, jnp.logical_not(to_two))):

        @pl.when(here)
        def _():
            copy = pltpu.make_async_copy(staged, ref, sem)
            copy.start()
            copy.wait()


def own_half_kernel(half_ref, one_ref, two_ref, staged, sem, *, scale):
    unpacked(half_ref, staged, scale)
    written(staged, sem, one_ref, two_ref, lax.rem(lax.axis_index("lon"), 2) == 0)


def other_half_kernel(other_ref, one_in, two_in, one_ref, two_ref, staged, sem, *, scale):
    unpacked(other_ref, staged, scale)
    written(staged, sem, one_ref, two_ref, lax.rem(lax.axis_index("lon"), 2) == 1)


def unpack(kernel, packed, into, kernel_shape, scale):
    anywhere = pl.BlockSpec(memory_space=pl.ANY)
    return pl.pallas_call(
        functools.partial(kernel, scale=scale),
        out_shape=(kernel_shape, kernel_shape),
        in_specs=[pl.BlockSpec(memory_space=pltpu.VMEM)] + [anywhere] * len(into),
        out_specs=(anywhere, anywhere),
        input_output_aliases={1: 0, 2: 1} if into else {},
        scratch_shapes=[pltpu.VMEM(kernel_shape.shape, F32), pltpu.SemaphoreType.DMA],
        compiler_params=pltpu.CompilerParams(vmem_limit_bytes=VMEM_LIMIT),
    )(packed, *into)


def call(kernel, outs, args, scratch=(), flops=0, pinned=0):
    args = [pltpu.with_memory_space_constraint(a, pltpu.HBM) for a in args[:pinned]] + args[pinned:]
    space = [pl.BlockSpec(memory_space=pltpu.HBM)] * pinned
    space += [pl.BlockSpec(memory_space=pltpu.VMEM)] * (len(args) - pinned)
    moved = sum(math.prod(a.shape) * a.dtype.itemsize for a in list(args) + list(outs))
    return pl.pallas_call(
        kernel,
        out_shape=tuple(outs),
        in_specs=space,
        out_specs=tuple(pl.BlockSpec(memory_space=pltpu.VMEM) for _ in outs),
        scratch_shapes=list(scratch),
        compiler_params=pltpu.CompilerParams(vmem_limit_bytes=VMEM_LIMIT),
        cost_estimate=pl.CostEstimate(flops=flops, bytes_accessed=moved, transcendentals=0),
    )(*args)


def native(rows_first):
    return with_layout_constraint(rows_first.transpose(1, 0, 2), Layout((0, 1, 2)))


def on_device(
    fields_in, weight_one, weight_two, cotangent, north_map, north_code, south_map, south_code
):
    chans, rows, cols = fields_in.shape
    n = lax.axis_size("lon")
    lat_count = lax.axis_size("lat")
    pixel_total = rows * cols * n * lat_count
    shape = jax.ShapeDtypeStruct
    square = shape((3 * chans, 3 * chans), BF)
    low = shape((rows, chans, cols), BF)
    chooser = shape((3 * cols, 4 * cols), BF)
    x, c, packed, forward_one, back_one, forward_two, back_two, chooser, hot = call(
        pack_kernel,
        [low, low, shape((6, chans, cols), BF)] + [square] * 4 + [chooser, shape((16, chans, cols), BF)],
        [fields_in, cotangent, weight_one, weight_two],
        [
            pltpu.VMEM((chans, rows, cols), BF),
            pltpu.VMEM((chans, rows, cols), BF),
            pltpu.VMEM(weight_one.shape, BF),
            pltpu.VMEM(weight_two.shape, BF),
            pltpu.SemaphoreType.DMA((2, chans // 32)),
            pltpu.SemaphoreType.DMA((2,)),
        ],
        pinned=4,
    )
    gathered = lax.all_gather(packed, "lon", axis=0)
    strip = shape((chans, 4 * cols), BF)
    five = shape((5, chans, cols), BF)
    sx, sc, to_south, to_north = call(
        strip_kernel, [strip, strip, five, five], [chooser, x, c, gathered]
    )
    southward = [(i, (i + 1) % lat_count) for i in range(lat_count)]
    northward = [(target, source) for source, target in southward]
    from_north = lax.ppermute(to_south, "lat", southward)
    from_south = lax.ppermute(to_north, "lat", northward)

    conv_flops = 2 * 9 * chans * chans * rows * cols
    taller = shape((rows + 2, chans, cols), BF)
    edges = shape((chans, cols), BF)
    patches = shape((4, chans, cols), F32)
    partial = shape((3 * chans, 3 * chans), F32)
    h, d, pole, patch, rim, part_one, part_two = call(
        interior_kernel,
        [taller, taller, shape((4, chans, cols), BF), patches, shape((chans, cols), F32)] + [partial] * 2,
        [north_map, north_code, south_map, south_code, hot]
        + [x, c, gathered, sx, sc]
        + [forward_one, back_two, back_one],
        [
            pltpu.VMEM((n * chans, cols), BF),
            pltpu.VMEM((3, chans, n * cols), BF),
            pltpu.VMEM((2, chans, n * cols), BF),
            pltpu.VMEM((chans, n * cols), F32),
            pltpu.VMEM((n, chans, cols), F32),
            pltpu.VMEM((n, chans, cols), BF),
            pltpu.VMEM((n, chans, cols), BF),
        ]
        + [pltpu.SMEM((n,), jnp.int32)] * 4
        + [pltpu.SemaphoreType.DMA((4,))],
        pinned=4,
        flops=2 * conv_flops,
    )
    h, d, hs, ds, grads = call(
        finish_kernel,
        [taller, taller, edges, edges, shape((2, 9 * chans // 2, cols), F32)],
        [h, d, part_one, part_two, pole, patch, x, c, sx, sc, from_north, from_south, forward_one, back_two],
        [
            pltpu.VMEM((rows + 4, chans, cols), BF),
            pltpu.VMEM((rows + 4, chans, cols), BF),
            pltpu.VMEM((chans, 4 * cols), BF),
            pltpu.VMEM((chans, 4 * cols), BF),
            pltpu.VMEM((chans, cols), F32),
            pltpu.VMEM((chans, cols), F32),
            pltpu.VMEM((3 * chans, 3 * chans), F32),
            pltpu.VMEM((3 * chans, 3 * chans), F32),
        ],
        flops=2 * conv_flops,
    )

    mine = lax.axis_index("lon") % 2
    swap = [(i, i ^ 1) for i in range(n)]
    kept = lax.dynamic_index_in_dim(grads, mine, 0, keepdims=False)
    given = lax.dynamic_index_in_dim(grads, 1 - mine, 0, keepdims=False)
    half = kept + lax.ppermute(given, "lon", swap)
    device_count = n * lat_count
    bits = [1 << k for k in range(device_count.bit_length() - 1) if 1 << k != lat_count]
    groups = [bits[k : k + 2] for k in range(0, len(bits) - 1, 2)]
    middle = len(groups) // 2
    left = [bits[-1:]] if len(bits) % 2 else []
    orders = groups[middle:] + groups[:middle] + left, groups + left
    stages = len(orders[0])
    for k in range(stages):
        sent = half.astype(BF)
        if k == 0:
            sent, h = lax.optimization_barrier((sent, h))
        if k == 1:
            sent, d = lax.optimization_barrier((sent, d))
        got = [sent]
        for step in range(1, 1 << len(orders[0][k])):
            jumps = [sum(bit for at, bit in enumerate(order[k]) if step >> at & 1) for order in orders]
            pairs = [(i, i ^ jumps[i // lat_count % 2]) for i in range(device_count)]
            got.append(lax.ppermute(sent, ("lon", "lat"), pairs))
        got = [part.astype(F32) for part in got]
        half = (got[0] + got[3]) + (got[2] + got[1]) if len(got) == 4 else got[0] + got[1]
        if k == 0:
            (out,) = call(out_kernel, [low], [h, hs, forward_two], flops=conv_flops)
            out = native(out)
            half, out = lax.optimization_barrier((half, out))
        if k == 1:
            (d_fields,) = call(fields_kernel, [low], [d, ds, rim, back_one], flops=conv_flops)
            d_fields = native(d_fields)
            half, d_fields = lax.optimization_barrier((half, d_fields))
    other = lax.ppermute(half, "lon", swap)
    kernel_shape = shape(weight_one.shape, F32)
    scale = 1.0 / math.sqrt(pixel_total)
    into = unpack(own_half_kernel, half, (), kernel_shape, scale)
    one, two = unpack(other_half_kernel, other, into, kernel_shape, scale)
    return (out, d_fields, one, two)


def solution(mesh):
    placed = (P(None, "lat", "lon"), P(), P(), P(None, "lat", "lon"), P(), P(), P(), P())
    return jax.shard_map(
        on_device,
        mesh=mesh,
        in_specs=placed,
        out_specs=(P(None, "lat", "lon"), P(None, "lat", "lon"), P(), P()),
        check_vma=False,
    )
```

```python
import functools
import math

import jax
import jax.numpy as jnp
from jax import lax
from jax.experimental import pallas as pl
from jax.experimental.pallas import tpu as pltpu
from jax.experimental.layout import Layout, with_layout_constraint
from jax.sharding import PartitionSpec as P

BF = jnp.bfloat16
F32 = jnp.float32
GELU_K = math.sqrt(2.0 / math.pi)
VMEM_LIMIT = 48 * 1024 * 1024


def mm(a, b):
    return jnp.dot(a, b, preferred_element_type=F32)


def mm_t(a, b):
    return lax.dot_general(a, b, (((1,), (1,)), ((), ())), preferred_element_type=F32)


def lane_of(like):
    return lax.broadcasted_iota(jnp.int32, like.shape, like.ndim - 1)


def rot(x, by):
    return pltpu.roll(x, by, x.ndim - 1)


def gelu_parts(u):
    square = u * u
    t = jnp.tanh(GELU_K * u * (1.0 + 0.044715 * square))
    half = 0.5 + 0.5 * t
    slope = half + (0.5 * GELU_K) * u * (1.0 - t * t) * (1.0 + (3 * 0.044715) * square)
    return u * half, slope


def arrange(w_ref, forward_ref, back_ref):
    chans = w_ref.shape[2]
    diagonal = lax.broadcasted_iota(jnp.int32, (chans, chans), 0) == lax.broadcasted_iota(
        jnp.int32, (chans, chans), 1
    )
    eye = jnp.where(diagonal, 1.0, 0.0).astype(BF)
    for s in range(3):
        here = slice(s * chans, (s + 1) * chans)
        forward_ref[here] = jnp.concatenate([w_ref[r, s] for r in range(3)], axis=1)
        flipped = jnp.concatenate([w_ref[2 - r, 2 - s] for r in range(3)], axis=0)
        back_ref[here] = mm_t(eye, flipped).astype(BF)


def strip_chooser(rows, out_ref):
    source = lax.broadcasted_iota(jnp.int32, out_ref.shape, 0)
    target = lax.broadcasted_iota(jnp.int32, (1, out_ref.shape[1]), 1)
    block, side, row = target // 128, target % 128 // 64, target % 64 - 2
    wanted = 128 * (side + block // 2) + 4 * row + block
    wanted = jnp.where((row >= 0) & (row < rows), wanted, -1)
    out_ref[...] = jnp.where(source == wanted, 1.0, 0.0).astype(BF)


def end_choosers(out_ref):
    _, chans, cols = out_ref.shape
    lane = lax.broadcasted_iota(jnp.int32, (chans, cols), 1)
    spot = lax.broadcasted_iota(jnp.int32, (chans, cols), 0)
    at_end = jnp.where(lane == jnp.where(spot < 32, 0, cols - 1), spot % 16, -1)
    for m in range(16):
        out_ref[m] = jnp.where(at_end == m, 1.0, 0.0).astype(BF)


def pack_kernel(
    x_hbm, c_hbm, w1_hbm, w2_hbm,
    x_ref, c_ref, out_ref, f1_ref, b1_ref, f2_ref, b2_ref, chooser_ref, hot_ref,
    xin, cin, w1_ref, w2_ref, sems, weight_sems,
):
    rows, chans, _ = x_ref.shape
    bottom = jnp.where(lax.axis_index("lat") == 0, 0, 1)
    edge = bottom * (rows - 1)
    beside = 1 + bottom * (rows - 3)
    sides = ((x_hbm, xin, x_ref), (c_hbm, cin, c_ref))
    copies = []
    for side, (src, held, _) in enumerate(sides):
        pieces = []
        for k, start in enumerate(range(0, chans, 32)):
            here = pl.ds(start, 32)
            copy = pltpu.make_async_copy(src.at[here], held.at[here], sems.at[side, k])
            copy.start()
            pieces.append((copy, here))
        copies.append(pieces)
    weights = [
        pltpu.make_async_copy(src, dst, weight_sems.at[k])
        for k, (src, dst) in enumerate(((w1_hbm, w1_ref), (w2_hbm, w2_ref)))
    ]
    for copy in weights:
        copy.start()
    strip_chooser(rows, chooser_ref)
    end_choosers(hot_ref)
    for side, (_, held, dst) in enumerate(sides):
        for copy, here in copies[side]:
            copy.wait()
            dst[:, here] = jnp.swapaxes(held[here], 0, 1)
        out_ref[2 * side] = dst[edge]
        out_ref[2 * side + 1] = dst[beside]
        packed = jnp.zeros(dst.shape[1:], F32)
        lane = lane_of(packed)
        for i in range(rows):
            turned = rot(dst[i].astype(F32), (4 * i + 2) % 128)
            packed = jnp.where((lane >= 4 * i) & (lane < 4 * i + 4), turned, packed)
        out_ref[4 + side] = packed.astype(BF)
    for copy in weights:
        copy.wait()
    arrange(w1_ref, f1_ref, b1_ref)
    arrange(w2_ref, f2_ref, b2_ref)


def strip_kernel(
    chooser_ref, x_ref, c_ref, all_ref,
    sx_ref, sc_ref, south_ref, north_ref,
):
    rows, chans, cols = x_ref.shape
    n = all_ref.shape[0]
    me = lax.axis_index("lon")
    west = lax.rem(me + n - 1, n)
    east = lax.rem(me + 1, n)
    to_south = jnp.zeros((chans, cols), F32)
    to_north = jnp.zeros((chans, cols), F32)
    lane = lane_of(to_south)
    pair = (lane % 64) // 2
    for at, ref in ((0, sx_ref), (1, sc_ref)):
        taken = jnp.concatenate([all_ref[west, 4 + at], all_ref[me, 4 + at], all_ref[east, 4 + at]], axis=1)
        strip = mm(taken, chooser_ref[...])
        ref[...] = strip.astype(BF)
        for b in range(4):
            m = 4 * at + b
            piece = strip[:, 128 * b : 128 * b + 128]
            to_south = jnp.where(pair == m, rot(piece, (2 * m - rows) % 128), to_south)
            to_north = jnp.where(pair == m, rot(piece, (2 * m - 2) % 128), to_north)
    for ref, start, corner in ((south_ref, rows - 2, to_south), (north_ref, 0, to_north)):
        for k in range(2):
            ref[k] = x_ref[start + k]
            ref[2 + k] = c_ref[start + k]
        ref[4] = corner.astype(BF)


def shifted_rows(ref, at):
    both = ref[pl.ds(at, 2)]
    lane = lane_of(both[0])
    zero = jnp.zeros_like(both[0])
    parts = []
    for k in range(2):
        ahead = jnp.where(lane == lane.shape[1] - 1, zero, rot(both[k], lane.shape[1] - 1))
        behind = jnp.where(lane == 0, zero, rot(both[k], 1))
        parts.append(jnp.concatenate([ahead, both[k], behind], axis=0))
    return jnp.concatenate(parts, axis=1)


def row_stack(strip):
    wide = strip.astype(F32)
    parts = [wide[:, at : at + 128] for at in range(0, wide.shape[1], 128)]
    above = jnp.concatenate([rot(p, 1) for p in parts], axis=1).astype(BF)
    below = jnp.concatenate([rot(p, 127) for p in parts], axis=1).astype(BF)
    return jnp.concatenate([above, strip, below], axis=0)


def joined(z, chans, place, edge_w, edge_e):
    lane = lane_of(edge_w)
    low = jnp.where(lane == 0, rot(edge_w, 128 - place), rot(z[:chans], 1))
    high = jnp.where(lane == 127, rot(edge_e, 63 - place), rot(z[2 * chans :], 127))
    return low + z[chans : 2 * chans] + high


def pair_of_rows(ref, at):
    four = ref[pl.ds(at, 4)]
    _, chans, cols = four.shape
    return jnp.concatenate(
        [four[:3].reshape(3 * chans, cols), four[1:].reshape(3 * chans, cols)], axis=1
    )


def ring_sum(z, chans):
    return rot(z[:chans], 1) + z[chans : 2 * chans] + rot(z[2 * chans :], z.shape[1] - 1)


def with_edges(a, west, east, group):
    chans = west.shape[0]
    parts = []
    for edge, start in ((west, 16 * group), (east, 64 + 16 * group)):
        term = edge[:, start : start + 16]
        high = term.astype(BF).astype(F32)
        parts += [high, term - high]
    middle = jnp.concatenate(parts, axis=1)
    none = jnp.zeros_like(middle)
    return jnp.concatenate([a, jnp.concatenate([none, middle, none], axis=0).astype(BF)], axis=1)


def interior_kernel(
    nmap_hbm, ncode_hbm, smap_hbm, scode_hbm, hot, x_ref, c_ref, all_ref, sx_ref, sc_ref, a1_ref, a2_ref, a3_ref,
    h_ref, d_ref, pole_ref, patch_ref, rim_ref, acc1, acc2,
    picked, stack, around, slopes, tiles, hring, dring, nmap, ncode, smap, scode, sems,
):
    tables = [
        pltpu.make_async_copy(src, dst, sems.at[k])
        for k, (src, dst) in enumerate(
            ((nmap_hbm, nmap), (ncode_hbm, ncode), (smap_hbm, smap), (scode_hbm, scode))
        )
    ]
    for table in tables:
        table.start()
    rows, chans, cols = x_ref.shape
    a1 = a1_ref[...]
    a2 = a2_ref[...]
    zx = mm(a1, row_stack(sx_ref[:, 128:384]))
    zc = mm(a2, row_stack(sc_ref[:, 128:384]))
    groups = range((rows + 2) // 16 + 1)
    a1_edges = [with_edges(a1, zx[:chans, :128], zx[2 * chans :, 128:], g) for g in groups]
    a2_edges = [with_edges(a2, zc[:chans, :128], zc[2 * chans :, 128:], g) for g in groups]
    lane = lax.broadcasted_iota(jnp.int32, (chans, cols), 1)
    def summed(z):
        low = jnp.where(lane == 0, 0.0, rot(z[:chans], 1))
        high = jnp.where(lane == cols - 1, 0.0, rot(z[2 * chans :], 127))
        return low + z[chans : 2 * chans] + high

    def product(choices, ref, y):
        four = ref[y - 1 : y + 3]
        halves = [
            jnp.concatenate([four[k : k + 3].reshape(3 * chans, cols), hot[(y + 2 + k) % 16]], axis=0)
            for k in range(2)
        ]
        if (y + 2) // 16 == (y + 3) // 16:
            z = mm(choices[(y + 2) // 16], jnp.concatenate(halves, axis=1))
            return z[:, :cols], z[:, cols:]
        return [mm(choices[(y + 2 + k) // 16], halves[k]) for k in range(2)]

    def two_rows(y):
        for k, (z1, z2) in enumerate(zip(product(a1_edges, x_ref, y), product(a2_edges, c_ref, y))):
            value, slope = gelu_parts(summed(z1))
            h_ref[y + 1 + k] = value.astype(BF)
            d_ref[y + 1 + k] = (slope * summed(z2)).astype(BF)

    def gradients(y):
        two = mm_t(shifted_rows(c_ref, y), pair_of_rows(h_ref, y))
        one = mm_t(shifted_rows(d_ref, y + 1), pair_of_rows(x_ref, y - 1))
        acc2[...] = two if y == 2 else acc2[...] + two
        acc1[...] = one if y == 2 else acc1[...] + one

    todo = list(range(1, rows - 1, 2))
    for y in todo[:4]:
        two_rows(y)
    for table in tables:
        table.wait()
    parts = pole_ring(
        rows, all_ref, a1, a2, a3_ref, pole_ref, patch_ref, rim_ref,
        picked, stack, around, slopes, tiles, hring, dring, nmap, ncode, smap, scode,
    )
    for y in todo[4:]:
        next(parts, None)
        two_rows(y)
    for _ in parts:
        pass
    for y in range(2, rows - 2, 2):
        gradients(y)


def pole_ring(
    rows, all_ref, a1, a2, a3_ref, pole_ref, patch_ref, rim_ref,
    picked, stack, around, slopes, tiles, hring, dring, nmap, ncode, smap, scode,
):
    n, _, chans, cols = all_ref.shape
    lat = lax.axis_index("lat")
    me = lax.axis_index("lon")
    at_top = lat == 0
    at_pole = at_top | (lat == lax.axis_size("lat") - 1)
    block = (chans, cols)
    lane = lax.broadcasted_iota(jnp.int32, block, 1)
    west = lax.rem(me + n - 1, n)
    east = lax.rem(me + 1, n)
    first = jnp.where(at_top, 0, 2)
    last = 2 - first
    place = jnp.where(at_top, 1, rows + 2)
    inner = jnp.where(at_top, 2, rows + 1)
    flip = jnp.where(
        lax.broadcasted_iota(jnp.int32, (cols, cols), 0)
        + lax.broadcasted_iota(jnp.int32, (cols, cols), 1)
        == cols - 1,
        1.0,
        0.0,
    ).astype(BF)
    spans = [slice(128 * b, 128 * b + 128) for b in range(n)]
    partner = [jnp.where(at_top, nmap[b], smap[b]) for b in range(n)]
    code = [jnp.where(at_top, ncode[b], scode[b]) for b in range(n)]

    def partner_of(b):
        return jnp.where(at_top, nmap[b], smap[b])

    def code_of(b):
        return jnp.where(at_top, ncode[b], scode[b])

    def halves(wide):
        high = wide.astype(BF)
        return high, (wide - high.astype(F32)).astype(BF)

    for b in range(n):
        picked[b * chans : (b + 1) * chans] = all_ref[partner[b], 0]
    turned = mm(picked[...], flip)
    for b in range(n):
        here = slice(b * chans, (b + 1) * chans)
        across = jnp.where(code[b] == 1, turned[here], picked[here].astype(F32))
        tiles[b] = across
        stack[first, :, spans[b]] = across.astype(BF)
        stack[1, :, spans[b]] = all_ref[b, 0]
        stack[last, :, spans[b]] = all_ref[b, 1]
    yield

    def ends(held, at, west_tile, east_tile):
        held = jnp.where(lane == at, rot(west_tile, at + 1), held)
        return jnp.where(lane == 64 + at, rot(east_tile, 64 + at), held)

    none = jnp.zeros(block, F32)
    pole_ref[3] = tiles[me].astype(BF)
    patch_ref[2] = ends(none, place, tiles[west], tiles[east])
    u = ring_sum(mm(a1, stack[...].reshape(3 * chans, n * cols)), chans)
    value, slope = gelu_parts(u)
    slopes[...] = slope
    for b in range(n):
        hring[b] = value[:, spans[b]].astype(BF)
    yield

    wide = a2.astype(F32)
    empty = jnp.zeros((3 * chans, chans), F32)
    over = jnp.where(
        at_top,
        jnp.concatenate([wide[:, 2 * chans :], empty], axis=1),
        jnp.concatenate([empty, wide[:, :chans]], axis=1),
    )
    rest = jnp.where(at_top, wide[:, chans:], wide[:, : 2 * chans])
    near = jnp.where(at_top, 0, 1)
    for b in range(n):
        around[near, :, spans[b]] = all_ref[b, 2]
        around[1 - near, :, spans[b]] = all_ref[b, 3]
    both = around[...].reshape(2 * chans, n * cols)
    rim = ring_sum(mm(over.astype(BF), both), chans)
    yield
    tall = jnp.concatenate([rim[:, span] for span in spans], axis=0)
    high, low = halves(tall)
    turned = mm(high, flip) + mm(low, flip)
    for b in range(n):
        here = slice(b * chans, (b + 1) * chans)
        tiles[partner[b]] = jnp.where(code[b] == 1, turned[here], tall[here])
    yield
    back = ring_sum(mm(rest.astype(BF), both), chans)
    for b in range(n):
        dring[b] = (slopes[:, spans[b]] * (back[:, spans[b]] + tiles[b])).astype(BF)
    yield

    origin = 0
    for b in range(n):
        origin = origin + jnp.where(partner[b] == me, b, 0)
    three = jnp.concatenate(
        [dring[lax.rem(origin + n - 1, n)], dring[origin], dring[lax.rem(origin + 1, n)]], axis=1
    )
    wide = a3_ref[...].astype(F32)
    over = jnp.where(at_top, wide[:, 2 * chans :], wide[:, :chans])
    rim = ring_sum(mm(over.astype(BF), three), chans)[:, cols : 2 * cols]
    high, low = halves(rim)
    rim = jnp.where(code_of(origin) == 1, mm(high, flip) + mm(low, flip), rim)
    rim_ref[...] = jnp.where(at_pole, rim, none)
    yield

    pole_ref[0] = hring[me]
    pole_ref[1] = dring[me]
    whose = (me, west, east)
    found = jnp.concatenate([hring[partner_of(b)] for b in whose], axis=0)
    turned = mm(found, flip)
    own, beyond_west, beyond_east = (
        jnp.where(
            code_of(b) == 1,
            turned[k * chans : (k + 1) * chans],
            found[k * chans : (k + 1) * chans].astype(F32),
        )
        for k, b in enumerate(whose)
    )
    pole_ref[2] = own.astype(BF)
    held = ends(none, place, beyond_west, beyond_east)
    patch_ref[0] = ends(held, inner, hring[west].astype(F32), hring[east].astype(F32))
    patch_ref[1] = ends(none, inner, dring[west].astype(F32), dring[east].astype(F32))
    mine = dring[me].astype(F32)
    patch_ref[3] = jnp.where(lane < 64, rot(mine, inner), rot(mine, 65 + inner))


def rows_at_once(z1, z2, xw, xeast, cw, ceast, chans, place, h_ref, d_ref, at):
    for k in range(2):
        span = slice(128 * k, 128 * k + 128)
        u = joined(z1[:, span], chans, place + k, xw, xeast)
        back = joined(z2[:, span], chans, place + k, cw, ceast)
        value, slope = gelu_parts(u)
        h_ref[at + k] = value.astype(BF)
        d_ref[at + k] = (slope * back).astype(BF)


def finish_kernel(
    hin_ref, din_ref, in1_ref, in2_ref, pole_ref, patch_ref, x_ref, c_ref, sx_ref, sc_ref, fn_ref, fs_ref, a1_ref, a2_ref,
    h_ref, d_ref, hs_ref, ds_ref, g_ref,
    xe, ce, sxe, sce, dcol, xrim, acc1, acc2,
):
    rows, chans, cols = x_ref.shape
    lat = lax.axis_index("lat")
    at_top = lat == 0
    at_bottom = lat == lax.axis_size("lat") - 1
    block = (chans, cols)
    lane = lax.broadcasted_iota(jnp.int32, block, 1)
    row_lane = lane % 64
    h_ref[2:rows] = hin_ref[2:rows]
    d_ref[2:rows] = din_ref[2:rows]

    xe[2 : rows + 2] = x_ref[...]
    ce[2 : rows + 2] = c_ref[...]
    xe[0:2] = fn_ref[0:2]
    ce[0:2] = fn_ref[2:4]
    xe[rows + 2 : rows + 4] = fs_ref[0:2]
    ce[rows + 2 : rows + 4] = fs_ref[2:4]
    corner_n = fn_ref[4].astype(F32)
    corner_s = fs_ref[4].astype(F32)
    for at, (src, dst) in enumerate(((sx_ref, sxe), (sc_ref, sce))):
        for b in range(4):
            m = 4 * at + b
            piece = src[:, 128 * b : 128 * b + 128].astype(F32)
            piece = jnp.where(row_lane < 2, rot(corner_n, (-2 * m) % 128), piece)
            piece = jnp.where(
                (row_lane >= rows + 2) & (row_lane < rows + 4),
                rot(corner_s, (rows + 2 - 2 * m) % 128),
                piece,
            )
            dst[:, 128 * b : 128 * b + 128] = piece.astype(BF)

    a1 = a1_ref[...]
    a2 = a2_ref[...]
    zx = mm(a1, row_stack(sxe[...]))
    zc = mm(a2, row_stack(sce[...]))

    def both_ends(z):
        return [
            z[:chans, at : at + 128] + z[chans : 2 * chans, at + 128 : at + 256] + z[2 * chans :, at + 256 : at + 384]
            for at in (0, 128)
        ]

    west_side = lane < 64
    found = [(value, slope * back) for (value, slope), back in zip(map(gelu_parts, both_ends(zx)), both_ends(zc))]
    hs_ref[...] = jnp.where(west_side, found[0][0], found[1][0]).astype(BF)
    ds_ref[...] = jnp.where(west_side, found[0][1], found[1][1]).astype(BF)
    dcol[...] = jnp.where(west_side, found[1][1], found[0][1])
    xrim[...] = jnp.where(west_side, sxe[:, 128:256].astype(F32), sxe[:, 256:384].astype(F32))
    xw, xeast = zx[:chans, 128:256], zx[2 * chans :, 256:384]
    cw, ceast = zc[:chans, 128:256], zc[2 * chans :, 256:384]
    for t in (0, rows):
        rows_at_once(
            mm(a1, pair_of_rows(xe, t)), mm(a2, pair_of_rows(ce, t)),
            xw, xeast, cw, ceast, chans, t + 1, h_ref, d_ref, t,
        )

    @pl.when(at_top | at_bottom)
    def _():
        place = jnp.where(at_top, 1, rows + 2)
        inner = jnp.where(at_top, 2, rows + 1)
        outer_row = jnp.where(at_top, 0, rows + 1)
        inner_row = jnp.where(at_top, 1, rows)
        h_ref[inner_row] = pole_ref[0]
        d_ref[inner_row] = pole_ref[1]
        h_ref[outer_row] = pole_ref[2]
        d_ref[outer_row] = jnp.zeros(block, BF)
        xe[jnp.where(at_top, 1, rows + 2)] = pole_ref[3]
        at_place = row_lane == place
        at_pole = at_place | (row_lane == inner)
        hs_ref[...] = jnp.where(at_pole, patch_ref[0], hs_ref[...].astype(F32)).astype(BF)
        ds_ref[...] = jnp.where(at_pole, patch_ref[1], ds_ref[...].astype(F32)).astype(BF)
        xrim[...] = jnp.where(at_place, patch_ref[2], xrim[...])
        dcol[...] = jnp.where(row_lane == inner, patch_ref[3], dcol[...])

    own = (row_lane >= 2) & (row_lane < rows + 2)
    none = jnp.zeros(block, F32)

    def rim_terms(west_part, east_part):
        return jnp.concatenate(
            [
                jnp.where(own & (lane < 64), west_part, none),
                none,
                jnp.where(own & (lane >= 64), east_part, none),
            ],
            axis=0,
        ).astype(BF)

    west_cot = sce[:, 256:384].astype(F32)
    east_cot = sce[:, 128:256].astype(F32)
    acc2[...] = in2_ref[...] + mm_t(rim_terms(west_cot, east_cot), row_stack(hs_ref[...]))
    acc1[...] = in1_ref[...] + mm_t(rim_terms(dcol[...], dcol[...]), row_stack(xrim[...].astype(BF)))
    for y in (0, rows - 2):
        acc2[...] += mm_t(shifted_rows(ce, y + 2), pair_of_rows(h_ref, y))
        acc1[...] += mm_t(shifted_rows(d_ref, y + 1), pair_of_rows(xe, y + 1))
    g2 = acc2[...]
    g1 = acc1[...]
    middle = 3 * chans // 2
    for k, g in enumerate((g2, g1)):
        g_ref[k, : 3 * chans] = g[:, :cols]
        g_ref[k, 3 * chans :] = jnp.concatenate([g[:middle, cols:], g[middle:, cols:]], axis=1)


def out_kernel(h_ref, hs_ref, b2_ref, out_ref):
    rows, chans, _ = out_ref.shape
    b2 = b2_ref[...]
    zh = mm(b2, row_stack(hs_ref[...]))

    def two_rows(step, _):
        t = 2 * step
        z = mm(b2, pair_of_rows(h_ref, t))
        for k in range(2):
            row = joined(z[:, 128 * k : 128 * k + 128], chans, t + k + 2, zh[:chans], zh[2 * chans :])
            out_ref[t + k] = row.astype(BF)
        return 0

    lax.fori_loop(0, rows // 2, two_rows, 0, unroll=True)


def fields_kernel(d_ref, ds_ref, rim_ref, b1_ref, out_ref):
    rows, chans, _ = out_ref.shape
    lat = lax.axis_index("lat")
    b1 = b1_ref[...]
    zd = mm(b1, row_stack(ds_ref[...]))

    def two_rows(step, _):
        t = 2 * step
        z = mm(b1, pair_of_rows(d_ref, t))
        for k in range(2):
            row = joined(z[:, 128 * k : 128 * k + 128], chans, t + k + 2, zd[:chans], zd[2 * chans :])
            rim_here = ((t + k == 0) & (lat == 0)) | (
                (t + k == rows - 1) & (lat == lax.axis_size("lat") - 1)
            )
            out_ref[t + k] = (row + jnp.where(rim_here, 1.0, 0.0) * rim_ref[...]).astype(BF)
        return 0

    lax.fori_loop(0, rows // 2, two_rows, 0, unroll=True)


def unpacked(packed_ref, staged, scale):
    chans = staged.shape[2]
    low, high = slice(0, chans), slice(chans, 2 * chans)
    base, half = 3 * chans, chans // 2
    for s in range(3):
        wide = packed_ref[s * chans : (s + 1) * chans] * scale
        staged[0, s] = wide[:, low]
        staged[1, s] = wide[:, high]
    staged[2, 0] = packed_ref[base : base + chans, low] * scale
    staged[2, 1, :half] = packed_ref[base + chans : base + 3 * half, low] * scale
    staged[2, 1, half:] = packed_ref[base : base + half, high] * scale
    staged[2, 2] = packed_ref[base + half : base + 3 * half, high] * scale


def written(staged, sem, one_ref, two_ref, to_two):
    for ref, here in ((two_ref, to_two), (one_ref, jnp.logical_not(to_two))):

        @pl.when(here)
        def _():
            copy = pltpu.make_async_copy(staged, ref, sem)
            copy.start()
            copy.wait()


def own_half_kernel(half_ref, one_ref, two_ref, staged, sem, *, scale):
    unpacked(half_ref, staged, scale)
    written(staged, sem, one_ref, two_ref, lax.rem(lax.axis_index("lon"), 2) == 0)


def other_half_kernel(other_ref, one_in, two_in, one_ref, two_ref, staged, sem, *, scale):
    unpacked(other_ref, staged, scale)
    written(staged, sem, one_ref, two_ref, lax.rem(lax.axis_index("lon"), 2) == 1)


def unpack(kernel, packed, into, kernel_shape, scale):
    anywhere = pl.BlockSpec(memory_space=pl.ANY)
    return pl.pallas_call(
        functools.partial(kernel, scale=scale),
        out_shape=(kernel_shape, kernel_shape),
        in_specs=[pl.BlockSpec(memory_space=pltpu.VMEM)] + [anywhere] * len(into),
        out_specs=(anywhere, anywhere),
        input_output_aliases={1: 0, 2: 1} if into else {},
        scratch_shapes=[pltpu.VMEM(kernel_shape.shape, F32), pltpu.SemaphoreType.DMA],
        compiler_params=pltpu.CompilerParams(vmem_limit_bytes=VMEM_LIMIT),
    )(packed, *into)


def call(kernel, outs, args, scratch=(), flops=0, pinned=0):
    args = [pltpu.with_memory_space_constraint(a, pltpu.HBM) for a in args[:pinned]] + args[pinned:]
    space = [pl.BlockSpec(memory_space=pltpu.HBM)] * pinned
    space += [pl.BlockSpec(memory_space=pltpu.VMEM)] * (len(args) - pinned)
    moved = sum(math.prod(a.shape) * a.dtype.itemsize for a in list(args) + list(outs))
    return pl.pallas_call(
        kernel,
        out_shape=tuple(outs),
        in_specs=space,
        out_specs=tuple(pl.BlockSpec(memory_space=pltpu.VMEM) for _ in outs),
        scratch_shapes=list(scratch),
        compiler_params=pltpu.CompilerParams(vmem_limit_bytes=VMEM_LIMIT),
        cost_estimate=pl.CostEstimate(flops=flops, bytes_accessed=moved, transcendentals=0),
    )(*args)


def native(rows_first):
    return with_layout_constraint(rows_first.transpose(1, 0, 2), Layout((0, 1, 2)))


def on_device(
    fields_in, weight_one, weight_two, cotangent, north_map, north_code, south_map, south_code
):
    chans, rows, cols = fields_in.shape
    n = lax.axis_size("lon")
    lat_count = lax.axis_size("lat")
    pixel_total = rows * cols * n * lat_count
    shape = jax.ShapeDtypeStruct
    square = shape((3 * chans, 3 * chans), BF)
    low = shape((rows, chans, cols), BF)
    chooser = shape((3 * cols, 4 * cols), BF)
    x, c, packed, forward_one, back_one, forward_two, back_two, chooser, hot = call(
        pack_kernel,
        [low, low, shape((6, chans, cols), BF)] + [square] * 4 + [chooser, shape((16, chans, cols), BF)],
        [fields_in, cotangent, weight_one, weight_two],
        [
            pltpu.VMEM((chans, rows, cols), BF),
            pltpu.VMEM((chans, rows, cols), BF),
            pltpu.VMEM(weight_one.shape, BF),
            pltpu.VMEM(weight_two.shape, BF),
            pltpu.SemaphoreType.DMA((2, chans // 32)),
            pltpu.SemaphoreType.DMA((2,)),
        ],
        pinned=4,
    )
    gathered = lax.all_gather(packed, "lon", axis=0)
    strip = shape((chans, 4 * cols), BF)
    five = shape((5, chans, cols), BF)
    sx, sc, to_south, to_north = call(
        strip_kernel, [strip, strip, five, five], [chooser, x, c, gathered]
    )
    southward = [(i, (i + 1) % lat_count) for i in range(lat_count)]
    northward = [(target, source) for source, target in southward]
    from_north = lax.ppermute(to_south, "lat", southward)
    from_south = lax.ppermute(to_north, "lat", northward)

    conv_flops = 2 * 9 * chans * chans * rows * cols
    taller = shape((rows + 2, chans, cols), BF)
    edges = shape((chans, cols), BF)
    patches = shape((4, chans, cols), F32)
    partial = shape((3 * chans, 3 * chans), F32)
    h, d, pole, patch, rim, part_one, part_two = call(
        interior_kernel,
        [taller, taller, shape((4, chans, cols), BF), patches, shape((chans, cols), F32)] + [partial] * 2,
        [north_map, north_code, south_map, south_code, hot]
        + [x, c, gathered, sx, sc]
        + [forward_one, back_two, back_one],
        [
            pltpu.VMEM((n * chans, cols), BF),
            pltpu.VMEM((3, chans, n * cols), BF),
            pltpu.VMEM((2, chans, n * cols), BF),
            pltpu.VMEM((chans, n * cols), F32),
            pltpu.VMEM((n, chans, cols), F32),
            pltpu.VMEM((n, chans, cols), BF),
            pltpu.VMEM((n, chans, cols), BF),
        ]
        + [pltpu.SMEM((n,), jnp.int32)] * 4
        + [pltpu.SemaphoreType.DMA((4,))],
        pinned=4,
        flops=2 * conv_flops,
    )
    h, d, hs, ds, grads = call(
        finish_kernel,
        [taller, taller, edges, edges, shape((2, 9 * chans // 2, cols), F32)],
        [h, d, part_one, part_two, pole, patch, x, c, sx, sc, from_north, from_south, forward_one, back_two],
        [
            pltpu.VMEM((rows + 4, chans, cols), BF),
            pltpu.VMEM((rows + 4, chans, cols), BF),
            pltpu.VMEM((chans, 4 * cols), BF),
            pltpu.VMEM((chans, 4 * cols), BF),
            pltpu.VMEM((chans, cols), F32),
            pltpu.VMEM((chans, cols), F32),
            pltpu.VMEM((3 * chans, 3 * chans), F32),
            pltpu.VMEM((3 * chans, 3 * chans), F32),
        ],
        flops=2 * conv_flops,
    )

    mine = lax.axis_index("lon") % 2
    swap = [(i, i ^ 1) for i in range(n)]
    kept = lax.dynamic_index_in_dim(grads, mine, 0, keepdims=False)
    given = lax.dynamic_index_in_dim(grads, 1 - mine, 0, keepdims=False)
    half = kept + lax.ppermute(given, "lon", swap)
    device_count = n * lat_count
    bits = [1 << k for k in range(device_count.bit_length() - 1) if 1 << k != lat_count]
    groups = [bits[k : k + 2] for k in range(0, len(bits) - 1, 2)]
    middle = len(groups) // 2
    left = [bits[-1:]] if len(bits) % 2 else []
    orders = groups[middle:] + groups[:middle] + left, groups + left
    stages = len(orders[0])
    for k in range(stages):
        sent = half.astype(BF)
        if k == 0:
            sent, h = lax.optimization_barrier((sent, h))
        if k == 1:
            sent, d = lax.optimization_barrier((sent, d))
        got = [sent]
        for step in range(1, 1 << len(orders[0][k])):
            jumps = [sum(bit for at, bit in enumerate(order[k]) if step >> at & 1) for order in orders]
            pairs = [(i, i ^ jumps[i // lat_count % 2]) for i in range(device_count)]
            got.append(lax.ppermute(sent, ("lon", "lat"), pairs))
        got = [part.astype(F32) for part in got]
        half = (got[0] + got[3]) + (got[2] + got[1]) if len(got) == 4 else got[0] + got[1]
        if k == 0:
            (out,) = call(out_kernel, [low], [h, hs, forward_two], flops=conv_flops)
            out = native(out)
            half, out = lax.optimization_barrier((half, out))
        if k == 1:
            (d_fields,) = call(fields_kernel, [low], [d, ds, rim, back_one], flops=conv_flops)
            d_fields = native(d_fields)
            half, d_fields = lax.optimization_barrier((half, d_fields))
    other = lax.ppermute(half, "lon", swap)
    kernel_shape = shape(weight_one.shape, F32)
    scale = 1.0 / math.sqrt(pixel_total)
    into = unpack(own_half_kernel, half, (), kernel_shape, scale)
    one, two = unpack(other_half_kernel, other, into, kernel_shape, scale)
    return (out, d_fields, one, two)


def solution(mesh):
    placed = (P(None, "lat", "lon"), P(), P(), P(None, "lat", "lon"), P(), P(), P(), P())
    return jax.shard_map(
        on_device,
        mesh=mesh,
        in_specs=placed,
        out_specs=(P(None, "lat", "lon"), P(None, "lat", "lon"), P(), P()),
        check_vma=False,
    )
```
